32 devices in a mesh: dp: 2 (over core), expert: 16 (over z, y, x).
Axes of the slice: x: 2, y: 2, z: 4, core: 2. Of those that a mesh axis runs over, the one named last changes fastest.
Arguments:
- tokens: bfloat16 [4096, 2048], P(('dp', 'expert')), may hold values from -6 to 6
- attn_gain: bfloat16 [2048], P(('dp', 'expert')), may hold values from 0.5 to 1.5
- kv_gain: bfloat16 [512], P(('dp', 'expert')), may hold values from 0.5 to 1.5
- ffn_gain: bfloat16 [2048], P(('dp', 'expert')), may hold values from 0.5 to 1.5
- q_weight: bfloat16 [2048, 3072], P(('dp', 'expert')), may hold values from -0.125 to 0.125
- kv_down_weight: bfloat16 [2048, 576], P(('dp', 'expert')), may hold values from -0.125 to 0.125
- kv_up_weight: bfloat16 [512, 4096], P(('dp', 'expert')), may hold values from -0.25 to 0.25
- out_weight: bfloat16 [2048, 2048], P(('dp', 'expert')), may hold values from -0.5 to 0.5
- shared_gate_up: bfloat16 [2048, 2, 2816], P(('dp', 'expert')), may hold values from -0.125 to 0.125
- shared_down: bfloat16 [2816, 2048], P(('dp', 'expert')), may hold values from -0.109375 to 0.109375
- expert_gate_up: bfloat16 [16, 2048, 2, 1408], P('expert', 'dp'), may hold values from -0.125 to 0.125
- expert_down: bfloat16 [16, 1408, 2048], P('expert', 'dp'), may hold values from -0.15625 to 0.15625
- routes: int32 [4096, 6], P(('dp', 'expert')), may hold values from 0 to 15, all different within a row; in each aligned block of 128 rows (0 to 127, 128 to 255, ...) at most 72 rows name the same one
- gates: float32 [4096, 6], P(('dp', 'expert')), may hold values from 0.2 to 0.5
- lengths: int32 [32, 2], P(('dp', 'expert')), may hold values from 1 to 96, 128 in all within a row
- out_grad: bfloat16 [4096, 2048], P(('dp', 'expert')), may hold values from -6 to 6
Outputs:
- output: bfloat16 [4096, 2048], P(('dp', 'expert'))
- grad_tokens: bfloat16 [4096, 2048], P(('dp', 'expert'))
- grad_attn_gain: float32 [2048], P(('dp', 'expert'))
- grad_kv_gain: float32 [512], P(('dp', 'expert'))
- grad_ffn_gain: float32 [2048], P(('dp', 'expert'))
- grad_q_weight: float32 [2048, 3072], P(('dp', 'expert'))
- grad_kv_down: float32 [2048, 576], P(('dp', 'expert'))
- grad_kv_up: float32 [512, 4096], P(('dp', 'expert'))
- grad_out_weight: float32 [2048, 2048], P(('dp', 'expert'))
- grad_shared_gate_up: float32 [2048, 2, 2816], P(('dp', 'expert'))
- grad_shared_down: float32 [2816, 2048], P(('dp', 'expert'))
- grad_expert_gate_up: float32 [16, 2048, 2, 1408], P('expert', 'dp')
- grad_expert_down: float32 [16, 1408, 2048], P('expert', 'dp')
The draws below stay inside these ranges and needn't reach their ends.
Inputs may be any that keep to these rules, and one draw needn't show every extreme that they name: `routes`: A token's 6 experts are distinct. Among the 128 rows of one device, each expert is named by at most 72 rows, a bound that some block reaches. `lengths`: each row sums to 128; no entry exceeds 96.
All inputs are finite; a program needn't handle non-finite values.
Results may differ from the reference program's by a relative error of at most 0.019.
Values may be sent and summed in bfloat16 or wider, within the bound.
No kernel may reach another device: no remote copies, remote signals or barrier semaphores. Data moves between devices by JAX's collectives and lax.ppermute only.
A program may use at most 320 MiB of HBM per device.

```python
import math
import jax
import jax.numpy as jnp
import numpy as np
from jax import lax

D = 2048
H = 16
DH = 128
DR = 64
DV = 128
KVR = 512
FE = 1408
FS = 2816
TOP = 6
DOCS = 2
TOK_DEV = 128
EXPERTS = 16
MOST_LEN = 96
CAP = 72
TOKENS = 4096
N_DP = 2
N_EXPERT = 16


def strengthened(values, own_key, source, target, parts, factor):
    owner, partner = [(jnp.arange(values.shape[dim]) // (values.shape[dim] // parts)).reshape([-1 if axis == dim else 1 for axis in range(values.ndim)]) for dim in (source, target)]
    chosen = jax.random.permutation(own_key, parts)[partner]
    strong = (owner == chosen) | (owner == (partner + parts // 2) % parts)
    return jnp.where(strong, factor * values, values)


def shard_levels(own_key, dims, shards, least, high):
    level = 1.0
    for position, blocks in shards:
        steps = jax.random.uniform(jax.random.fold_in(jax.random.fold_in(own_key, 6), position), (blocks,), jnp.float32, least / len(shards), high / len(shards))
        level = level * jnp.repeat(jnp.exp(steps), dims[position] // blocks).reshape((-1,) + (1,) * (len(dims) - 1 - position))
    return level


def length_profile(amount, total, bound, skew):
    portions = [(1 << 20) // math.isqrt(rank ** skew) + 1 for rank in range(2, amount + 1)]
    surplus, given = total - bound - (amount - 1), [1] * (amount - 1)
    while surplus > 0:
        movable = [i for i in range(amount - 1) if given[i] < bound]
        whole, budget = sum([portions[i] for i in movable]), surplus
        for i in movable:
            more = min(bound - given[i], max(1, budget * portions[i] // whole), surplus)
            given[i] = given[i] + more
            surplus = surplus - more
    return np.array([bound] + given)


def uneven(key, number_of, total, most, lean):
    if number_of == 2:
        one = jax.random.randint(key, (), max(1, total - most), min(most, total - 1) + 1)
        return jnp.stack([one, total - one])
    sizes = jnp.asarray(length_profile(number_of, total, most, lean), jnp.int32)
    pairs = (number_of - 1) // 2
    giver, receiver = sizes[1:1 + 2 * pairs:2], sizes[2:2 + 2 * pairs:2]
    slack = jnp.minimum(giver - 1, most - receiver)
    moved = jax.random.randint(jax.random.fold_in(key, 1), (pairs,), 0, 1 << 20) % (slack + 1)
    sizes = sizes.at[1:1 + 2 * pairs:2].set(giver - moved).at[2:2 + 2 * pairs:2].set(receiver + moved)
    return sizes[jax.random.permutation(jax.random.fold_in(key, 2), number_of)]


def shared_out(rng, own, number, rows, count, top, bound, lean):
    sequence = jax.random.permutation(rng, count)
    crowded, common = shares(count, rows * top, bound, lean, True), shares(count, rows * top, bound, lean, False)
    places = jnp.arange(count)

    def named(tallies, turn):
        used = int((tallies > 0).sum())
        fixed = max(1, used // 4)
        passed = fixed + (places - fixed + turn * (used - fixed)) % max(1, count - fixed)
        return jnp.zeros((count,), jnp.int32).at[sequence[jnp.where(places < fixed, places, passed)]].set(jnp.asarray(tallies, jnp.int32))

    tallies = jnp.where(number % 4 == 0, named(crowded, number // 4), named(common, number - number // 4 - 1))
    mixed = jax.random.permutation(jax.random.fold_in(own, 3), count)
    source_of, receiver = mixed[0:count // 2 * 2:2], mixed[1:count // 2 * 2:2]
    margin = jnp.minimum(tallies[source_of] - 1, bound - tallies[receiver]) // 2
    margin = jnp.where((source_of == sequence[0]) | (receiver == sequence[0]) | (tallies[receiver] == 0), 0, jnp.maximum(margin, 0))
    passed = jax.random.randint(jax.random.fold_in(own, 4), (count // 2,), 0, 1 << 20) % (margin + 1)
    tallies = tallies.at[source_of].add(-passed).at[receiver].add(passed)
    labels = jnp.searchsorted(jnp.cumsum(tallies), jnp.arange(rows * top), side="right").astype(jnp.int32)
    table = labels.reshape(top, rows).T
    table = table[jax.random.permutation(jax.random.fold_in(own, 1), rows)]
    turn = jax.random.randint(jax.random.fold_in(own, 2), (rows, 1), 0, top)
    return jnp.take_along_axis(table, (jnp.arange(top)[None, :] + turn) % top, axis=1)


def shares(number_of, total, reach, lean, full):
    loads = [(1 << 20) // math.isqrt(grade ** lean) + 1 for grade in range(1, number_of + 1)]
    largest = reach if full else min(reach, max(-(-total // number_of), total * loads[0] // sum(loads)))
    least = 1 if total - largest >= number_of - 1 else 0
    holding, rest = [largest] + [least] * (number_of - 1), total - largest - least * (number_of - 1)
    while rest > 0:
        movable = [i for i in range(1, number_of) if holding[i] < largest] or [i for i in range(1, number_of) if holding[i] < reach]
        mass, budget = sum([loads[i] for i in movable]), rest
        for i in movable:
            addition = min(reach - holding[i], max(1, budget * loads[i] // mass), rest)
            holding[i] = holding[i] + addition
            rest = rest - addition
    return np.array(holding)


def centred(key, shape, deviation, most, cuts=(), held_as=jnp.bfloat16):
    values = jax.random.normal(key, shape, jnp.float32) * deviation
    if len(cuts) > 0:
        values = shard_levels(key, shape, cuts, -0.22, 0.18) * values
    return jnp.clip(values, min=-most, max=most).astype(held_as)


def gaussian_with(own_key, dims, width, limit, split, heavy, held_as=jnp.bfloat16):
    entries = width * jax.random.normal(own_key, dims, jnp.float32)
    if split:
        entries = entries * shard_levels(own_key, dims, split, -0.22, 0.18)
    return jnp.clip(strengthened(entries, jax.random.fold_in(own_key, 3), *heavy), -limit, limit).astype(held_as)


def setup_inputs(seed: int = 0) -> dict:
    streams_of = jax.random.split(jax.random.key(seed), 17)
    tokens = gaussian_with(streams_of[0], (TOKENS, D), 1.0, 6.0, ((0, 32),), (0, 1, 32, 2.75))
    attn_gain = jnp.clip(1.0 + 0.1 * jax.random.normal(streams_of[1], (D,), jnp.float32), 0.5, 1.5).astype(jnp.bfloat16)
    kv_gain = jnp.clip(1.0 + 0.1 * jax.random.normal(streams_of[2], (KVR,), jnp.float32), 0.5, 1.5).astype(jnp.bfloat16)
    ffn_gain = jnp.clip(1.0 + 0.1 * jax.random.normal(streams_of[3], (D,), jnp.float32), 0.5, 1.5).astype(jnp.bfloat16)
    q_weight = centred(streams_of[4], (D, H * (DH + DR)), D ** -0.5, 0.125, ((0, 32),))
    kv_down_weight = centred(streams_of[5], (D, KVR + DR), D ** -0.5, 0.125, ((0, 32),))
    kv_up_weight = centred(streams_of[6], (KVR, H * (DH + DV)), KVR ** -0.5, 0.25, ((0, 32),))
    out_weight = centred(streams_of[7], (H * DV, D), (H * DV // 16) ** -0.5, 0.5, ((0, 32),))
    shared_gate_up = centred(streams_of[8], (D, 2, FS), D ** -0.5, 0.125, ((0, 32),))
    shared_down = centred(streams_of[9], (FS, D), FS ** -0.5, 0.109375, ((0, 32),))
    expert_gate_up = centred(streams_of[10], (EXPERTS, D, 2, FE), D ** -0.5, 0.125, ((0, 16), (1, 2)))
    expert_down = centred(streams_of[11], (EXPERTS, FE, D), FE ** -0.5, 0.15625, ((0, 16), (1, 2)))
    routes_keys = jax.random.split(jax.random.fold_in(streams_of[12], 1), TOKENS // TOK_DEV)
    routes_turns = jax.random.permutation(jax.random.fold_in(streams_of[12], 3), TOKENS // TOK_DEV)
    routes = jax.vmap(lambda own, number: shared_out(jax.random.fold_in(streams_of[12], 2), own, number, TOK_DEV, EXPERTS, TOP, CAP, 1))(routes_keys, routes_turns).reshape((TOKENS, TOP))
    gates = jnp.clip(0.2 + 0.3 * jax.random.uniform(streams_of[13], (TOKENS, TOP), jnp.float32) ** shard_levels(streams_of[13], (TOKENS, TOP), ((0, 32),), -0.2, 0.2), 0.2, 0.5)
    lengths = jax.vmap(lambda own: uneven(own, DOCS, TOK_DEV, MOST_LEN, 1))(jax.random.split(streams_of[14], (N_DP * N_EXPERT))).reshape((N_DP * N_EXPERT, DOCS)).astype(jnp.int32)
    out_grad = centred(streams_of[15], (TOKENS, D), 1.0, 6.0, ((0, 32),))
    return {"tokens": tokens, "attn_gain": attn_gain, "kv_gain": kv_gain, "ffn_gain": ffn_gain, "q_weight": q_weight, "kv_down_weight": kv_down_weight, "kv_up_weight": kv_up_weight, "out_weight": out_weight, "shared_gate_up": shared_gate_up, "shared_down": shared_down, "expert_gate_up": expert_gate_up, "expert_down": expert_down, "routes": routes, "gates": gates, "lengths": lengths, "out_grad": out_grad}


norm_eps = 1e-06
rope_base = 50000.0
masked_score = -1e+30

@jax.custom_vjp
def low(v):
    return lax.optimization_barrier(v.astype(jnp.bfloat16)).astype(jnp.float32)

@jax.custom_vjp
def low_back(v):
    return v

def low_keep(v):
    return (low(v), None)

def low_pass(kept, grad):
    return (grad,)

def back_keep(v):
    return (v, None)

def back_low(kept, grad):
    return (low(grad),)
low.defvjp(low_keep, low_pass)
low_back.defvjp(back_keep, back_low)

def product(left, right):
    return jnp.dot(left, right, precision=lax.Precision.HIGHEST)

def norm_apply(values, scales):
    return values * lax.rsqrt(lax.optimization_barrier(jnp.mean(values * values, axis=-1, keepdims=True)) + norm_eps) * scales

def rotate(values, cosine_table, sine_table):
    half_width = values.shape[-1] // 2
    front_half = values[..., :half_width]
    back_half = values[..., half_width:]
    return jnp.concatenate([front_half * cosine_table - back_half * sine_table, front_half * sine_table + back_half * cosine_table], axis=-1)

def swish_gate(gate_up):
    gate_part = gate_up[..., 0, :]
    return gate_part * jax.nn.sigmoid(gate_part) * gate_up[..., 1, :]

def layout(lengths_row, row_count):
    doc_ends = jnp.cumsum(lengths_row).astype(jnp.int32)
    places = jnp.arange(row_count, dtype=jnp.int32)
    passed_end = (places[:, None] >= doc_ends[None, :]).astype(jnp.int32)
    doc_ids = lax.optimization_barrier(jnp.sum(passed_end, axis=1)).astype(jnp.int32)
    starts = lax.optimization_barrier(jnp.sum(passed_end * lengths_row[None, :].astype(jnp.int32), axis=1)).astype(jnp.int32)
    return (doc_ids, places - starts)

def angles(offsets, rope_width):
    frequency = rope_base ** (-2.0 * jnp.arange(rope_width // 2, dtype=jnp.float32) / rope_width)
    turned = offsets.astype(jnp.float32)[:, None] * frequency[None, :]
    return (jnp.cos(turned), jnp.sin(turned))

def attend_block(pieces):
    queries, key_heads, values, doc_ids = pieces
    places = jnp.arange(queries.shape[0], dtype=jnp.int32)
    allowed = (doc_ids[:, None] == doc_ids[None, :]) & (places[:, None] >= places[None, :])
    scores = jnp.einsum('thd,shd->hts', queries, key_heads, precision=lax.Precision.HIGHEST) * (DH + DR) ** (-0.5)
    scores = low_back(jnp.where(allowed[None], scores, masked_score))
    highest = lax.optimization_barrier(jnp.max(scores, axis=-1, keepdims=True))
    weights = jnp.exp(scores - highest)
    weights_low = low(weights / lax.optimization_barrier(jnp.sum(weights, axis=-1, keepdims=True)))
    return jnp.einsum('hts,shd->thd', weights_low, values, precision=lax.Precision.HIGHEST)

def forward(params, routes, gates, lengths):
    tokens, attn_gain, kv_gain, ffn_gain, q_weight, kv_down_weight, kv_up_weight, out_weight, shared_gate_up, shared_down, expert_gate_up, expert_down = params
    token_count = tokens.shape[0]
    blocks = token_count // TOK_DEV
    normed = low(norm_apply(tokens, attn_gain))
    q_heads = low_back(product(normed, q_weight)).reshape(token_count, H, DH + DR)
    kv_joint = low_back(product(normed, kv_down_weight))
    kv_normed = low(norm_apply(kv_joint[:, :KVR], kv_gain))
    kv_heads = low_back(product(kv_normed, kv_up_weight)).reshape(token_count, H, DH + DV)
    doc_ids, offsets = jax.vmap(lambda row: layout(row, TOK_DEV))(lengths)
    cosine_table, sine_table = angles(offsets.reshape(-1), DR)
    queries = low(jnp.concatenate([q_heads[..., :DH], rotate(q_heads[..., DH:], cosine_table[:, None], sine_table[:, None])], axis=-1))
    rope_key = rotate(kv_joint[:, KVR:], cosine_table, sine_table)
    key_heads = low(jnp.concatenate([kv_heads[..., :DH], jnp.broadcast_to(rope_key[:, None, :], (token_count, H, DR))], axis=-1))
    values = low(kv_heads[..., DH:])
    attended = lax.map(jax.checkpoint(attend_block), (queries.reshape(blocks, TOK_DEV, H, DH + DR), key_heads.reshape(blocks, TOK_DEV, H, DH + DR), values.reshape(blocks, TOK_DEV, H, DV), doc_ids))
    attended = low(low_back(attended.reshape(token_count, H * DV)))
    resid = tokens + low_back(product(attended, out_weight))
    ffn_in = low(norm_apply(resid, ffn_gain))
    shared_pair = low_back(jnp.einsum('td,dcf->tcf', ffn_in, shared_gate_up, precision=lax.Precision.HIGHEST))
    shared_term = product(low(swish_gate(shared_pair)), shared_down)
    picks = routes[:, :, None] == jnp.arange(EXPERTS, dtype=jnp.int32)[None, None, :]
    combined = lax.optimization_barrier(jnp.sum(gates[:, :, None] * picks.astype(jnp.float32), axis=1))

    def expert_step(running, pieces):
        pair_weight, down_weight, expert_share = pieces
        inputs = low_back(ffn_in)
        expert_pair = low_back(jnp.einsum('td,dcf->tcf', inputs, pair_weight, precision=lax.Precision.HIGHEST))
        hidden = low(swish_gate(expert_pair))
        result = low_back(low(product(hidden, down_weight)))
        return (running + expert_share[:, None] * result, None)
    routed_sum, unused = lax.scan(jax.checkpoint(expert_step), jnp.zeros(tokens.shape, jnp.float32), (expert_gate_up, expert_down, combined.T))
    return resid + shared_term + routed_sum

def reference(tokens, attn_gain, kv_gain, ffn_gain, q_weight, kv_down_weight, kv_up_weight, out_weight, shared_gate_up, shared_down, expert_gate_up, expert_down, routes, gates, lengths, out_grad):
    params = tuple((item.astype(jnp.float32) for item in (tokens, attn_gain, kv_gain, ffn_gain, q_weight, kv_down_weight, kv_up_weight, out_weight, shared_gate_up, shared_down, expert_gate_up, expert_down)))
    result, pullback = jax.vjp(lambda *items: forward(items, routes, gates.astype(jnp.float32), lengths), *params)
    gradients = pullback(out_grad.astype(jnp.float32))
    return (result.astype(jnp.bfloat16), gradients[0].astype(jnp.bfloat16), gradients[1], gradients[2], gradients[3], gradients[4], gradients[5], gradients[6], gradients[7], gradients[8], gradients[9], gradients[10], gradients[11])
```

```python
import jax
import jax.numpy as jnp
from jax import lax
from jax.sharding import PartitionSpec as P

H = 16
DH = 128
DR = 64
DV = 128
KVR = 512
TOP = 6
SPLIT = ("dp", "expert")

f32 = jnp.float32
bf16 = jnp.bfloat16

norm_eps = 1e-06
rope_base = 50000.0
masked_score = -1e30


def norm_apply(values, scales):
    return values * lax.rsqrt(jnp.mean(values * values, axis=-1, keepdims=True) + norm_eps) * scales


def norm_back(values, scales, upstream):
    unused, pullback = jax.vjp(norm_apply, values, scales.astype(f32))
    return pullback(upstream)


def rotate(values, cosine_table, sine_table):
    half_width = values.shape[-1] // 2
    front_half = values[..., :half_width]
    back_half = values[..., half_width:]
    return jnp.concatenate(
        [
            front_half * cosine_table - back_half * sine_table,
            front_half * sine_table + back_half * cosine_table,
        ],
        axis=-1,
    )


def swish_gate(gate_part, up_part):
    return gate_part * jax.nn.sigmoid(gate_part) * up_part


def swish_back(gate_part, up_part, upstream):
    unused, pullback = jax.vjp(swish_gate, gate_part, up_part)
    return jnp.concatenate(pullback(upstream), axis=-1)


def layout(lengths_row, row_count):
    doc_ends = jnp.cumsum(lengths_row)
    places = jnp.arange(row_count, dtype=jnp.int32)
    passed_end = (places[:, None] >= doc_ends[None, :]).astype(jnp.int32)
    doc_ids = jnp.sum(passed_end, axis=1)
    starts = jnp.sum(passed_end * lengths_row[None, :], axis=1)
    return (doc_ids, places - starts)


def angles(offsets, rope_width):
    frequency = rope_base ** (-2.0 * jnp.arange(rope_width // 2, dtype=f32) / rope_width)
    turned = offsets.astype(f32)[..., None] * frequency
    return (jnp.cos(turned), jnp.sin(turned))


def dot(left, right):
    return jnp.dot(left, right, preferred_element_type=f32)


def pick(values, place, axis):
    return lax.dynamic_index_in_dim(values, place, axis, keepdims=False)


def dp_gather(values):
    if lax.axis_size("dp") != 2:
        return lax.all_gather(values, "dp")
    other = lax.ppermute(values, "dp", [(0, 1), (1, 0)])
    first = lax.axis_index("dp") == 0
    return jnp.stack([jnp.where(first, values, other), jnp.where(first, other, values)])


def dp_swap(values):
    if lax.axis_size("dp") != 2:
        return lax.all_to_all(values, "dp", split_axis=0, concat_axis=0)
    core = lax.axis_index("dp")
    own = pick(values, core, 0)
    other = lax.ppermute(pick(values, 1 - core, 0), "dp", [(0, 1), (1, 0)])
    first = core == 0
    return jnp.stack([jnp.where(first, own, other), jnp.where(first, other, own)])


def dp_scatter(values, sent=f32):
    if lax.axis_size("dp") != 2:
        return lax.psum_scatter(values.astype(sent), "dp", scatter_dimension=0).astype(f32)
    core = lax.axis_index("dp")
    other = lax.ppermute(pick(values, 1 - core, 0).astype(sent), "dp", [(0, 1), (1, 0)])
    return pick(values, core, 0).astype(f32) + other.astype(f32)


def dp_sum(values):
    if lax.axis_size("dp") != 2:
        return lax.psum(values, "dp")
    return values + lax.ppermute(values, "dp", [(0, 1), (1, 0)])


def bits_of(count):
    return [1 << place for place in reversed(range(count.bit_length() - 1))]


def partner(values, bit):
    count = lax.axis_size("expert")
    return lax.ppermute(values, "expert", [(i, i ^ bit) for i in range(count)])


def gather(values, order):
    me = lax.axis_index("expert")
    held = []
    for bit in order:
        other = partner(values, bit)
        low = (me & bit) == 0
        values = jnp.stack(
            [jnp.where(low, values, other), jnp.where(low, other, values)],
            axis=sum(1 for known in held if known > bit),
        )
        held.append(bit)
    return values.reshape((-1,) + values.shape[len(held) :])


def scatter(values, order, kept=f32):
    me = lax.axis_index("expert")
    bits = bits_of(lax.axis_size("expert"))
    values = values.reshape((2,) * len(bits) + values.shape[1:])
    for step, bit in enumerate(order):
        axis = bits.index(bit)
        bits = [known for known in bits if known != bit]
        place = ((me & bit) != 0).astype(jnp.int32)
        other = partner(pick(values, 1 - place, axis), bit)
        values = pick(values, place, axis).astype(f32) + other.astype(f32)
        values = values.astype(bf16 if bits else kept)
    return values


def gather_near(values, order):
    held = []
    for bit in order:
        other = partner(values, bit)
        values = jnp.stack([values, other], axis=sum(1 for known in held if known > bit))
        held.append(bit)
    return values.reshape((-1,) + values.shape[len(held) :])


def scatter_near(values, order, kept=f32):
    bits = bits_of(lax.axis_size("expert"))
    values = values.reshape((2,) * len(bits) + values.shape[1:])
    for step, bit in enumerate(order):
        axis = bits.index(bit)
        bits = [known for known in bits if known != bit]
        other = partner(lax.index_in_dim(values, 1, axis, keepdims=False), bit)
        values = lax.index_in_dim(values, 0, axis, keepdims=False).astype(f32) + other.astype(f32)
        values = values.astype(bf16 if bits else kept)
    return values


def orders():
    bits = bits_of(lax.axis_size("expert"))
    return bits, bits[:-2] + bits[-1:] + bits[-2:-1]


def gather_both(values, how):
    first, second = orders()
    middle = values.shape[-1] // 2
    return how(values[..., :middle], first), how(values[..., middle:], second)


def scatter_both(left, right, how):
    first, second = orders()
    return jnp.concatenate([how(left, first[::-1]), how(right, second[::-1])], axis=-1)


def shards(
    tokens,
    attn_gain,
    kv_gain,
    ffn_gain,
    q_weight,
    kv_down_weight,
    kv_up_weight,
    out_weight,
    shared_gate_up,
    shared_down,
    expert_gate_up,
    expert_down,
    routes,
    gates,
    lengths,
    out_grad,
):
    row_count, width = tokens.shape
    dp_count = lax.axis_size("dp")
    expert_count = lax.axis_size("expert")
    core = lax.axis_index("dp")
    me = lax.axis_index("expert")
    heads = H // dp_count
    scale_factor = (DH + DR) ** (-0.5)
    first_order, second_order = orders()
    chip_rows = dp_count * row_count
    slice_rows = kv_down_weight.shape[0]
    joint_width = KVR + DR

    combined = jnp.sum(
        jnp.where(
            routes[:, :, None] == jnp.arange(expert_count, dtype=jnp.int32),
            gates[:, :, None],
            0.0,
        ),
        axis=1,
    )
    gates_high = lax.reduce_precision(combined, 8, 7)
    gates_low = (combined - gates_high).astype(bf16)
    gates_flat = jnp.stack([gates_high.astype(bf16), gates_low]).reshape(-1)
    gate_rows = -(-gates_flat.shape[0] // joint_width)
    gates_flat = jnp.pad(gates_flat, (0, gate_rows * joint_width - gates_flat.shape[0]))
    gains = jnp.concatenate([attn_gain, ffn_gain, kv_gain])
    n_gain, n_kv_gain = attn_gain.shape[0], kv_gain.shape[0]
    gains = jnp.pad(gains, (0, joint_width - gains.shape[0]))
    small = jnp.concatenate(
        [kv_down_weight, gains[None], gates_flat.reshape(gate_rows, joint_width)], axis=0
    )
    small_all = gather(small, second_order)
    gates_all = small_all[:, slice_rows + 1 :].reshape(expert_count, -1)
    gates_all = gates_all[:, : 2 * row_count * expert_count]
    gates_all = gates_all.reshape(expert_count, 2, row_count, expert_count)
    near = me ^ jnp.arange(expert_count, dtype=jnp.int32)
    own_gate = jnp.take(pick(gates_all, me, 3).astype(f32).sum(axis=1), near, axis=0)

    joint_all = dp_gather(small_all[:, : slice_rows + 1])
    kv_down = joint_all[:, :, :slice_rows].reshape(width, joint_width)
    gains_all = joint_all[:, :, slice_rows]
    attn_scale = gains_all[..., :n_gain].reshape(-1)
    ffn_scale = gains_all[..., n_gain : 2 * n_gain].reshape(-1)
    kv_scale = gains_all[..., 2 * n_gain : 2 * n_gain + n_kv_gain].reshape(-1)

    q_own = dp_swap(q_weight.reshape(slice_rows, dp_count, -1).transpose(1, 0, 2))
    q_left, q_right = gather_both(q_own, gather)
    q_full = jnp.concatenate([q_left, q_right], axis=-1).transpose(1, 0, 2, 3)
    q_full = q_full.reshape(width, heads * (DH + DR))
    up_own = dp_swap(kv_up_weight.reshape(n_kv_gain, dp_count, -1).transpose(1, 0, 2))
    kv_up = gather(up_own, first_order).transpose(1, 0, 2, 3).reshape(KVR, heads * (DH + DV))
    out_left, out_right = gather_both(out_weight, gather)
    out_full = jnp.concatenate([out_left, out_right], axis=-1).reshape(heads * DV, width)

    pair_w = dp_gather(expert_gate_up[0].reshape(width // dp_count, -1)).reshape(width, -1)
    down_w = dp_gather(expert_down[0]).reshape(-1, width)
    hidden = down_w.shape[0]

    share = shared_down.shape[0]
    units = dp_count * share
    padded = -(-units // 128) * 128
    shared_w = shared_gate_up.reshape(slice_rows, 2, dp_count, expert_count, share)
    shared_w = shared_w.transpose(3, 0, 1, 2, 4).reshape(expert_count, slice_rows, 2 * units)
    shared_w = lax.all_to_all(shared_w, "expert", split_axis=0, concat_axis=0, tiled=True)
    shared_w = dp_gather(shared_w).reshape(width, 2, units)
    shared_w = jnp.pad(shared_w, ((0, 0), (0, 0), (0, padded - units))).reshape(width, 2 * padded)
    shared_out = dp_gather(shared_down).reshape(units, width)
    shared_out = jnp.pad(shared_out, ((0, padded - units), (0, 0)))

    resid_in = tokens.astype(f32)
    chip_in = dp_gather(tokens).reshape(chip_rows, width).astype(f32)
    normed = norm_apply(chip_in, attn_scale).astype(bf16)
    kv_joint = dot(normed, kv_down)
    latent = kv_joint[:, :KVR]
    kv_normed = norm_apply(latent, kv_scale).astype(bf16)
    q_heads = dot(normed, q_full).reshape(dp_count, row_count, heads, DH + DR)
    kv_heads = dot(kv_normed, kv_up).reshape(dp_count, row_count, heads, DH + DV)
    doc_ids, offsets = jax.vmap(lambda row: layout(row, row_count))(
        dp_gather(lengths).reshape(dp_count, -1)
    )
    cosine_table, sine_table = angles(offsets, DR)
    cosine_heads, sine_heads = cosine_table[:, :, None], sine_table[:, :, None]
    queries = jnp.concatenate(
        [q_heads[..., :DH], rotate(q_heads[..., DH:], cosine_heads, sine_heads)], axis=-1
    ).astype(bf16)
    rope_key = rotate(
        kv_joint[:, KVR:].reshape(dp_count, row_count, DR), cosine_table, sine_table
    )
    key_heads = jnp.concatenate(
        [
            kv_heads[..., :DH],
            jnp.broadcast_to(rope_key[:, :, None, :], (dp_count, row_count, heads, DR)),
        ],
        axis=-1,
    ).astype(bf16)
    values = kv_heads[..., DH:].astype(bf16)
    places = jnp.arange(row_count, dtype=jnp.int32)
    allowed = (doc_ids[:, :, None] == doc_ids[:, None, :]) & (places[:, None] >= places[None, :])
    scores = (
        jnp.einsum("bthd,bshd->bhts", queries, key_heads, preferred_element_type=f32)
        * scale_factor
    )
    scores = jnp.where(allowed[:, None], scores, masked_score)
    highest = jnp.max(scores, axis=-1, keepdims=True)
    weights = jnp.exp(scores - highest)
    probs = weights / jnp.sum(weights, axis=-1, keepdims=True)
    probs_low = probs.astype(bf16)
    attended = (
        jnp.einsum("bhts,bshd->bthd", probs_low, values, preferred_element_type=f32)
        .reshape(chip_rows, heads * DV)
        .astype(bf16)
    )
    resid = resid_in + dp_scatter(dot(attended, out_full).reshape(dp_count, row_count, width))
    ffn_in = norm_apply(resid, ffn_scale).astype(bf16)

    capacity = min(row_count, 3 * row_count * TOP // (2 * expert_count))
    slots = expert_count * capacity
    group_rows = expert_count * row_count
    live = own_gate > 0.0
    place = jnp.cumsum(live.astype(jnp.int32), axis=1) - 1
    chosen = (jnp.arange(capacity, dtype=jnp.int32)[None, :, None] == place[:, None, :]) & live[
        :, None, :
    ]
    slot_gate = jnp.sum(jnp.where(chosen, own_gate[:, None, :], 0.0), axis=2).reshape(slots, 1)
    chosen = chosen.astype(bf16)

    upstream = out_grad.astype(f32)
    grad_all = jnp.concatenate(gather_both(out_grad, gather_near), axis=-1)
    slot_grad = (
        jnp.einsum("rst,rtd->rsd", chosen, grad_all, preferred_element_type=f32).reshape(slots, width)
        * slot_gate
    ).astype(bf16)
    grad_rows = grad_all.reshape(group_rows, width)
    d_hidden = dot(slot_grad, down_w.T)
    d_shared_hidden = dot(grad_rows, shared_out.T)

    ffn_all = jnp.concatenate(gather_both(ffn_in, gather_near), axis=-1)
    ffn_rows = ffn_all.reshape(group_rows, width)
    rows = jnp.einsum("rst,rtd->rsd", chosen, ffn_all, preferred_element_type=f32)
    rows = rows.reshape(slots, width).astype(bf16)
    pair = dot(rows, pair_w)
    gate_part, up_part = pair[:, :hidden], pair[:, hidden:]
    expert_hidden = swish_gate(gate_part, up_part).astype(bf16)
    d_pair = swish_back(gate_part, up_part, d_hidden).astype(bf16)
    shared_pair = dot(ffn_rows, shared_w)
    shared_gate, shared_up = shared_pair[:, :padded], shared_pair[:, padded:]
    shared_hidden = swish_gate(shared_gate, shared_up).astype(bf16)
    d_shared_pair = swish_back(shared_gate, shared_up, d_shared_hidden).astype(bf16)

    middle = width // 2

    def to_tokens(slot_rows, shared_rows, shared_matrix):
        back = jnp.einsum(
            "rst,rsd->rtd",
            chosen,
            slot_rows.reshape(expert_count, capacity, -1),
            preferred_element_type=f32,
        )
        back = back.reshape(group_rows, -1) + dot(shared_rows, shared_matrix)
        return back.astype(bf16).reshape(expert_count, row_count, -1)

    d_parts = [
        to_tokens(dot(d_pair, part.T).astype(bf16), d_shared_pair, shared_part.T)
        for part, shared_part in (
            (pair_w[:middle], shared_w[:middle]),
            (pair_w[middle:], shared_w[middle:]),
        )
    ]
    d_ffn_in = scatter_both(d_parts[0], d_parts[1], scatter_near)

    out_parts = [
        to_tokens(
            (dot(expert_hidden, part) * slot_gate).astype(bf16), shared_hidden, shared_part
        )
        for part, shared_part in (
            (down_w[:, :middle], shared_out[:, :middle]),
            (down_w[:, middle:], shared_out[:, middle:]),
        )
    ]
    output = (resid + scatter_both(out_parts[0], out_parts[1], scatter_near)).astype(bf16)

    grad_pair = dp_scatter(dot(rows.T, d_pair).reshape(dp_count, width // dp_count, -1), bf16)
    grad_down = dp_scatter(
        dot(expert_hidden.T, slot_grad).reshape(dp_count, hidden // dp_count, width), bf16
    )
    grad_shared_out = dp_scatter(
        dot(shared_hidden.T, grad_rows)[:units].reshape(dp_count, share, width), bf16
    )
    grad_shared = dot(ffn_rows.T, d_shared_pair).reshape(width, 2, padded)[:, :, :units]
    grad_shared = grad_shared.reshape(dp_count, expert_count, slice_rows, 2 * units)
    grad_shared = dp_scatter(grad_shared, bf16).astype(bf16)
    grad_shared = lax.all_to_all(grad_shared, "expert", split_axis=0, concat_axis=0, tiled=True)
    grad_shared = grad_shared.reshape(expert_count, slice_rows, 2, dp_count, share)
    grad_shared = grad_shared.transpose(1, 2, 3, 0, 4).reshape(shared_gate_up.shape).astype(f32)

    d_norm_resid, grad_ffn_scale = norm_back(resid, ffn_scale, d_ffn_in)
    d_resid = upstream + d_norm_resid
    d_branch = dp_gather(d_resid.astype(bf16)).reshape(chip_rows, width)
    d_attended = (
        dot(d_branch, out_full.T).astype(bf16).reshape(dp_count, row_count, heads, DV)
    )
    out_blocks = (expert_count, slice_rows, middle)
    grad_out = scatter_both(
        dot(attended.T, d_branch[:, :middle]).astype(bf16).reshape(out_blocks),
        dot(attended.T, d_branch[:, middle:]).astype(bf16).reshape(out_blocks),
        scatter,
    )
    grad_values = jnp.einsum("bhts,bthd->bshd", probs_low, d_attended, preferred_element_type=f32)
    d_probs = jnp.einsum("bthd,bshd->bhts", d_attended, values, preferred_element_type=f32)
    d_scores = (probs * (d_probs - jnp.sum(d_probs * probs, axis=-1, keepdims=True))).astype(bf16)
    d_queries = (
        jnp.einsum("bhts,bshd->bthd", d_scores, key_heads, preferred_element_type=f32)
        * scale_factor
    )
    d_keys = (
        jnp.einsum("bhts,bthd->bshd", d_scores, queries, preferred_element_type=f32)
        * scale_factor
    )
    d_q_heads = jnp.concatenate(
        [d_queries[..., :DH], rotate(d_queries[..., DH:], cosine_heads, -sine_heads)], axis=-1
    )
    d_q_heads = d_q_heads.astype(bf16).reshape(chip_rows, heads * (DH + DR))
    d_rope_key = rotate(jnp.sum(d_keys[..., DH:], axis=2), cosine_table, -sine_table)
    d_kv_heads = (
        jnp.concatenate([d_keys[..., :DH], grad_values], axis=-1)
        .astype(bf16)
        .reshape(chip_rows, heads * (DH + DV))
    )
    d_joint = dp_sum(
        jnp.concatenate([dot(d_kv_heads, kv_up.T), d_rope_key.reshape(chip_rows, DR)], axis=-1)
    )
    d_latent, grad_kv_scale = norm_back(latent, kv_scale, d_joint[:, :KVR])
    d_kv_joint = jnp.concatenate([d_latent, d_joint[:, KVR:]], axis=-1).astype(bf16)

    q_cols = heads * (DH + DR) // 2
    by_rows = (dp_count, expert_count, slice_rows)

    def q_part(part):
        found = dot(normed.T, part).astype(bf16).reshape(by_rows + (part.shape[-1],))
        return found.transpose(1, 0, 2, 3)

    grad_q = scatter_both(q_part(d_q_heads[:, :q_cols]), q_part(d_q_heads[:, q_cols:]), scatter)
    grad_q = dp_swap(grad_q.astype(bf16)).transpose(1, 0, 2).reshape(q_weight.shape).astype(f32)
    grad_up = dot(kv_normed.T, d_kv_heads).astype(bf16)
    grad_up = grad_up.reshape(dp_count, expert_count, n_kv_gain, -1).transpose(1, 0, 2, 3)
    grad_up = scatter(grad_up, first_order[::-1])
    grad_up = dp_swap(grad_up.astype(bf16)).transpose(1, 0, 2)
    grad_up = grad_up.reshape(kv_up_weight.shape).astype(f32)

    d_normed = dp_scatter(dot(d_q_heads, q_full.T).reshape(dp_count, row_count, width))
    own_joint = pick(d_kv_joint.reshape(dp_count, row_count, joint_width), core, 0)
    d_normed = d_normed + dot(own_joint, kv_down.T)
    d_norm_in, grad_attn_scale = norm_back(resid_in, attn_scale, d_normed)
    grad_in = (d_resid + d_norm_in).astype(bf16)

    own_normed = pick(normed.reshape(chip_rows, dp_count, width // dp_count), core, 1)
    grad_kvdown = dot(own_normed.T, d_kv_joint).reshape(expert_count, slice_rows, joint_width)
    scale_sums = dp_scatter(
        jnp.concatenate(
            [
                grad_attn_scale.reshape(dp_count, expert_count, n_gain),
                grad_ffn_scale.reshape(dp_count, expert_count, n_gain),
            ],
            axis=-1,
        )
    )
    kv_sums = pick(grad_kv_scale.reshape(dp_count, expert_count, n_kv_gain), core, 0)
    scale_sums = jnp.concatenate([scale_sums, kv_sums], axis=-1)
    scale_sums = jnp.pad(scale_sums, ((0, 0), (0, joint_width - scale_sums.shape[-1])))
    small_sums = scatter(
        jnp.concatenate([grad_kvdown, scale_sums[:, None]], axis=1).astype(bf16),
        second_order[::-1],
    )
    grad_kvdown = small_sums[:slice_rows]
    scale_sums = small_sums[slice_rows]

    return (
        output,
        grad_in,
        scale_sums[:n_gain],
        scale_sums[2 * n_gain : 2 * n_gain + n_kv_gain],
        scale_sums[n_gain : 2 * n_gain],
        grad_q,
        grad_kvdown,
        grad_up,
        grad_out,
        grad_shared,
        grad_shared_out,
        grad_pair.reshape(expert_gate_up.shape),
        grad_down.reshape(expert_down.shape),
    )


def solution(mesh):
    rows = P(SPLIT, None)
    each = P(SPLIT)
    cube = P(SPLIT, None, None)
    pair = P("expert", "dp", None, None)
    down = P("expert", "dp", None)
    dense = (rows, rows, rows, rows, cube, rows)
    return jax.shard_map(
        shards,
        mesh=mesh,
        in_specs=(rows, each, each, each) + dense + (pair, down, rows, rows, rows, rows),
        out_specs=(rows, rows, each, each, each) + dense + (pair, down),
        check_vma=False,
    )
```

```python
import functools

import jax
import jax.numpy as jnp
from jax import lax
from jax.experimental import pallas as pl
from jax.experimental.pallas import tpu as pltpu
from jax.sharding import PartitionSpec as P

H = 16
DH = 128
DR = 64
DV = 128
KVR = 512
TOP = 6
SPLIT = ("dp", "expert")
ROPE_LANES = 128

f32 = jnp.float32
bf16 = jnp.bfloat16

norm_eps = 1e-06
rope_base = 50000.0
masked_score = -1e30


def norm_apply(values, scales):
    return values * lax.rsqrt(jnp.mean(values * values, axis=-1, keepdims=True) + norm_eps) * scales


def norm_back(values, scales, upstream):
    unused, pullback = jax.vjp(norm_apply, values, scales.astype(f32))
    return pullback(upstream)


def rotate(values, cosine_table, sine_table):
    half_width = values.shape[-1] // 2
    front_half = values[..., :half_width]
    back_half = values[..., half_width:]
    return jnp.concatenate(
        [
            front_half * cosine_table - back_half * sine_table,
            front_half * sine_table + back_half * cosine_table,
        ],
        axis=-1,
    )


def swish_gate(gate_part, up_part):
    return gate_part * jax.nn.sigmoid(gate_part) * up_part


def swish_back(gate_part, up_part, upstream):
    unused, pullback = jax.vjp(swish_gate, gate_part, up_part)
    return jnp.concatenate(pullback(upstream), axis=-1)


def layout(lengths_row, row_count):
    doc_ends = jnp.cumsum(lengths_row)
    places = jnp.arange(row_count, dtype=jnp.int32)
    passed_end = (places[:, None] >= doc_ends[None, :]).astype(jnp.int32)
    doc_ids = jnp.sum(passed_end, axis=1)
    starts = jnp.sum(passed_end * lengths_row[None, :], axis=1)
    return (doc_ids, places - starts)


def angles(offsets, rope_width):
    frequency = rope_base ** (-2.0 * jnp.arange(rope_width // 2, dtype=f32) / rope_width)
    turned = offsets.astype(f32)[..., None] * frequency
    return (jnp.cos(turned), jnp.sin(turned))


def dot(left, right):
    return jnp.dot(left, right, preferred_element_type=f32)


def pick(values, place, axis):
    return lax.dynamic_index_in_dim(values, place, axis, keepdims=False)


def dp_gather(values):
    if lax.axis_size("dp") != 2:
        return lax.all_gather(values, "dp")
    other = lax.ppermute(values, "dp", [(0, 1), (1, 0)])
    first = lax.axis_index("dp") == 0
    return jnp.stack([jnp.where(first, values, other), jnp.where(first, other, values)])


def dp_swap(values):
    if lax.axis_size("dp") != 2:
        return lax.all_to_all(values, "dp", split_axis=0, concat_axis=0)
    core = lax.axis_index("dp")
    own = pick(values, core, 0)
    other = lax.ppermute(pick(values, 1 - core, 0), "dp", [(0, 1), (1, 0)])
    first = core == 0
    return jnp.stack([jnp.where(first, own, other), jnp.where(first, other, own)])


def dp_scatter(values, sent=f32):
    if lax.axis_size("dp") != 2:
        return lax.psum_scatter(values.astype(sent), "dp", scatter_dimension=0).astype(f32)
    core = lax.axis_index("dp")
    other = lax.ppermute(pick(values, 1 - core, 0).astype(sent), "dp", [(0, 1), (1, 0)])
    return pick(values, core, 0).astype(f32) + other.astype(f32)


def dp_sum(values):
    if lax.axis_size("dp") != 2:
        return lax.psum(values, "dp")
    return values + lax.ppermute(values, "dp", [(0, 1), (1, 0)])


def bits_of(count):
    return [1 << place for place in reversed(range(count.bit_length() - 1))]


def partner(values, bit):
    count = lax.axis_size("expert")
    return lax.ppermute(values, "expert", [(i, i ^ bit) for i in range(count)])


def gathering(values, order, held=(), lead=0):
    me = lax.axis_index("expert")
    held = list(held)
    for bit in order:
        other = yield partner(values, bit)
        low = (me & bit) == 0
        values = jnp.stack(
            [jnp.where(low, values, other), jnp.where(low, other, values)],
            axis=lead + sum(1 for known in held if known > bit),
        )
        held.append(bit)
    return values.reshape(values.shape[:lead] + (-1,) + values.shape[lead + len(held) :])


def scattering(values, order, bits, kept=f32, lead=0):
    me = lax.axis_index("expert")
    bits = list(bits)
    values = values.reshape(values.shape[:lead] + (2,) * len(bits) + values.shape[lead + 1 :])
    for step, bit in enumerate(order):
        axis = lead + bits.index(bit)
        bits.remove(bit)
        place = ((me & bit) != 0).astype(jnp.int32)
        other = yield partner(pick(values, 1 - place, axis), bit)
        values = pick(values, place, axis).astype(f32) + other.astype(f32)
        values = values.astype(kept if step + 1 == len(order) else bf16)
    if bits:
        values = values.reshape(values.shape[:lead] + (-1,) + values.shape[lead + len(bits) :])
    return values


def later(steps, values, chain):
    for _ in range(steps):
        values = yield values
    return (yield from chain(values))


def begun(chain, values):
    while True:
        try:
            values = chain.send(values)
        except StopIteration as stop:
            return stop.value
        values = yield values


def last_of(chain, values):
    try:
        chain.send(values)
    except StopIteration as stop:
        return stop.value


def pair_swapping(values, bit, axis):
    place = ((lax.axis_index("expert") & bit) != 0).astype(jnp.int32)
    own = pick(values, place, axis)
    other = yield partner(pick(values, 1 - place, axis), bit)
    low = place == 0
    return jnp.stack([jnp.where(low, own, other), jnp.where(low, other, own)])


def march(*chains, jobs=()):
    results, found = [None] * len(chains), []
    live = {i: next(chain) for i, chain in enumerate(chains)}
    waiting = [operands for _, *operands in jobs]
    while live or len(found) < len(jobs):
        step = len(found)
        job = jobs[step][0](results, found, *waiting[step]) if step < len(jobs) else ()
        live, job, waiting = lax.optimization_barrier((live, job, waiting[step + 1 :]))
        waiting = [()] * (step + 1) + waiting
        found.append(job)
        following = {}
        for i, values in live.items():
            try:
                following[i] = chains[i].send(values)
            except StopIteration as stop:
                results[i] = stop.value
        live = following
    return results, found


def skip(results, found):
    return ()


def alone(chain, *markers):
    values = next(chain)
    step = 0
    while True:
        if step < len(markers):
            values = after(values, markers[step])
        step += 1
        try:
            values = chain.send(values)
        except StopIteration as stop:
            return stop.value


def after(values, *others):
    return lax.optimization_barrier((values, others))[0]


def thirds(width):
    side = width // 128 // 3 * 128
    return (0, side), (side, width - side), (width - side, width)


def whole_orders(bits, pair_bit):
    far, second, first = [bit for bit in bits if bit != pair_bit]
    return (
        (second, far, first, pair_bit),
        (far, first, pair_bit, second),
        (far, pair_bit, second, first),
    )


def lanes_dot(left, right):
    return lax.dot_general(left, right, (((1,), (1,)), ((), ())), preferred_element_type=f32)


def rows_dot(left, right):
    return lax.dot_general(left, right, (((0,), (0,)), ((), ())), preferred_element_type=f32)


def head_lanes(heads):
    lane = lax.broadcasted_iota(jnp.int32, (1, ROPE_LANES), 1) // (DR // 2)
    return [(lane == head).astype(f32) for head in range(heads)]


def attend_kernel(
    heads,
    x_ref,
    gain_ref,
    kv_gain_ref,
    down_ref,
    q_ref,
    up_ref,
    out_ref,
    cos_ref,
    sin_ref,
    column_ref,
    row_ref,
    normed_ref,
    joint_ref,
    kv_normed_ref,
    heads_ref,
    keys_ref,
    values_ref,
    probs_ref,
    attended_ref,
    sum_ref,
):
    nope = heads * DH
    rows = x_ref.shape[0]
    x = x_ref[...].astype(f32)
    scale = lax.rsqrt(jnp.mean(x * x, axis=-1, keepdims=True) + norm_eps)
    normed_ref[...] = (x * scale * gain_ref[...]).astype(bf16)
    joint_ref[...] = dot(normed_ref[...], down_ref[...])
    latent = joint_ref[:, :KVR]
    scale = lax.rsqrt(jnp.mean(latent * latent, axis=-1, keepdims=True) + norm_eps)
    kv_normed_ref[...] = (latent * scale * kv_gain_ref[...]).astype(bf16)
    cos, sin = cos_ref[...], sin_ref[...]
    front = joint_ref[:, KVR : KVR + ROPE_LANES]
    back = joint_ref[:, KVR + ROPE_LANES :]
    keys_ref[:, nope : nope + ROPE_LANES] = (front * cos - back * sin).astype(bf16)
    keys_ref[:, nope + ROPE_LANES :] = (front * sin + back * cos).astype(bf16)
    q = dot(normed_ref[...], q_ref[:, : nope + 2 * ROPE_LANES])
    front = q[:, nope : nope + ROPE_LANES]
    back = q[:, nope + ROPE_LANES :]
    heads_ref[:, :nope] = q[:, :nope].astype(bf16)
    heads_ref[:, nope : nope + ROPE_LANES] = (front * cos - back * sin).astype(bf16)
    heads_ref[:, nope + ROPE_LANES :] = (front * sin + back * cos).astype(bf16)
    kv = dot(kv_normed_ref[...], up_ref[...])
    for head in range(heads):
        start = head * (DH + DV)
        keys_ref[:, head * DH : (head + 1) * DH] = kv[:, start : start + DH].astype(bf16)
        values_ref[:, head * DV : (head + 1) * DV] = kv[:, start + DH : start + DH + DV].astype(bf16)
    tile = probs_ref.shape[-1]
    causal = lax.broadcasted_iota(jnp.int32, (tile, tile), 0) >= lax.broadcasted_iota(
        jnp.int32, (tile, tile), 1
    )
    own = head_lanes(heads)
    for block in range(rows // tile):
        part = pl.ds(block * tile, tile)
        allowed = (column_ref[part, :] == row_ref[block]) & causal
        rotary = heads_ref[part, nope:].astype(f32)
        for head in range(heads):
            both = jnp.concatenate([own[head], own[head]], axis=-1)
            scores = lanes_dot(
                heads_ref[part, head * DH : (head + 1) * DH],
                keys_ref[part, head * DH : (head + 1) * DH],
            ) + lanes_dot((rotary * both).astype(bf16), keys_ref[part, nope:])
            scores = jnp.where(allowed, scores * (DH + DR) ** (-0.5), masked_score)
            weights = jnp.exp(scores - jnp.max(scores, axis=-1, keepdims=True))
            probs = weights / jnp.sum(weights, axis=-1, keepdims=True)
            probs_ref[block * heads + head] = probs
            attended_ref[part, head * DV : (head + 1) * DV] = dot(
                probs.astype(bf16), values_ref[part, head * DV : (head + 1) * DV]
            ).astype(bf16)
    sum_ref[...] = dot(attended_ref[...], out_ref[...]).astype(sum_ref.dtype)


def attend_back_kernel(
    heads,
    branch_ref,
    out_ref,
    probs_ref,
    heads_ref,
    keys_ref,
    values_ref,
    joint_ref,
    kv_gain_ref,
    up_ref,
    q_ref,
    down_ref,
    cos_ref,
    sin_ref,
    d_q_ref,
    d_kv_ref,
    d_joint_ref,
    d_gain_ref,
    sum_ref,
    d_key_ref,
):
    nope = heads * DH
    rows = branch_ref.shape[0]
    tile = probs_ref.shape[-1]
    factor = (DH + DR) ** (-0.5)
    d_attended = lanes_dot(branch_ref[...], out_ref[...]).astype(bf16)
    own = head_lanes(heads)
    for block in range(rows // tile):
        part = slice(block * tile, (block + 1) * tile)
        rotary = heads_ref[part, nope:].astype(f32)
        d_rotary = jnp.zeros((tile, 2 * ROPE_LANES), f32)
        d_key = jnp.zeros((tile, 2 * ROPE_LANES), f32)
        for head in range(heads):
            both = jnp.concatenate([own[head], own[head]], axis=-1)
            columns = slice(head * DH, (head + 1) * DH)
            start = head * (DH + DV)
            upstream = d_attended[part, head * DV : (head + 1) * DV]
            probs = probs_ref[block * heads + head]
            d_kv_ref[part, start + DH : start + DH + DV] = rows_dot(
                probs.astype(bf16), upstream
            ).astype(bf16)
            d_probs = lanes_dot(upstream, values_ref[part, head * DV : (head + 1) * DV])
            d_scores = probs * (d_probs - jnp.sum(d_probs * probs, axis=-1, keepdims=True))
            d_scores = d_scores.astype(bf16)
            d_q_ref[part, columns] = (dot(d_scores, keys_ref[part, columns]) * factor).astype(bf16)
            d_rotary = d_rotary + dot(d_scores, keys_ref[part, nope:]) * (factor * both)
            d_kv_ref[part, start : start + DH] = (
                rows_dot(d_scores, heads_ref[part, columns]) * factor
            ).astype(bf16)
            d_key = d_key + rows_dot(d_scores, (rotary * both).astype(bf16)) * factor
        cos, sin = cos_ref[part, :], sin_ref[part, :]
        front, back = d_rotary[:, :ROPE_LANES], d_rotary[:, ROPE_LANES:]
        d_q_ref[part, nope : nope + ROPE_LANES] = (front * cos + back * sin).astype(bf16)
        d_q_ref[part, nope + ROPE_LANES :] = (back * cos - front * sin).astype(bf16)
        front, back = d_key[:, :ROPE_LANES], d_key[:, ROPE_LANES:]
        d_key_ref[part, :ROPE_LANES] = front * cos + back * sin
        d_key_ref[part, ROPE_LANES:] = back * cos - front * sin
    d_kv_normed = lanes_dot(d_kv_ref[...], up_ref[...])
    latent = joint_ref[:, :KVR]
    scale = lax.rsqrt(jnp.mean(latent * latent, axis=-1, keepdims=True) + norm_eps)
    d_gain_ref[0] = jnp.sum(d_kv_normed * latent * scale, axis=0, keepdims=True)
    d_kv_normed = d_kv_normed * kv_gain_ref[...]
    fall = jnp.mean(d_kv_normed * latent, axis=-1, keepdims=True) * scale * scale * scale
    d_joint_ref[:, :KVR] = (d_kv_normed * scale - latent * fall).astype(bf16)
    d_joint_ref[:, KVR:] = d_key_ref[...].astype(bf16)
    sum_ref[...] = (
        lanes_dot(d_q_ref[...], q_ref[:, : nope + 2 * ROPE_LANES])
        + lanes_dot(d_joint_ref[...], down_ref[...])
    ).astype(sum_ref.dtype)


def by_rows_call(kernel, rows, chunk, streamed, fixed_, outs, scratch=(), order=None):
    steps = rows // chunk
    operands, specs = [], []
    for name in order:
        if name in streamed:
            value = streamed[name]
            block = (value.shape[0] // steps,) + value.shape[1:]
            index = lambda i, ndim=value.ndim: (i,) + (0,) * (ndim - 1)
        else:
            value = fixed_[name]
            block = value.shape
            index = lambda i, ndim=value.ndim: (0,) * ndim
        operands.append(value)
        specs.append(pl.BlockSpec(block, index))
    out_specs = [
        pl.BlockSpec((shape[0] // steps,) + shape[1:], lambda i, ndim=len(shape): (i,) + (0,) * (ndim - 1))
        for shape, dtype in outs
    ]
    return pl.pallas_call(
        kernel,
        grid=(steps,),
        in_specs=specs,
        out_specs=out_specs,
        out_shape=[jax.ShapeDtypeStruct(shape, dtype) for shape, dtype in outs],
        scratch_shapes=scratch,
        compiler_params=pltpu.CompilerParams(vmem_limit_bytes=56 * 2**20),
    )(*operands)


def shards(
    tokens,
    attn_gain,
    kv_gain,
    ffn_gain,
    q_weight,
    kv_down_weight,
    kv_up_weight,
    out_weight,
    shared_gate_up,
    shared_down,
    expert_gate_up,
    expert_down,
    routes,
    gates,
    lengths,
    out_grad,
):
    row_count, width = tokens.shape
    dp_count = lax.axis_size("dp")
    expert_count = lax.axis_size("expert")
    core = lax.axis_index("dp")
    me = lax.axis_index("expert")
    scale_factor = (DH + DR) ** (-0.5)
    slice_rows = kv_down_weight.shape[0]
    joint_width = KVR + DR
    n_gain, n_kv_gain = attn_gain.shape[0], kv_gain.shape[0]

    bits = bits_of(expert_count)
    head_step = expert_count * dp_count // H
    pair_bit = max(4, head_step)
    rest = [bit for bit in bits if bit != pair_bit]
    head_low = pair_bit // head_step
    head_high = H // (dp_count * 2 * head_low)
    heads = head_high * head_low
    blocks = 2 * dp_count
    pair_rows = blocks * row_count

    far, second, first = rest
    orders = whole_orders(bits, pair_bit)
    parts = thirds(width)

    def column_parts(values):
        return [values[..., low:high] for low, high in parts]

    combined = jnp.sum(
        jnp.where(
            routes[:, :, None] == jnp.arange(expert_count, dtype=jnp.int32),
            gates[:, :, None],
            0.0,
        ),
        axis=1,
    ).T
    gates_high = lax.reduce_precision(combined, 8, 7)
    gates_low = (combined - gates_high).astype(bf16)
    gates_both = jnp.stack([gates_high.astype(bf16), gates_low], axis=1)
    gate_cols = 4 * row_count
    gates_both = gates_both.reshape(-1, gate_cols)
    gate_rows = gates_both.shape[0]
    gates_both = jnp.pad(gates_both, ((0, 0), (0, joint_width - gate_cols)))
    gains = jnp.concatenate([attn_gain, ffn_gain, kv_gain, lengths[0].astype(bf16)])
    gains = jnp.pad(gains, (0, joint_width - gains.shape[0]))[None]
    gain_row = slice_rows + gate_rows
    spare = -(gain_row + 1) % 16
    small = jnp.concatenate(
        [kv_down_weight, gates_both, jnp.pad(gains, ((0, spare), (0, 0)))], axis=0
    )

    def turned(values):
        split = values.reshape(values.shape[0], dp_count, expert_count, slice_rows)
        return split.transpose(0, 2, 1, 3).reshape(values.shape)

    def turned_back(values):
        split = values.reshape(values.shape[0], expert_count, dp_count, slice_rows)
        return split.transpose(0, 2, 1, 3).reshape(values.shape)

    q_cols = heads * (DH + DR)
    up_cols = heads * (DH + DV) * n_kv_gain // slice_rows
    head_cols = q_cols + up_cols
    head_rows = dp_count * slice_rows

    def by_pair(weight, head_width, *cuts):
        split = weight.reshape(-1, dp_count, head_high, 2, head_low, head_width)
        split = split.transpose(1, 3, 0, 2, 4, 5)
        lead = (dp_count, 2, slice_rows, -1)
        return [part.reshape(lead) for part in jnp.split(split, cuts, axis=-1)]

    by_head = dp_swap(
        jnp.concatenate(
            by_pair(q_weight, DH + DR, DH, DH + DR // 2) + by_pair(kv_up_weight, DH + DV), axis=-1
        )
    )
    nope_cols = heads * DH
    rope_cols = heads * DR // 2

    def spread(columns):
        if rope_cols == ROPE_LANES:
            return columns
        parts = jnp.split(columns[:, :q_cols], (nope_cols, nope_cols + rope_cols), axis=-1)
        room = ((0, 0), (0, ROPE_LANES - rope_cols))
        return jnp.concatenate([parts[0], jnp.pad(parts[1], room), jnp.pad(parts[2], room)], axis=-1)

    def unspread(columns):
        if rope_cols == ROPE_LANES:
            return columns
        parts = jnp.split(columns, (nope_cols, nope_cols + ROPE_LANES), axis=-1)
        return jnp.concatenate([parts[0], parts[1][:, :rope_cols], parts[2][:, :rope_cols]], axis=-1)

    out_cut = out_weight.reshape(slice_rows, -1, 2, head_cols).transpose(2, 1, 0, 3)
    out_cut = out_cut.reshape(2, -1, head_cols)
    head_cut = head_rows * 3 // 8
    out_mid = out_cut.shape[1] // 2

    share = shared_down.shape[0]
    units = dp_count * share
    padded = -(-units // 128) * 128

    def shared_by_unit(results, found, weight):
        split = weight.reshape(slice_rows, 2, dp_count, expert_count, share)
        split = split.transpose(3, 0, 1, 2, 4).reshape(expert_count, slice_rows, 2, units)
        split = jnp.pad(split, ((0, 0), (0, 0), (0, 0), (0, padded - units)))
        return split.reshape(expert_count, slice_rows, 2 * padded)

    pair_w = lax.all_gather(expert_gate_up[0].reshape(width // dp_count, -1), "dp", tiled=True)
    down_w = lax.all_gather(expert_down[0], "dp", tiled=True)
    def shared_weights(split, shared_down):
        split = lax.all_to_all(split, "expert", split_axis=0, concat_axis=0, tiled=True)
        down = dp_gather(shared_down).reshape(units, width)
        down = jnp.pad(down, ((0, padded - units), (0, 0)))
        return dp_gather(split).reshape(width, 2 * padded), down

    def attend(all_rows, small_all, by_head, out_parts):
        joint_all = dp_gather(small_all[:, :slice_rows])
        kv_down = joint_all.transpose(1, 0, 2, 3).reshape(width, joint_width)
        front, back = kv_down[:, KVR : KVR + DR // 2], kv_down[:, KVR + DR // 2 :]
        copies = 2 * ROPE_LANES // DR
        kv_down = jnp.concatenate([kv_down[:, :KVR]] + [front] * copies + [back] * copies, axis=-1)
        gains_all = dp_gather(small_all[:, gain_row])
        attn_scale = gains_all[..., :n_gain].transpose(1, 0, 2).reshape(-1)
        ffn_scale = gains_all[..., n_gain : 2 * n_gain].reshape(-1)
        n_gains = 2 * n_gain + n_kv_gain
        kv_scale = gains_all[..., 2 * n_gain : n_gains].reshape(-1)
        all_lengths = gains_all[..., n_gains : n_gains + lengths.shape[1]].astype(jnp.int32)
        low = me & ~pair_bit
        all_lengths = jnp.stack([pick(all_lengths, low, 1), pick(all_lengths, low | pair_bit, 1)])
        all_lengths = all_lengths.reshape(blocks, -1)
        doc_ids, offsets = jax.vmap(lambda row: layout(row, row_count))(all_lengths)
        cos, sin = [
            jnp.tile(table.reshape(pair_rows, DR // 2), (1, copies))
            for table in angles(offsets, DR)
        ]
        all_rows = dp_gather(all_rows).transpose(1, 0, 2, 3).reshape(pair_rows, width)
        by_head = jnp.concatenate(by_head, axis=1)
        q_full = spread(by_head.reshape(width, head_cols))
        kv_up = by_head[..., q_cols:].reshape(expert_count, dp_count, n_kv_gain, -1)
        kv_up = kv_up.transpose(1, 0, 2, 3).reshape(KVR, heads * (DH + DV))
        out_full = jnp.concatenate(out_parts, axis=1)
        at = bits.index(pair_bit)
        out_full = out_full.reshape((2,) * len(bits) + (-1, slice_rows, head_cols))
        out_full = jnp.moveaxis(out_full, (len(bits), at), (-3, -2)).reshape(heads * DV, width)
        wide = nope_cols + 2 * ROPE_LANES
        outs = by_rows_call(
            functools.partial(attend_kernel, heads),
            pair_rows,
            4 * row_count,
            dict(
                x=all_rows,
                cos=cos,
                sin=sin,
                column=doc_ids.reshape(pair_rows, 1),
                row=doc_ids.reshape(blocks, 1, row_count),
            ),
            dict(
                gain=attn_scale.astype(f32)[None],
                kv_gain=kv_scale.astype(f32)[None],
                down=kv_down,
                q=q_full,
                up=kv_up,
                out=out_full,
            ),
            (
                ((pair_rows, width), bf16),
                ((pair_rows, KVR + 2 * ROPE_LANES), f32),
                ((pair_rows, KVR), bf16),
                ((pair_rows, wide), bf16),
                ((pair_rows, wide), bf16),
                ((pair_rows, heads * DV), bf16),
                ((blocks * heads, row_count, row_count), f32),
                ((pair_rows, heads * DV), bf16),
                ((pair_rows, width), bf16),
            ),
            order=("x", "gain", "kv_gain", "down", "q", "up", "out", "cos", "sin", "column", "row"),
        )
        return outs, (q_full, kv_up, out_full, kv_down), (attn_scale, kv_scale, ffn_scale), (cos, sin)

    def cut_out(found):
        at = bits.index(pair_bit)
        found = found.reshape((2,) * len(rest) + (slice_rows, -1, 2, head_cols))
        found = jnp.moveaxis(found, (-3, -2), (len(bits), at))
        return found.reshape(expert_count, -1, head_cols)

    def by_owner(found):
        found = found.reshape(2, dp_count, row_count, -1).transpose(1, 0, 2, 3)
        return dp_scatter(found, bf16).astype(bf16)

    (all_rows, by_head), (shared_split,) = march(
        gathering(turned(tokens), [pair_bit]),
        pair_swapping(by_head, pair_bit, 1),
        jobs=((shared_by_unit, shared_gate_up),),
    )
    by_head = by_head.reshape(2, head_rows, head_cols)
    held_grad = []
    results, found = march(
        *(
            gathering(part, order, [pair_bit])
            for part, order in (
                (by_head[:, :head_cut], (second, far, first)),
                (by_head[:, head_cut:], (far, first, second)),
                (out_cut[:, :out_mid], (second, first, far)),
                (out_cut[:, out_mid:], (far, second, first)),
            )
        ),
        gathering(small, (far, first, second, pair_bit)),
        jobs=((skip,), (skip,), (lambda results, found, part: held_grad.append(part), out_grad)),
    )

    grad_all = lax.all_gather(held_grad[0], "expert")
    outs, weights, scales, tables = attend(all_rows, results[4], results[:2], results[2:4])
    normed, joint, kv_normed, query_parts, key_parts, values, probs, attended, attended_sum = outs
    q_full, kv_up, out_full, kv_down = weights
    attn_scale, kv_scale, ffn_scale = scales
    attended_sum = by_owner(attended_sum)
    shared_w, shared_out = shared_weights(shared_split, shared_down)
    hidden = down_w.shape[0]
    gates_all = results[4][:, slice_rows:gain_row, :gate_cols]
    gates_all = gates_all.reshape(expert_count, expert_count, 2, row_count)
    own_gate = pick(gates_all, me, 1).astype(f32).sum(axis=1)

    capacity = min(row_count, 3 * row_count * TOP // (2 * expert_count))
    slots = expert_count * capacity
    group_rows = expert_count * row_count
    grad_rows = grad_all.reshape(group_rows, width)

    def choose(results, found, own_gate, grad_all):
        live = own_gate > 0.0
        place = jnp.cumsum(live.astype(jnp.int32), axis=1) - 1
        chosen = jnp.arange(capacity, dtype=jnp.int32)[None, :, None] == place[:, None, :]
        chosen = chosen & live[:, None, :]
        slot_gate = jnp.sum(jnp.where(chosen, own_gate[:, None, :], 0.0), axis=2)
        slot_gate = slot_gate.reshape(slots, 1)
        chosen = chosen.astype(bf16)
        slot_grad = jnp.einsum("rst,rtd->rsd", chosen, grad_all, preferred_element_type=f32)
        return chosen, slot_gate, (slot_grad.reshape(slots, width) * slot_gate).astype(bf16)

    (attended_sum,), ((chosen, slot_gate, slot_grad),) = march(
        scattering(attended_sum, [pair_bit], [pair_bit]), jobs=((choose, own_gate, grad_all),)
    )
    resid_in = tokens.astype(f32)
    upstream = out_grad.astype(f32)
    resid = resid_in + attended_sum
    ffn_in = norm_apply(resid, ffn_scale).astype(bf16)

    def back_hidden(results, found, slot_grad, matrix):
        return dot(slot_grad, matrix.T)

    ffn_parts, (d_hidden, d_shared_hidden, *unused) = march(
        *(gathering(part, order) for part, order in zip(column_parts(ffn_in), orders)),
        jobs=((back_hidden, slot_grad, down_w), (back_hidden, grad_rows, shared_out)),
    )
    ffn_all = jnp.concatenate(ffn_parts, axis=-1)
    ffn_rows = ffn_all.reshape(group_rows, width)
    rows = jnp.einsum("rst,rtd->rsd", chosen, ffn_all, preferred_element_type=f32)
    rows = rows.reshape(slots, width).astype(bf16)
    pair = dot(rows, pair_w)
    gate_part, up_part = pair[:, :hidden], pair[:, hidden:]
    expert_hidden = swish_gate(gate_part, up_part).astype(bf16)
    d_pair = swish_back(gate_part, up_part, d_hidden).astype(bf16)
    shared_pair = dot(ffn_rows, shared_w)
    shared_gate, shared_up = shared_pair[:, :padded], shared_pair[:, padded:]
    shared_hidden = swish_gate(shared_gate, shared_up).astype(bf16)
    d_shared_pair = swish_back(shared_gate, shared_up, d_shared_hidden).astype(bf16)

    def to_tokens(slot_rows, shared_rows, shared_matrix):
        back = jnp.einsum(
            "rst,rsd->rtd",
            chosen,
            slot_rows.reshape(expert_count, capacity, -1),
            preferred_element_type=f32,
        )
        back = back.reshape(group_rows, -1) + dot(shared_rows, shared_matrix)
        return back.astype(bf16).reshape(expert_count, row_count, -1)

    d_rows = dot(d_pair, pair_w.T).astype(bf16)
    d_parts = [
        to_tokens(d_rows[:, low:high], d_shared_pair, shared_w[low:high].T) for low, high in parts
    ]

    kept_rows = (expert_hidden, d_pair, rows, shared_hidden, d_shared_pair, slot_grad)
    (expert_hidden, d_pair, rows, shared_hidden, d_shared_pair, slot_grad) = after(
        kept_rows, d_parts
    )

    def output_part(results, found, expert_hidden, shared_hidden):
        down = (dot(expert_hidden, down_w) * slot_gate).astype(bf16)
        return to_tokens(down, shared_hidden, shared_out)

    def halves(found):
        if dp_count != 2:
            return lax.psum_scatter(found.astype(bf16), "dp", scatter_dimension=0), ()
        return pick(found, core, 0), pick(found, 1 - core, 0).astype(bf16)

    def exchanged(kept, sent):
        if dp_count != 2:
            return kept.astype(f32)
        return kept + lax.ppermute(sent, "dp", [(0, 1), (1, 0)]).astype(f32)

    def pair_gradient(place, rows, d_pair):
        rows = pick(rows.reshape(slots, dp_count, -1), place, 1)
        return dot(rows.T, d_pair)

    def pair_kept(results, found, rows, d_pair):
        if dp_count != 2:
            found = dot(rows.T, d_pair).astype(bf16).reshape(dp_count, width // dp_count, -1)
            return lax.psum_scatter(found, "dp", scatter_dimension=0)
        return pair_gradient(core, rows, d_pair)

    def pair_sent(results, found, rows, d_pair):
        if dp_count != 2:
            return ()
        return pair_gradient(1 - core, rows, d_pair).astype(bf16)

    def down_gradient(results, found, expert_hidden, slot_grad):
        return halves(
            dot(expert_hidden.T, slot_grad).reshape(dp_count, hidden // dp_count, width)
        )

    def shared_gradient(results, found, shared_hidden, d_shared_pair):
        down = dot(shared_hidden.T, grad_rows)[:units].reshape(dp_count, share, width)
        both = dot(ffn_rows.T, d_shared_pair)
        both = both.reshape(dp_count, expert_count, slice_rows, 2 * padded)
        return dp_scatter(down, bf16), dp_scatter(both, bf16).astype(bf16)

    d_sums, found = march(
        *(scattering(part, order[::-1], bits) for part, order in zip(d_parts, orders)),
        jobs=(
            (pair_sent, rows, d_pair),
            (down_gradient, expert_hidden, slot_grad),
            (shared_gradient, shared_hidden, d_shared_pair),
            (output_part, expert_hidden, shared_hidden),
        ),
    )
    sent, down_halves, (grad_shared_out, grad_shared), out_part = found
    rows, d_pair = after((rows, d_pair), d_sums)
    d_ffn_in = jnp.concatenate(d_sums, axis=-1)

    d_norm_resid, grad_ffn_scale = norm_back(resid, ffn_scale, d_ffn_in)
    d_resid = upstream + d_norm_resid
    (d_branch,), (kept,) = march(
        gathering(d_resid.astype(bf16), [pair_bit]), jobs=((pair_kept, rows, d_pair),)
    )
    pair_halves = (kept, sent)

    def attend_back(results, found, d_branch):
        d_branch = dp_gather(d_branch).transpose(1, 0, 2, 3).reshape(pair_rows, width)
        steps = pair_rows // (4 * row_count)
        wide = nope_cols + 2 * ROPE_LANES
        outs = by_rows_call(
            functools.partial(attend_back_kernel, heads),
            pair_rows,
            4 * row_count,
            dict(
                branch=d_branch,
                probs=probs,
                heads=query_parts,
                keys=key_parts,
                values=values,
                joint=joint,
                cos=tables[0],
                sin=tables[1],
            ),
            dict(
                out=out_full,
                kv_gain=kv_scale.astype(f32)[None],
                up=kv_up,
                q=q_full,
                down=kv_down,
            ),
            (
                ((pair_rows, wide), bf16),
                ((pair_rows, heads * (DH + DV)), bf16),
                ((pair_rows, KVR + 2 * ROPE_LANES), bf16),
                ((steps, 1, KVR), f32),
                ((pair_rows, width), bf16),
            ),
            scratch=[pltpu.VMEM((4 * row_count, 2 * ROPE_LANES), f32)],
            order=(
                "branch", "out", "probs", "heads", "keys", "values", "joint", "kv_gain", "up", "q",
                "down", "cos", "sin",
            ),
        )
        return d_branch, outs

    def back_sum(results, found):
        return by_owner(found[0][1][4])

    def weight_gradients(results, found):
        d_branch, (d_q_heads, d_kv_heads, d_joint, unused, unused) = found[0]
        grad_q = unspread(dot(normed.T, d_q_heads)).astype(bf16)
        grad_q = grad_q.reshape(expert_count, head_rows, q_cols)
        grad_up = dot(kv_normed.T, d_kv_heads).astype(bf16)
        grad_up = grad_up.reshape(dp_count, expert_count, n_kv_gain, -1).transpose(1, 0, 2, 3)
        grad_up = grad_up.reshape(expert_count, head_rows, up_cols)
        by_head = jnp.concatenate([grad_q, grad_up], axis=-1)
        grad_out = cut_out(dot(attended.T, d_branch).astype(bf16))
        grad_kvdown = dot(normed.T, d_joint)
        rotary = grad_kvdown[:, KVR:].reshape(width, 2, -1, DR // 2).sum(axis=2)
        grad_kvdown = jnp.concatenate([grad_kvdown[:, :KVR], rotary.reshape(width, DR)], axis=-1)
        grad_kvdown = grad_kvdown.reshape(expert_count, dp_count, slice_rows, joint_width)
        return by_head, grad_out, dp_scatter(grad_kvdown.transpose(1, 0, 2, 3), bf16)

    results, found = march(
        *(
            scattering(part, order[::-1], bits)
            for part, order in zip(column_parts(out_part), orders)
        ),
        jobs=((attend_back, d_branch), (back_sum,), (weight_gradients,)),
    )
    output = (resid + jnp.concatenate(results, axis=-1)).astype(bf16)
    grad_heads, grad_out, grad_kvdown = found[2]
    d_normed = found[1]
    grad_kv_scale = found[0][1][3].sum(axis=0)
    d_normed = alone(scattering(d_normed, [pair_bit], [pair_bit]))
    pair_halves, down_halves, grad_shared = after((pair_halves, down_halves, grad_shared), results)
    d_norm_in, grad_attn_scale = norm_back(turned(resid_in), attn_scale, d_normed)
    grad_in = (d_resid + turned_back(d_norm_in)).astype(bf16)
    scale_sums = jnp.concatenate(
        [
            grad_attn_scale.reshape(expert_count, dp_count, n_gain).transpose(1, 0, 2),
            grad_ffn_scale.reshape(dp_count, expert_count, n_gain),
            grad_kv_scale.reshape(dp_count, expert_count, n_kv_gain),
        ],
        axis=-1,
    )
    scale_sums = jnp.pad(scale_sums, ((0, 0), (0, 0), (0, joint_width - scale_sums.shape[-1])))
    scale_sums = dp_scatter(scale_sums)[:, None]
    small_sums = jnp.concatenate([grad_kvdown, scale_sums], axis=1).astype(bf16)

    def finish_pair(results, found, kept, sent):
        return exchanged(kept, sent).reshape(expert_gate_up.shape)

    def finish_down(results, found, kept, sent, shared):
        shared = lax.all_to_all(shared, "expert", split_axis=0, concat_axis=0, tiled=True)
        return exchanged(kept, sent).reshape(expert_down.shape), shared

    def finish_shared(results, found):
        both = found[1][1].reshape(expert_count, slice_rows, 2, padded)[..., :units]
        both = both.reshape(expert_count, slice_rows, 2, dp_count, share)
        return both.transpose(1, 2, 3, 0, 4).reshape(shared_gate_up.shape).astype(f32)

    def whole_heads(found, rows, *widths):
        cuts = [heads * sum(widths[: i + 1]) for i in range(len(widths) - 1)]
        lead = (dp_count, 2, rows, head_high, head_low, -1)
        found = jnp.concatenate(
            [part.reshape(lead) for part in jnp.split(found, cuts, axis=-1)], axis=-1
        )
        return found.transpose(2, 0, 3, 1, 4, 5).reshape(rows, -1).astype(f32)

    summed, found = march(
        scattering(small_sums, (pair_bit, second, first, far), bits),
        *(
            scattering(part, order, bits, bf16)
            for part, order in (
                (grad_heads[:, :head_cut], (first, far, second)),
                (grad_heads[:, head_cut:], (second, first, far)),
                (grad_out[:, :out_mid], (far, first, second)),
                (grad_out[:, out_mid:], (first, second, far)),
            )
        ),
        jobs=(
            (finish_pair, *pair_halves),
            (finish_down, *down_halves, grad_shared),
            (finish_shared,),
        ),
    )
    grad_pair, (grad_down, unused), grad_shared = found[:3]
    by_head = jnp.concatenate(summed[1:3], axis=1)
    by_head = alone(pair_swapping(by_head, pair_bit, 0)).reshape(2, dp_count, slice_rows, head_cols)
    by_head = dp_swap(by_head.transpose(1, 0, 2, 3))
    grad_q = whole_heads(by_head[..., :q_cols], slice_rows, DH, DR // 2, DR // 2)
    grad_up = by_head[..., q_cols:].reshape(dp_count, 2, n_kv_gain, -1)
    grad_up = whole_heads(grad_up, n_kv_gain, DH + DV)
    grad_out = jnp.concatenate(summed[3:5], axis=1).reshape(2, -1, slice_rows, head_cols)
    grad_out = grad_out.transpose(2, 1, 0, 3).reshape(out_weight.shape).astype(f32)
    small_sums = summed[0]
    grad_kvdown = small_sums[:slice_rows]
    scale_sums = small_sums[slice_rows]

    return (
        output,
        grad_in,
        scale_sums[:n_gain],
        scale_sums[2 * n_gain : 2 * n_gain + n_kv_gain],
        scale_sums[n_gain : 2 * n_gain],
        grad_q,
        grad_kvdown,
        grad_up,
        grad_out,
        grad_shared,
        grad_shared_out,
        grad_pair,
        grad_down,
    )


def solution(mesh):
    rows = P(SPLIT, None)
    each = P(SPLIT)
    cube = P(SPLIT, None, None)
    pair = P("expert", "dp", None, None)
    down = P("expert", "dp", None)
    dense = (rows, rows, rows, rows, cube, rows)
    return jax.shard_map(
        shards,
        mesh=mesh,
        in_specs=(rows, each, each, each) + dense + (pair, down, rows, rows, rows, rows),
        out_specs=(rows, rows, each, each, each) + dense + (pair, down),
        check_vma=False,
    )
```

```python
import functools

import jax
import jax.numpy as jnp
from jax import lax
from jax.experimental import pallas as pl
from jax.experimental.pallas import tpu as pltpu
from jax.sharding import PartitionSpec as P

H = 16
DH = 128
DR = 64
DV = 128
KVR = 512
TOP = 6
SPLIT = ("dp", "expert")
ROPE_LANES = 128

f32 = jnp.float32
bf16 = jnp.bfloat16

norm_eps = 1e-06
rope_base = 50000.0
masked_score = -1e30


def norm_apply(values, scales):
    return values * lax.rsqrt(jnp.mean(values * values, axis=-1, keepdims=True) + norm_eps) * scales


def norm_back(values, scales, upstream):
    unused, pullback = jax.vjp(norm_apply, values, scales.astype(f32))
    return pullback(upstream)


def rotate(values, cosine_table, sine_table):
    half_width = values.shape[-1] // 2
    front_half = values[..., :half_width]
    back_half = values[..., half_width:]
    return jnp.concatenate(
        [
            front_half * cosine_table - back_half * sine_table,
            front_half * sine_table + back_half * cosine_table,
        ],
        axis=-1,
    )


def swish_gate(gate_part, up_part):
    return gate_part * jax.nn.sigmoid(gate_part) * up_part


def swish_back(gate_part, up_part, upstream):
    unused, pullback = jax.vjp(swish_gate, gate_part, up_part)
    return jnp.concatenate(pullback(upstream), axis=-1)


def layout(lengths_row, row_count):
    doc_ends = jnp.cumsum(lengths_row)
    places = jnp.arange(row_count, dtype=jnp.int32)
    passed_end = (places[:, None] >= doc_ends[None, :]).astype(jnp.int32)
    doc_ids = jnp.sum(passed_end, axis=1)
    starts = jnp.sum(passed_end * lengths_row[None, :], axis=1)
    return (doc_ids, places - starts)


def angles(offsets, rope_width):
    frequency = rope_base ** (-2.0 * jnp.arange(rope_width // 2, dtype=f32) / rope_width)
    turned = offsets.astype(f32)[..., None] * frequency
    return (jnp.cos(turned), jnp.sin(turned))


def dot(left, right):
    return jnp.dot(left, right, preferred_element_type=f32)


def pick(values, place, axis):
    return lax.dynamic_index_in_dim(values, place, axis, keepdims=False)


def dp_gather(values):
    if lax.axis_size("dp") != 2:
        return lax.all_gather(values, "dp")
    other = lax.ppermute(values, "dp", [(0, 1), (1, 0)])
    first = lax.axis_index("dp") == 0
    return jnp.stack([jnp.where(first, values, other), jnp.where(first, other, values)])


def dp_swap(values):
    if lax.axis_size("dp") != 2:
        return lax.all_to_all(values, "dp", split_axis=0, concat_axis=0)
    core = lax.axis_index("dp")
    own = pick(values, core, 0)
    other = lax.ppermute(pick(values, 1 - core, 0), "dp", [(0, 1), (1, 0)])
    first = core == 0
    return jnp.stack([jnp.where(first, own, other), jnp.where(first, other, own)])


def dp_scatter(values, sent=f32):
    if lax.axis_size("dp") != 2:
        return lax.psum_scatter(values.astype(sent), "dp", scatter_dimension=0).astype(f32)
    core = lax.axis_index("dp")
    other = lax.ppermute(pick(values, 1 - core, 0).astype(sent), "dp", [(0, 1), (1, 0)])
    return pick(values, core, 0).astype(f32) + other.astype(f32)


def dp_sum(values):
    if lax.axis_size("dp") != 2:
        return lax.psum(values, "dp")
    return values + lax.ppermute(values, "dp", [(0, 1), (1, 0)])


def bits_of(count):
    return [1 << place for place in reversed(range(count.bit_length() - 1))]


def partner(values, bit):
    count = lax.axis_size("expert")
    return lax.ppermute(values, "expert", [(i, i ^ bit) for i in range(count)])


def gathering(values, order, held=(), lead=0, whole=True):
    me = lax.axis_index("expert")
    held = list(held)
    for step, bit in enumerate(order):
        if not whole and step + 1 == len(order):
            values = values.reshape(-1, values.shape[-1])
            return values, (yield partner(values, bit))
        other = yield partner(values, bit)
        low = (me & bit) == 0
        values = jnp.stack(
            [jnp.where(low, values, other), jnp.where(low, other, values)],
            axis=lead + sum(1 for known in held if known > bit),
        )
        held.append(bit)
    return values.reshape(values.shape[:lead] + (-1,) + values.shape[lead + len(held) :])


def scattering(values, order, bits, kept=f32, lead=0):
    me = lax.axis_index("expert")
    bits = list(bits)
    split = isinstance(values, tuple)
    if not split:
        values = values.reshape(values.shape[:lead] + (2,) * len(bits) + values.shape[lead + 1 :])
    for step, bit in enumerate(order):
        axis = lead + bits.index(bit)
        bits.remove(bit)
        place = ((me & bit) != 0).astype(jnp.int32)
        if split and step == 0:
            own, sent = values
        else:
            own, sent = pick(values, place, axis), pick(values, 1 - place, axis)
        other = yield partner(sent, bit)
        if step + 1 < len(order):
            values = own + other
        else:
            values = (own.astype(f32) + other.astype(f32)).astype(kept)
        if split and step == 0:
            values = values.reshape((2,) * len(bits) + (-1,) + values.shape[-1:])
    if bits:
        values = values.reshape(values.shape[:lead] + (-1,) + values.shape[lead + len(bits) :])
    return values


def later(steps, values, chain):
    for _ in range(steps):
        values = yield values
    return (yield from chain(values))


def begun(chain, values):
    while True:
        try:
            values = chain.send(values)
        except StopIteration as stop:
            return stop.value
        values = yield values


def last_of(chain, values):
    try:
        chain.send(values)
    except StopIteration as stop:
        return stop.value


def deferred(steps, make):
    for _ in range(steps):
        yield ()
    return (yield from make())


def pair_swapping(values, bit, axis):
    place = ((lax.axis_index("expert") & bit) != 0).astype(jnp.int32)
    own = pick(values, place, axis)
    other = yield partner(pick(values, 1 - place, axis), bit)
    low = place == 0
    return jnp.stack([jnp.where(low, own, other), jnp.where(low, other, own)])


def march(*chains, jobs=()):
    results, found = [None] * len(chains), []
    live = {i: next(chain) for i, chain in enumerate(chains)}
    waiting = [operands for _, *operands in jobs]
    while live or len(found) < len(jobs):
        step = len(found)
        job = jobs[step][0](results, found, *waiting[step]) if step < len(jobs) else ()
        live, job, waiting = lax.optimization_barrier((live, job, waiting[step + 1 :]))
        waiting = [()] * (step + 1) + waiting
        found.append(job)
        following = {}
        for i, values in live.items():
            try:
                following[i] = chains[i].send(values)
            except StopIteration as stop:
                results[i] = stop.value
        live = following
    return results, found


def skip(results, found):
    return ()


def alone(chain, *markers):
    values = next(chain)
    step = 0
    while True:
        if step < len(markers):
            values = after(values, markers[step])
        step += 1
        try:
            values = chain.send(values)
        except StopIteration as stop:
            return stop.value


def after(values, *others):
    return lax.optimization_barrier((values, others))[0]


def thirds(width):
    side = width // 128 // 3 * 128
    return (0, side), (side, width - side), (width - side, width)


def whole_orders(bits, pair_bit):
    far, second, first = [bit for bit in bits if bit != pair_bit]
    return (
        (second, far, first, pair_bit),
        (far, first, pair_bit, second),
        (far, pair_bit, second, first),
    )


def lanes_dot(left, right):
    return lax.dot_general(left, right, (((1,), (1,)), ((), ())), preferred_element_type=f32)


def rows_dot(left, right):
    return lax.dot_general(left, right, (((0,), (0,)), ((), ())), preferred_element_type=f32)


def head_lanes(heads):
    lane = lax.broadcasted_iota(jnp.int32, (1, ROPE_LANES), 1) // (DR // 2)
    return [(lane == head).astype(f32) for head in range(heads)]


def attend_kernel(
    heads,
    x_ref,
    gain_ref,
    kv_gain_ref,
    down_ref,
    q_ref,
    up_ref,
    out_ref,
    cos_ref,
    sin_ref,
    column_ref,
    row_ref,
    normed_ref,
    joint_ref,
    kv_normed_ref,
    heads_ref,
    keys_ref,
    values_ref,
    probs_ref,
    attended_ref,
    sum_ref,
):
    nope = heads * DH
    rows = x_ref.shape[0]
    x = x_ref[...].astype(f32)
    scale = lax.rsqrt(jnp.mean(x * x, axis=-1, keepdims=True) + norm_eps)
    normed_ref[...] = (x * scale * gain_ref[...]).astype(bf16)
    joint_ref[...] = dot(normed_ref[...], down_ref[...])
    latent = joint_ref[:, :KVR]
    scale = lax.rsqrt(jnp.mean(latent * latent, axis=-1, keepdims=True) + norm_eps)
    kv_normed_ref[...] = (latent * scale * kv_gain_ref[...]).astype(bf16)
    cos, sin = cos_ref[...], sin_ref[...]
    copies = 2 * ROPE_LANES // DR
    front = jnp.concatenate([joint_ref[:, KVR : KVR + DR // 2]] * copies, axis=-1)
    back = jnp.concatenate([joint_ref[:, KVR + DR // 2 :]] * copies, axis=-1)
    keys_ref[:, nope : nope + ROPE_LANES] = (front * cos - back * sin).astype(bf16)
    keys_ref[:, nope + ROPE_LANES :] = (front * sin + back * cos).astype(bf16)
    q = dot(normed_ref[...], q_ref[:, : nope + 2 * ROPE_LANES])
    front = q[:, nope : nope + ROPE_LANES]
    back = q[:, nope + ROPE_LANES :]
    heads_ref[:, :nope] = q[:, :nope].astype(bf16)
    heads_ref[:, nope : nope + ROPE_LANES] = (front * cos - back * sin).astype(bf16)
    heads_ref[:, nope + ROPE_LANES :] = (front * sin + back * cos).astype(bf16)
    kv = dot(kv_normed_ref[...], up_ref[...])
    for head in range(heads):
        start = head * (DH + DV)
        keys_ref[:, head * DH : (head + 1) * DH] = kv[:, start : start + DH].astype(bf16)
        values_ref[:, head * DV : (head + 1) * DV] = kv[:, start + DH : start + DH + DV].astype(bf16)
    tile = probs_ref.shape[-1]
    causal = lax.broadcasted_iota(jnp.int32, (tile, tile), 0) >= lax.broadcasted_iota(
        jnp.int32, (tile, tile), 1
    )
    own = head_lanes(heads)
    for block in range(rows // tile):
        part = pl.ds(block * tile, tile)
        allowed = (column_ref[part, :] == row_ref[block]) & causal
        rotary = heads_ref[part, nope:].astype(f32)
        for head in range(heads):
            both = jnp.concatenate([own[head], own[head]], axis=-1)
            scores = lanes_dot(
                heads_ref[part, head * DH : (head + 1) * DH],
                keys_ref[part, head * DH : (head + 1) * DH],
            ) + lanes_dot((rotary * both).astype(bf16), keys_ref[part, nope:])
            scores = jnp.where(allowed, scores * (DH + DR) ** (-0.5), masked_score)
            weights = jnp.exp(scores - jnp.max(scores, axis=-1, keepdims=True))
            probs = weights / jnp.sum(weights, axis=-1, keepdims=True)
            probs_ref[block * heads + head] = probs
            attended_ref[part, head * DV : (head + 1) * DV] = dot(
                probs.astype(bf16), values_ref[part, head * DV : (head + 1) * DV]
            ).astype(bf16)
    sum_ref[...] = dot(attended_ref[...], out_ref[...]).astype(sum_ref.dtype)


def attend_back_kernel(
    heads,
    branch_ref,
    out_ref,
    probs_ref,
    heads_ref,
    keys_ref,
    values_ref,
    joint_ref,
    kv_gain_ref,
    up_ref,
    q_ref,
    down_ref,
    cos_ref,
    sin_ref,
    d_q_ref,
    d_kv_ref,
    d_joint_ref,
    d_gain_ref,
    sum_ref,
    d_key_ref,
):
    nope = heads * DH
    rows = branch_ref.shape[0]
    tile = probs_ref.shape[-1]
    factor = (DH + DR) ** (-0.5)
    d_attended = lanes_dot(branch_ref[...], out_ref[...]).astype(bf16)
    own = head_lanes(heads)
    for block in range(rows // tile):
        part = slice(block * tile, (block + 1) * tile)
        rotary = heads_ref[part, nope:].astype(f32)
        d_rotary = jnp.zeros((tile, 2 * ROPE_LANES), f32)
        d_key = jnp.zeros((tile, 2 * ROPE_LANES), f32)
        for head in range(heads):
            both = jnp.concatenate([own[head], own[head]], axis=-1)
            columns = slice(head * DH, (head + 1) * DH)
            start = head * (DH + DV)
            upstream = d_attended[part, head * DV : (head + 1) * DV]
            probs = probs_ref[block * heads + head]
            d_kv_ref[part, start + DH : start + DH + DV] = rows_dot(
                probs.astype(bf16), upstream
            ).astype(bf16)
            d_probs = lanes_dot(upstream, values_ref[part, head * DV : (head + 1) * DV])
            d_scores = probs * (d_probs - jnp.sum(d_probs * probs, axis=-1, keepdims=True))
            d_scores = d_scores.astype(bf16)
            d_q_ref[part, columns] = (dot(d_scores, keys_ref[part, columns]) * factor).astype(bf16)
            d_rotary = d_rotary + dot(d_scores, keys_ref[part, nope:]) * (factor * both)
            d_kv_ref[part, start : start + DH] = (
                rows_dot(d_scores, heads_ref[part, columns]) * factor
            ).astype(bf16)
            d_key = d_key + rows_dot(d_scores, (rotary * both).astype(bf16)) * factor
        cos, sin = cos_ref[part, :], sin_ref[part, :]
        front, back = d_rotary[:, :ROPE_LANES], d_rotary[:, ROPE_LANES:]
        d_q_ref[part, nope : nope + ROPE_LANES] = (front * cos + back * sin).astype(bf16)
        d_q_ref[part, nope + ROPE_LANES :] = (back * cos - front * sin).astype(bf16)
        front, back = [
            sum(half[:, at : at + DR // 2] for at in range(0, ROPE_LANES, DR // 2))
            for half in (d_key[:, :ROPE_LANES], d_key[:, ROPE_LANES:])
        ]
        cos, sin = cos[:, : DR // 2], sin[:, : DR // 2]
        d_key_ref[part, : DR // 2] = front * cos + back * sin
        d_key_ref[part, DR // 2 :] = back * cos - front * sin
    d_kv_normed = lanes_dot(d_kv_ref[...], up_ref[...])
    latent = joint_ref[:, :KVR]
    scale = lax.rsqrt(jnp.mean(latent * latent, axis=-1, keepdims=True) + norm_eps)
    d_gain_ref[0] = jnp.sum(d_kv_normed * latent * scale, axis=0, keepdims=True)
    d_kv_normed = d_kv_normed * kv_gain_ref[...]
    fall = jnp.mean(d_kv_normed * latent, axis=-1, keepdims=True) * scale * scale * scale
    d_joint_ref[:, :KVR] = (d_kv_normed * scale - latent * fall).astype(bf16)
    d_joint_ref[:, KVR:] = d_key_ref[...].astype(bf16)
    sum_ref[...] = (
        lanes_dot(d_q_ref[...], q_ref[:, : nope + 2 * ROPE_LANES])
        + lanes_dot(d_joint_ref[...], down_ref[...])
    ).astype(sum_ref.dtype)


def by_rows_call(
    kernel, steps, order, streamed, fixed, outs, scratch=(), group=lambda i: i, scalars=(), half=None
):
    half = half or ()

    def spec(name, shape):
        rest = (0,) * (len(shape) - 1)
        if name in half:
            block = (shape[0] * 2 // steps,) + shape[1:]
            return pl.BlockSpec(block, lambda i, *unused: (i // 2,) + rest)
        block = (shape[0] // steps,) + shape[1:]
        return pl.BlockSpec(block, lambda i, *unused: (group(i),) + rest)

    operands, specs = [], []
    for name in order:
        if name in streamed:
            operands.append(streamed[name])
            specs.append(spec(name, streamed[name].shape))
        else:
            value = fixed[name]
            operands.append(value)
            specs.append(
                pl.BlockSpec(
                    value.shape,
                    lambda i, *unused, ndim=value.ndim: (0,) * ndim,
                    pipeline_mode=pl.Buffered(1),
                )
            )
    return pl.pallas_call(
        kernel,
        grid_spec=pltpu.PrefetchScalarGridSpec(
            num_scalar_prefetch=len(scalars),
            grid=(steps,),
            in_specs=specs,
            out_specs=[spec(name, shape) for name, shape, dtype in outs],
            scratch_shapes=scratch,
        ),
        out_shape=[jax.ShapeDtypeStruct(shape, dtype) for name, shape, dtype in outs],
        compiler_params=pltpu.CompilerParams(vmem_limit_bytes=60 * 2**20),
    )(*scalars, *operands)


def one_hot(slot_ref, place, count):
    slots = slot_ref[place]
    return lax.broadcasted_iota(jnp.int32, (count, slots.shape[1]), 0) == slots


def swiglu_back(gate_part, up_part, upstream):
    sigmoid = jax.nn.sigmoid(gate_part)
    silu = gate_part * sigmoid
    slope = sigmoid + silu * (1.0 - sigmoid)
    return silu * up_part, upstream * up_part * slope, upstream * silu


def gradient_kernel(
    count, grad_ref, slot_ref, gate_ref, down_ref, shared_ref, picked_ref, d_hidden_ref, d_shared_ref
):
    span = slot_ref.shape[-1]
    for place in range(slot_ref.shape[0]):
        chosen = one_hot(slot_ref, place, count)
        gate = jnp.sum(jnp.where(chosen, gate_ref[place], 0.0), axis=1, keepdims=True)
        found = dot(chosen.astype(bf16), grad_ref[place * span : (place + 1) * span])
        picked_ref[place * count : (place + 1) * count] = (found * gate).astype(bf16)
    d_hidden_ref[...] = lanes_dot(picked_ref[...], down_ref[...])
    d_shared_ref[...] = lanes_dot(grad_ref[...], shared_ref[...])


def halves_in(me_ref, refs, x_ref, parts, span):
    for (start, stop), (held_ref, came_ref), mine in zip(parts, refs, my_places(me_ref)):
        if start == 0:
            here = lax.rem(pl.program_id(0), 2) == mine

            @pl.when(here)
            def _():
                x_ref[:, start:stop] = held_ref[...]

            @pl.when(jnp.logical_not(here))
            def _():
                x_ref[:, start:stop] = came_ref[...]

            continue
        size = span if start == parts[1][0] else span // 2
        for at in range(2 * span // size):
            turn, place = (at // 2, at % 2) if size < span else (0, at)
            source = slice(turn * size, (turn + 1) * size)
            x_ref[at * size : (at + 1) * size, start:stop] = jnp.where(
                mine == place, held_ref[source].astype(f32), came_ref[source].astype(f32)
            ).astype(bf16)


def halves_out(me_ref, refs, values, which, span):
    (kept_ref, sent_ref), mine = refs[which], my_places(me_ref)[which]
    if which == 0:
        here = lax.rem(pl.program_id(0), 2) == mine

        @pl.when(here)
        def _():
            kept_ref[...] = values.astype(bf16)

        @pl.when(jnp.logical_not(here))
        def _():
            sent_ref[...] = values.astype(bf16)

        return
    size = span if which == 1 else span // 2
    for turn in range(span // size):
        low = values[2 * turn * size : (2 * turn + 1) * size]
        high = values[(2 * turn + 1) * size : (2 * turn + 2) * size]
        target = slice(turn * size, (turn + 1) * size)
        kept_ref[target] = jnp.where(mine == 0, low, high).astype(bf16)
        sent_ref[target] = jnp.where(mine == 0, high, low).astype(bf16)


def my_places(me_ref):
    return me_ref[0], me_ref[1], me_ref[2]


def expert_kernel(
    count,
    me_ref,
    slot_ref,
    d_hidden_ref,
    d_shared_ref,
    pair_ref,
    shared_ref,
    left_ref,
    left_came_ref,
    middle_ref,
    middle_came_ref,
    right_ref,
    right_came_ref,
    x_ref,
    rows_ref,
    hidden_ref,
    d_pair_ref,
    shared_hidden_ref,
    d_shared_pair_ref,
    left_kept_ref,
    left_sent_ref,
    middle_kept_ref,
    middle_sent_ref,
    right_kept_ref,
    right_sent_ref,
):
    span = slot_ref.shape[-1]
    parts = thirds(x_ref.shape[-1])
    halves_in(
        me_ref,
        ((left_ref, left_came_ref), (middle_ref, middle_came_ref), (right_ref, right_came_ref)),
        x_ref,
        parts,
        span,
    )
    places = range(slot_ref.shape[0])
    chosen = [one_hot(slot_ref, place, count).astype(bf16) for place in places]
    for place in places:
        rows_ref[place * count : (place + 1) * count] = dot(
            chosen[place], x_ref[place * span : (place + 1) * span]
        ).astype(bf16)
    hidden = hidden_ref.shape[-1]
    units, d_gate, d_up = swiglu_back(
        dot(rows_ref[...], pair_ref[:, :hidden]),
        dot(rows_ref[...], pair_ref[:, hidden:]),
        d_hidden_ref[...],
    )
    hidden_ref[...] = units.astype(bf16)
    d_pair_ref[:, :hidden] = d_gate.astype(bf16)
    d_pair_ref[:, hidden:] = d_up.astype(bf16)
    padded = shared_hidden_ref.shape[-1]
    units, d_gate, d_up = swiglu_back(
        dot(x_ref[...], shared_ref[:, :padded]),
        dot(x_ref[...], shared_ref[:, padded:]),
        d_shared_ref[...],
    )
    shared_hidden_ref[...] = units.astype(bf16)
    d_shared_pair_ref[:, :padded] = d_gate.astype(bf16)
    d_shared_pair_ref[:, padded:] = d_up.astype(bf16)
    refs = (
        (left_kept_ref, left_sent_ref),
        (middle_kept_ref, middle_sent_ref),
        (right_kept_ref, right_sent_ref),
    )
    for which, (start, stop) in enumerate(parts):
        back = lanes_dot(d_pair_ref[...], pair_ref[start:stop]).astype(bf16)
        found = [
            rows_dot(chosen[place], back[place * count : (place + 1) * count])
            + lanes_dot(d_shared_pair_ref[place * span : (place + 1) * span], shared_ref[start:stop])
            for place in places
        ]
        halves_out(me_ref, refs, jnp.concatenate(found, axis=0), which, span)


def output_kernel(
    count,
    me_ref,
    hidden_ref,
    shared_hidden_ref,
    slot_ref,
    gate_ref,
    down_ref,
    shared_ref,
    left_kept_ref,
    left_sent_ref,
    middle_kept_ref,
    middle_sent_ref,
    right_kept_ref,
    right_sent_ref,
    rows_ref,
):
    span = slot_ref.shape[-1]
    places = range(slot_ref.shape[0])
    chosen = [one_hot(slot_ref, place, count) for place in places]
    found = dot(hidden_ref[...], down_ref[...])
    for place in places:
        at = slice(place * count, (place + 1) * count)
        gate = jnp.sum(jnp.where(chosen[place], gate_ref[place], 0.0), axis=1, keepdims=True)
        rows_ref[at] = (found[at] * gate).astype(bf16)
    refs = (
        (left_kept_ref, left_sent_ref),
        (middle_kept_ref, middle_sent_ref),
        (right_kept_ref, right_sent_ref),
    )
    for which, (start, stop) in enumerate(thirds(down_ref.shape[-1])):
        found = [
            rows_dot(
                chosen[place].astype(bf16),
                rows_ref[place * count : (place + 1) * count, start:stop],
            )
            + dot(shared_hidden_ref[place * span : (place + 1) * span], shared_ref[:, start:stop])
            for place in places
        ]
        halves_out(me_ref, refs, jnp.concatenate(found, axis=0), which, span)


def columns_kernel(place_ref, left_ref, right_ref, out_ref):
    out_ref[...] = rows_dot(left_ref[...], right_ref[...]).astype(out_ref.dtype)


def columns_product(left, right, place, parts, dtype):
    width = left.shape[1] // parts
    block = 256 if width % 256 == 0 else 128
    steps = width // block
    return pl.pallas_call(
        columns_kernel,
        grid_spec=pltpu.PrefetchScalarGridSpec(
            num_scalar_prefetch=1,
            grid=(steps,),
            in_specs=[
                pl.BlockSpec((left.shape[0], block), lambda i, place: (0, place[0] * steps + i)),
                pl.BlockSpec(right.shape, lambda i, place: (0, 0), pipeline_mode=pl.Buffered(1)),
            ],
            out_specs=pl.BlockSpec((block, right.shape[1]), lambda i, place: (i, 0)),
        ),
        out_shape=jax.ShapeDtypeStruct((width, right.shape[1]), dtype),
        compiler_params=pltpu.CompilerParams(vmem_limit_bytes=56 * 2**20),
    )(jnp.reshape(place, (1,)).astype(jnp.int32), left, right)


def shards(
    tokens,
    attn_gain,
    kv_gain,
    ffn_gain,
    q_weight,
    kv_down_weight,
    kv_up_weight,
    out_weight,
    shared_gate_up,
    shared_down,
    expert_gate_up,
    expert_down,
    routes,
    gates,
    lengths,
    out_grad,
):
    row_count, width = tokens.shape
    dp_count = lax.axis_size("dp")
    expert_count = lax.axis_size("expert")
    core = lax.axis_index("dp")
    me = lax.axis_index("expert")
    scale_factor = (DH + DR) ** (-0.5)
    slice_rows = kv_down_weight.shape[0]
    joint_width = KVR + DR
    n_gain, n_kv_gain = attn_gain.shape[0], kv_gain.shape[0]

    bits = bits_of(expert_count)
    head_step = expert_count * dp_count // H
    pair_bit = max(4, head_step)
    rest = [bit for bit in bits if bit != pair_bit]
    head_low = pair_bit // head_step
    head_high = H // (dp_count * 2 * head_low)
    heads = head_high * head_low
    blocks = 2 * dp_count
    pair_rows = blocks * row_count

    far, second, first = rest
    orders = whole_orders(bits, pair_bit)
    parts = thirds(width)

    def column_parts(values):
        return [values[..., low:high] for low, high in parts]

    combined = jnp.sum(
        jnp.where(
            routes[:, :, None] == jnp.arange(expert_count, dtype=jnp.int32),
            gates[:, :, None],
            0.0,
        ),
        axis=1,
    ).T
    gates_high = lax.reduce_precision(combined, 8, 7)
    gates_low = (combined - gates_high).astype(bf16)
    gates_both = jnp.stack([gates_high.astype(bf16), gates_low], axis=1)
    gate_cols = 4 * row_count
    gates_both = gates_both.reshape(-1, gate_cols)
    gate_rows = gates_both.shape[0]
    gates_both = jnp.pad(gates_both, ((0, 0), (0, joint_width - gate_cols)))
    gains = jnp.concatenate([attn_gain, ffn_gain, kv_gain, lengths[0].astype(bf16)])
    gains = jnp.pad(gains, (0, joint_width - gains.shape[0]))[None]
    gain_row = slice_rows + gate_rows
    spare = -(gain_row + 1) % 16
    small = jnp.concatenate(
        [kv_down_weight, gates_both, jnp.pad(gains, ((0, spare), (0, 0)))], axis=0
    )

    def turned(values):
        split = values.reshape(values.shape[0], dp_count, expert_count, slice_rows)
        return split.transpose(0, 2, 1, 3).reshape(values.shape)

    def turned_back(values):
        split = values.reshape(values.shape[0], expert_count, dp_count, slice_rows)
        return split.transpose(0, 2, 1, 3).reshape(values.shape)

    q_cols = heads * (DH + DR)
    up_cols = heads * (DH + DV) * n_kv_gain // slice_rows
    head_cols = q_cols + up_cols
    head_rows = dp_count * slice_rows

    def by_pair(weight, head_width, *cuts):
        split = weight.reshape(-1, dp_count, head_high, 2, head_low, head_width)
        split = split.transpose(1, 3, 0, 2, 4, 5)
        lead = (dp_count, 2, slice_rows, -1)
        return [part.reshape(lead) for part in jnp.split(split, cuts, axis=-1)]

    by_head = dp_swap(
        jnp.concatenate(
            by_pair(q_weight, DH + DR, DH, DH + DR // 2) + by_pair(kv_up_weight, DH + DV), axis=-1
        )
    )
    nope_cols = heads * DH
    rope_cols = heads * DR // 2

    def spread(columns):
        if rope_cols == ROPE_LANES:
            return columns
        parts = jnp.split(columns[:, :q_cols], (nope_cols, nope_cols + rope_cols), axis=-1)
        room = ((0, 0), (0, ROPE_LANES - rope_cols))
        return jnp.concatenate([parts[0], jnp.pad(parts[1], room), jnp.pad(parts[2], room)], axis=-1)

    def unspread(columns):
        if rope_cols == ROPE_LANES:
            return columns
        parts = jnp.split(columns, (nope_cols, nope_cols + ROPE_LANES), axis=-1)
        return jnp.concatenate([parts[0], parts[1][:, :rope_cols], parts[2][:, :rope_cols]], axis=-1)

    out_cut = out_weight.reshape(slice_rows, -1, 2, head_cols).transpose(2, 1, 0, 3)
    out_cut = out_cut.reshape(2, -1, head_cols)
    head_cut = head_rows * 3 // 8
    out_mid = out_cut.shape[1] // 2

    share = shared_down.shape[0]
    units = dp_count * share
    padded = -(-units // 128) * 128

    def shared_by_unit(results, found, weight):
        split = weight.reshape(slice_rows, 2, dp_count, expert_count, share)
        split = split.transpose(3, 0, 1, 2, 4).reshape(expert_count, slice_rows, 2, units)
        split = jnp.pad(split, ((0, 0), (0, 0), (0, 0), (0, padded - units)))
        return split.reshape(expert_count, slice_rows, 2 * padded)

    pair_w = lax.all_gather(expert_gate_up[0].reshape(width // dp_count, -1), "dp", tiled=True)
    down_w = lax.all_gather(expert_down[0], "dp", tiled=True)
    def shared_weights(split, shared_down):
        split = lax.all_to_all(split, "expert", split_axis=0, concat_axis=0, tiled=True)
        down = dp_gather(shared_down).reshape(units, width)
        down = jnp.pad(down, ((0, padded - units), (0, 0)))
        return dp_gather(split).reshape(width, 2 * padded), down

    def attend(all_rows, small_all, by_head, out_parts):
        joint_all = dp_gather(small_all[:, :slice_rows])
        kv_down = joint_all.transpose(1, 0, 2, 3).reshape(width, joint_width)
        copies = 2 * ROPE_LANES // DR
        gains_all = dp_gather(small_all[:, gain_row])
        attn_scale = gains_all[..., :n_gain].transpose(1, 0, 2).reshape(-1)
        ffn_scale = gains_all[..., n_gain : 2 * n_gain].reshape(-1)
        n_gains = 2 * n_gain + n_kv_gain
        kv_scale = gains_all[..., 2 * n_gain : n_gains].reshape(-1)
        all_lengths = gains_all[..., n_gains : n_gains + lengths.shape[1]].astype(jnp.int32)
        low = me & ~pair_bit
        all_lengths = jnp.stack([pick(all_lengths, low, 1), pick(all_lengths, low | pair_bit, 1)])
        all_lengths = all_lengths.reshape(blocks, -1)
        doc_ids, offsets = jax.vmap(lambda row: layout(row, row_count))(all_lengths)
        cos, sin = [
            jnp.tile(table.reshape(pair_rows, DR // 2), (1, copies))
            for table in angles(offsets, DR)
        ]
        all_rows = dp_gather(all_rows).transpose(1, 0, 2, 3).reshape(pair_rows, width)
        by_head = jnp.concatenate(by_head, axis=1)
        q_full = spread(by_head.reshape(width, head_cols))
        kv_up = by_head[..., q_cols:].reshape(expert_count, dp_count, n_kv_gain, -1)
        kv_up = kv_up.transpose(1, 0, 2, 3).reshape(KVR, heads * (DH + DV))
        out_full = jnp.concatenate(out_parts, axis=1)
        at = bits.index(pair_bit)
        out_full = out_full.reshape((2,) * len(bits) + (-1, slice_rows, head_cols))
        out_full = jnp.moveaxis(out_full, (len(bits), at), (-3, -2)).reshape(heads * DV, width)
        wide = nope_cols + 2 * ROPE_LANES
        outs = by_rows_call(
            functools.partial(attend_kernel, heads),
            pair_rows // (4 * row_count),
            ("x", "gain", "kv_gain", "down", "q", "up", "out", "cos", "sin", "column", "row"),
            dict(
                x=all_rows,
                cos=cos,
                sin=sin,
                column=doc_ids.reshape(pair_rows, 1),
                row=doc_ids.reshape(blocks, 1, row_count),
            ),
            dict(
                gain=attn_scale.astype(f32)[None],
                kv_gain=kv_scale.astype(f32)[None],
                down=kv_down,
                q=q_full,
                up=kv_up,
                out=out_full,
            ),
            (
                ("normed", (pair_rows, width), bf16),
                ("joint", (pair_rows, joint_width), f32),
                ("kv_normed", (pair_rows, KVR), bf16),
                ("heads", (pair_rows, wide), bf16),
                ("keys", (pair_rows, wide), bf16),
                ("values", (pair_rows, heads * DV), bf16),
                ("probs", (blocks * heads, row_count, row_count), f32),
                ("attended", (pair_rows, heads * DV), bf16),
                ("sum", (pair_rows, width), bf16),
            ),
        )
        return outs, (q_full, kv_up, out_full, kv_down), (attn_scale, kv_scale, ffn_scale), (cos, sin)

    def cut_out(found):
        at = bits.index(pair_bit)
        found = found.reshape((2,) * len(rest) + (slice_rows, -1, 2, head_cols))
        found = jnp.moveaxis(found, (-3, -2), (len(bits), at))
        return found.reshape(expert_count, -1, head_cols)

    def by_owner(found):
        found = found.reshape(2, dp_count, row_count, -1).transpose(1, 0, 2, 3)
        return dp_scatter(found, bf16).astype(bf16)

    (all_rows, by_head), (shared_split,) = march(
        gathering(turned(tokens), [pair_bit]),
        pair_swapping(by_head, pair_bit, 1),
        jobs=((shared_by_unit, shared_gate_up),),
    )
    by_head = by_head.reshape(2, head_rows, head_cols)
    held_grad = []
    results, found = march(
        *(
            gathering(part, order, [pair_bit])
            for part, order in (
                (by_head[:, :head_cut], (second, far, first)),
                (by_head[:, head_cut:], (far, first, second)),
                (out_cut[:, :out_mid], (second, first, far)),
                (out_cut[:, out_mid:], (far, second, first)),
            )
        ),
        gathering(small, (far, first, second, pair_bit)),
        jobs=((skip,), (skip,), (lambda results, found, part: held_grad.append(part), out_grad)),
    )

    grad_all = lax.all_gather(held_grad[0], "expert")
    outs, weights, scales, tables = attend(all_rows, results[4], results[:2], results[2:4])
    normed, joint, kv_normed, query_parts, key_parts, values, probs, attended, attended_sum = outs
    q_full, kv_up, out_full, kv_down = weights
    attn_scale, kv_scale, ffn_scale = scales
    attended_sum = by_owner(attended_sum)
    shared_w, shared_out = shared_weights(shared_split, shared_down)
    hidden = down_w.shape[0]
    gates_all = results[4][:, slice_rows:gain_row, :gate_cols]
    gates_all = gates_all.reshape(expert_count, expert_count, 2, row_count)
    own_gate = pick(gates_all, me, 1).astype(f32).sum(axis=1)

    capacity = min(row_count, 3 * row_count * TOP // (2 * expert_count))
    slots = expert_count * capacity
    group_rows = expert_count * row_count
    grad_rows = grad_all.reshape(group_rows, width)
    live = own_gate > 0.0
    slot = jnp.cumsum(live.astype(jnp.int32), axis=1) - 1
    slot = slot + capacity * (jnp.arange(expert_count, dtype=jnp.int32) % 2)[:, None]
    slot = jnp.where(live, slot, -1).reshape(expert_count // 2, 1, 2 * row_count)
    gate = own_gate.reshape(expert_count // 2, 1, 2 * row_count)
    chunk = 4 * row_count

    steps = group_rows // chunk
    my_place = [((me & bit) != 0).astype(jnp.int32) for bit in (pair_bit, second, first)]
    my_place = jnp.stack(my_place)

    def group(i):
        return i if pair_bit == 4 else (i % 2) * (steps // 2) + i // 2

    def halves_of(name):
        return [
            (f"{name}{i}{kind}", (group_rows // 2, high - low), bf16)
            for i, (low, high) in enumerate(parts)
            for kind in ("kept", "sent")
        ]

    def from_gradient(results, found, grad_rows):
        return by_rows_call(
            functools.partial(gradient_kernel, 2 * capacity),
            steps,
            ("grad", "slot", "gate", "down", "shared"),
            dict(grad=grad_rows, slot=slot, gate=gate),
            dict(down=down_w, shared=shared_out),
            (
                ("picked", (slots, width), bf16),
                ("d_hidden", (slots, hidden), f32),
                ("d_shared", (group_rows, padded), f32),
            ),
        )

    attended_sum = alone(scattering(attended_sum, [pair_bit], [pair_bit]))
    resid_in = tokens.astype(f32)
    upstream = out_grad.astype(f32)
    resid = resid_in + attended_sum
    ffn_in = norm_apply(resid, ffn_scale).astype(bf16)

    ffn_parts, ((slot_grad, d_hidden, d_shared_hidden), *unused) = march(
        *(gathering(part, order, whole=False) for part, order in zip(column_parts(ffn_in), orders)),
        jobs=((from_gradient, grad_rows),),
    )
    names = [f"in{i}{kind}" for i in range(3) for kind in ("held", "came")]
    ffn_parts = [part.reshape(group_rows // 2, -1) for both in ffn_parts for part in both]
    ffn_rows, rows, expert_hidden, d_pair, shared_hidden, d_shared_pair, *d_parts = by_rows_call(
        functools.partial(expert_kernel, 2 * capacity),
        steps,
        ["slot", "d_hidden", "d_shared", "pair", "shared"] + names,
        dict(zip(names, ffn_parts), slot=slot, d_hidden=d_hidden, d_shared=d_shared_hidden),
        dict(pair=pair_w, shared=shared_w),
        [
            ("x", (group_rows, width), bf16),
            ("rows", (slots, width), bf16),
            ("hidden", (slots, hidden), bf16),
            ("d_pair", (slots, 2 * hidden), bf16),
            ("shared_hidden", (group_rows, padded), bf16),
            ("d_shared_pair", (group_rows, 2 * padded), bf16),
        ]
        + halves_of("out"),
        group=group,
        scalars=(my_place,),
        half=("in0held", "in0came", "out0kept", "out0sent"),
    )
    d_parts = [(d_parts[2 * i], d_parts[2 * i + 1]) for i in range(3)]

    def output_part(results, found, expert_hidden, shared_hidden):
        return by_rows_call(
            functools.partial(output_kernel, 2 * capacity),
            steps,
            ("hidden", "shared_hidden", "slot", "gate", "down", "shared"),
            dict(hidden=expert_hidden, shared_hidden=shared_hidden, slot=slot, gate=gate),
            dict(down=down_w, shared=shared_out),
            halves_of("out"),
            scratch=[pltpu.VMEM((slots // steps, width), bf16)],
            group=group,
            scalars=(my_place,),
            half=("out0kept", "out0sent"),
        )

    def halves(found):
        if dp_count != 2:
            return lax.psum_scatter(found.astype(bf16), "dp", scatter_dimension=0), ()
        return pick(found, core, 0), pick(found, 1 - core, 0).astype(bf16)

    def exchanged(kept, sent):
        if dp_count != 2:
            return kept.astype(f32)
        return kept + lax.ppermute(sent, "dp", [(0, 1), (1, 0)]).astype(f32)

    def pair_kept(results, found, rows, d_pair):
        if dp_count != 2:
            found = dot(rows.T, d_pair).astype(bf16).reshape(dp_count, width // dp_count, -1)
            return lax.psum_scatter(found, "dp", scatter_dimension=0)
        return columns_product(rows, d_pair, core, dp_count, f32)

    def pair_sent(results, found, rows, d_pair):
        if dp_count != 2:
            return ()
        return columns_product(rows, d_pair, 1 - core, dp_count, bf16)

    def down_gradient(results, found, expert_hidden, slot_grad):
        return halves(
            dot(expert_hidden.T, slot_grad).reshape(dp_count, hidden // dp_count, width)
        )

    def shared_gradient(results, found, shared_hidden, d_shared_pair):
        down = columns_product(shared_hidden, grad_rows, jnp.int32(0), 1, f32)
        down = down[:units].reshape(dp_count, share, width)
        both = columns_product(ffn_rows, d_shared_pair, jnp.int32(0), 1, bf16)
        both = both.reshape(dp_count, expert_count, slice_rows, 2 * padded)
        return dp_scatter(down, bf16), dp_scatter(both, bf16).astype(bf16)

    d_sums, found = march(
        *(scattering(part, order[::-1], bits) for part, order in zip(d_parts, orders)),
        jobs=(
            (pair_sent, rows, d_pair),
            (down_gradient, expert_hidden, slot_grad),
            (shared_gradient, shared_hidden, d_shared_pair),
            (output_part, expert_hidden, shared_hidden),
        ),
    )
    sent, down_halves, (grad_shared_out, grad_shared), out_part = found
    rows, d_pair = after((rows, d_pair), d_sums)
    d_ffn_in = jnp.concatenate(d_sums, axis=-1)

    d_norm_resid, grad_ffn_scale = norm_back(resid, ffn_scale, d_ffn_in)
    d_resid = upstream + d_norm_resid
    out_part = [(out_part[2 * i], out_part[2 * i + 1]) for i in range(3)]

    def attend_back(results, found, d_branch):
        d_branch = dp_gather(d_branch).transpose(1, 0, 2, 3).reshape(pair_rows, width)
        steps = pair_rows // (4 * row_count)
        wide = nope_cols + 2 * ROPE_LANES
        outs = by_rows_call(
            functools.partial(attend_back_kernel, heads),
            steps,
            (
                "branch", "out", "probs", "heads", "keys", "values", "joint", "kv_gain", "up", "q",
                "down", "cos", "sin",
            ),
            dict(
                branch=d_branch,
                probs=probs,
                heads=query_parts,
                keys=key_parts,
                values=values,
                joint=joint,
                cos=tables[0],
                sin=tables[1],
            ),
            dict(
                out=out_full,
                kv_gain=kv_scale.astype(f32)[None],
                up=kv_up,
                q=q_full,
                down=kv_down,
            ),
            (
                ("d_q", (pair_rows, wide), bf16),
                ("d_kv", (pair_rows, heads * (DH + DV)), bf16),
                ("d_joint", (pair_rows, joint_width), bf16),
                ("d_gain", (steps, 1, KVR), f32),
                ("sum", (pair_rows, width), bf16),
            ),
            scratch=[pltpu.VMEM((4 * row_count, DR), f32)],
        )
        return d_branch, outs

    def weight_gradients(results, found):
        d_branch, (d_q_heads, d_kv_heads, d_joint, unused, unused) = found[0]
        grad_q = unspread(dot(normed.T, d_q_heads)).astype(bf16)
        grad_q = grad_q.reshape(expert_count, head_rows, q_cols)
        grad_up = dot(kv_normed.T, d_kv_heads).astype(bf16)
        grad_up = grad_up.reshape(dp_count, expert_count, n_kv_gain, -1).transpose(1, 0, 2, 3)
        grad_up = grad_up.reshape(expert_count, head_rows, up_cols)
        by_head = jnp.concatenate([grad_q, grad_up], axis=-1)
        grad_out = cut_out(dot(attended.T, d_branch).astype(bf16))
        grad_kvdown = dot(normed.T, d_joint)
        grad_kvdown = grad_kvdown.reshape(expert_count, dp_count, slice_rows, joint_width)
        return by_head, grad_out, dp_scatter(grad_kvdown.transpose(1, 0, 2, 3), bf16)

    sums = []

    def back_of(results, found):
        return attend_back(results, found, results[0])

    def sum_and_gradients(results, found):
        sums.append(by_owner(found[1][1][4]))
        return weight_gradients(results, found[1:])

    (unused, d_normed, *results), found = march(
        gathering(d_resid.astype(bf16), [pair_bit]),
        deferred(3, lambda: scattering(sums[0], [pair_bit], [pair_bit])),
        *(
            scattering(after(part, d_resid), order[::-1], bits)
            for part, order in zip(out_part, orders)
        ),
        jobs=((pair_kept, rows, d_pair), (back_of,), (sum_and_gradients,)),
    )
    pair_halves = (found[0], sent)
    output = (resid + jnp.concatenate(results, axis=-1)).astype(bf16)
    grad_heads, grad_out, grad_kvdown = found[2]
    grad_kv_scale = found[1][1][3].sum(axis=0)
    pair_halves, down_halves, grad_shared = after((pair_halves, down_halves, grad_shared), results)
    d_norm_in, grad_attn_scale = norm_back(turned(resid_in), attn_scale, d_normed)
    grad_in = (d_resid + turned_back(d_norm_in)).astype(bf16)
    scale_sums = jnp.concatenate(
        [
            grad_attn_scale.reshape(expert_count, dp_count, n_gain).transpose(1, 0, 2),
            grad_ffn_scale.reshape(dp_count, expert_count, n_gain),
            grad_kv_scale.reshape(dp_count, expert_count, n_kv_gain),
        ],
        axis=-1,
    )
    scale_sums = jnp.pad(scale_sums, ((0, 0), (0, 0), (0, joint_width - scale_sums.shape[-1])))
    scale_sums = dp_scatter(scale_sums)[:, None]
    small_sums = jnp.concatenate([grad_kvdown, scale_sums], axis=1).astype(bf16)

    def finish_pair(results, found, kept, sent):
        return exchanged(kept, sent).reshape(expert_gate_up.shape)

    def finish_down(results, found, kept, sent, shared):
        shared = lax.all_to_all(shared, "expert", split_axis=0, concat_axis=0, tiled=True)
        return exchanged(kept, sent).reshape(expert_down.shape), shared

    def finish_shared(results, found):
        both = found[1][1].reshape(expert_count, slice_rows, 2, padded)[..., :units]
        both = both.reshape(expert_count, slice_rows, 2, dp_count, share)
        return both.transpose(1, 2, 3, 0, 4).reshape(shared_gate_up.shape).astype(f32)

    def whole_heads(found, rows, *widths):
        cuts = [heads * sum(widths[: i + 1]) for i in range(len(widths) - 1)]
        lead = (dp_count, 2, rows, head_high, head_low, -1)
        found = jnp.concatenate(
            [part.reshape(lead) for part in jnp.split(found, cuts, axis=-1)], axis=-1
        )
        return found.transpose(2, 0, 3, 1, 4, 5).reshape(rows, -1).astype(f32)

    summed, found = march(
        scattering(small_sums, (pair_bit, second, first, far), bits),
        *(
            scattering(part, order, bits, bf16)
            for part, order in (
                (grad_heads[:, :head_cut], (first, far, second)),
                (grad_heads[:, head_cut:], (second, first, far)),
                (grad_out[:, :out_mid], (far, first, second)),
                (grad_out[:, out_mid:], (first, second, far)),
            )
        ),
        jobs=(
            (finish_pair, *pair_halves),
            (finish_down, *down_halves, grad_shared),
            (finish_shared,),
        ),
    )
    grad_pair, (grad_down, unused), grad_shared = found[:3]
    by_head = jnp.concatenate(summed[1:3], axis=1)
    by_head = alone(pair_swapping(by_head, pair_bit, 0)).reshape(2, dp_count, slice_rows, head_cols)
    by_head = dp_swap(by_head.transpose(1, 0, 2, 3))
    grad_q = whole_heads(by_head[..., :q_cols], slice_rows, DH, DR // 2, DR // 2)
    grad_up = by_head[..., q_cols:].reshape(dp_count, 2, n_kv_gain, -1)
    grad_up = whole_heads(grad_up, n_kv_gain, DH + DV)
    grad_out = jnp.concatenate(summed[3:5], axis=1).reshape(2, -1, slice_rows, head_cols)
    grad_out = grad_out.transpose(2, 1, 0, 3).reshape(out_weight.shape).astype(f32)
    small_sums = summed[0]
    grad_kvdown = small_sums[:slice_rows]
    scale_sums = small_sums[slice_rows]

    return (
        output,
        grad_in,
        scale_sums[:n_gain],
        scale_sums[2 * n_gain : 2 * n_gain + n_kv_gain],
        scale_sums[n_gain : 2 * n_gain],
        grad_q,
        grad_kvdown,
        grad_up,
        grad_out,
        grad_shared,
        grad_shared_out,
        grad_pair,
        grad_down,
    )


def solution(mesh):
    rows = P(SPLIT, None)
    each = P(SPLIT)
    cube = P(SPLIT, None, None)
    pair = P("expert", "dp", None, None)
    down = P("expert", "dp", None)
    dense = (rows, rows, rows, rows, cube, rows)
    return jax.shard_map(
        shards,
        mesh=mesh,
        in_specs=(rows, each, each, each) + dense + (pair, down, rows, rows, rows, rows),
        out_specs=(rows, rows, each, each, each) + dense + (pair, down),
        check_vma=False,
    )
```

```python
import functools

import jax
import jax.numpy as jnp
from jax import lax
from jax.experimental import pallas as pl
from jax.experimental.pallas import tpu as pltpu
from jax.sharding import PartitionSpec as P

H = 16
DH = 128
DR = 64
DV = 128
KVR = 512
TOP = 6
SPLIT = ("dp", "expert")
ROPE_LANES = 128

f32 = jnp.float32
bf16 = jnp.bfloat16

norm_eps = 1e-06
rope_base = 50000.0
masked_score = -1e30


def norm_apply(values, scales):
    return values * lax.rsqrt(jnp.mean(values * values, axis=-1, keepdims=True) + norm_eps) * scales


def norm_back(values, scales, upstream):
    unused, pullback = jax.vjp(norm_apply, values, scales.astype(f32))
    return pullback(upstream)


def rotate(values, cosine_table, sine_table):
    half_width = values.shape[-1] // 2
    front_half = values[..., :half_width]
    back_half = values[..., half_width:]
    return jnp.concatenate(
        [
            front_half * cosine_table - back_half * sine_table,
            front_half * sine_table + back_half * cosine_table,
        ],
        axis=-1,
    )


def swish_gate(gate_part, up_part):
    return gate_part * jax.nn.sigmoid(gate_part) * up_part


def swish_back(gate_part, up_part, upstream):
    unused, pullback = jax.vjp(swish_gate, gate_part, up_part)
    return jnp.concatenate(pullback(upstream), axis=-1)


def layout(lengths_row, row_count):
    doc_ends = jnp.cumsum(lengths_row)
    places = jnp.arange(row_count, dtype=jnp.int32)
    passed_end = (places[:, None] >= doc_ends[None, :]).astype(jnp.int32)
    doc_ids = jnp.sum(passed_end, axis=1)
    starts = jnp.sum(passed_end * lengths_row[None, :], axis=1)
    return (doc_ids, places - starts)


def angles(offsets, rope_width):
    frequency = rope_base ** (-2.0 * jnp.arange(rope_width // 2, dtype=f32) / rope_width)
    turned = offsets.astype(f32)[..., None] * frequency
    return (jnp.cos(turned), jnp.sin(turned))


def dot(left, right):
    return jnp.dot(left, right, preferred_element_type=f32)


def pick(values, place, axis):
    return lax.dynamic_index_in_dim(values, place, axis, keepdims=False)


def dp_gather(values):
    if lax.axis_size("dp") != 2:
        return lax.all_gather(values, "dp")
    other = lax.ppermute(values, "dp", [(0, 1), (1, 0)])
    first = lax.axis_index("dp") == 0
    return jnp.stack([jnp.where(first, values, other), jnp.where(first, other, values)])


def dp_swap(values):
    if lax.axis_size("dp") != 2:
        return lax.all_to_all(values, "dp", split_axis=0, concat_axis=0)
    core = lax.axis_index("dp")
    own = pick(values, core, 0)
    other = lax.ppermute(pick(values, 1 - core, 0), "dp", [(0, 1), (1, 0)])
    first = core == 0
    return jnp.stack([jnp.where(first, own, other), jnp.where(first, other, own)])


def dp_scatter(values, sent=f32):
    if lax.axis_size("dp") != 2:
        return lax.psum_scatter(values.astype(sent), "dp", scatter_dimension=0).astype(f32)
    core = lax.axis_index("dp")
    other = lax.ppermute(pick(values, 1 - core, 0).astype(sent), "dp", [(0, 1), (1, 0)])
    return pick(values, core, 0).astype(f32) + other.astype(f32)


def dp_sum(values):
    if lax.axis_size("dp") != 2:
        return lax.psum(values, "dp")
    return values + lax.ppermute(values, "dp", [(0, 1), (1, 0)])


def bits_of(count):
    return [1 << place for place in reversed(range(count.bit_length() - 1))]


def partner(values, bit):
    count = lax.axis_size("expert")
    return lax.ppermute(values, "expert", [(i, i ^ bit) for i in range(count)])


def gathering(values, order, held=(), lead=0, whole=True):
    me = lax.axis_index("expert")
    held = list(held)
    for step, bit in enumerate(order):
        if not whole and step + 1 == len(order):
            values = values.reshape((-1,) + values.shape[lead + len(held) :])
            if values.shape[1] % 128 == 0:
                values = values.reshape(-1, values.shape[-1])
            return values, (yield partner(values, bit))
        other = yield partner(values, bit)
        low = (me & bit) == 0
        values = jnp.stack(
            [jnp.where(low, values, other), jnp.where(low, other, values)],
            axis=lead + sum(1 for known in held if known > bit),
        )
        held.append(bit)
    return values.reshape(values.shape[:lead] + (-1,) + values.shape[lead + len(held) :])


def scattering(values, order, bits, kept=f32, lead=0):
    me = lax.axis_index("expert")
    bits = list(bits)
    split = isinstance(values, tuple)
    if not split:
        values = values.reshape(values.shape[:lead] + (2,) * len(bits) + values.shape[lead + 1 :])
    for step, bit in enumerate(order):
        axis = lead + bits.index(bit)
        bits.remove(bit)
        place = ((me & bit) != 0).astype(jnp.int32)
        if split and step == 0:
            own, sent = values
        else:
            own, sent = pick(values, place, axis), pick(values, 1 - place, axis)
        other = yield partner(sent, bit)
        if step + 1 < len(order):
            values = own + other
        else:
            values = (own.astype(f32) + other.astype(f32)).astype(kept)
        if split and step == 0:
            values = values.reshape((2,) * len(bits) + (-1,) + values.shape[-1:])
    if bits:
        values = values.reshape(values.shape[:lead] + (-1,) + values.shape[lead + len(bits) :])
    return values


def later(steps, values, chain):
    for _ in range(steps):
        values = yield values
    return (yield from chain(values))


def begun(chain, values):
    while True:
        try:
            values = chain.send(values)
        except StopIteration as stop:
            return stop.value
        values = yield values


def last_of(chain, values):
    try:
        chain.send(values)
    except StopIteration as stop:
        return stop.value


def deferred(steps, make):
    for _ in range(steps):
        yield ()
    return (yield from make())


def pair_swapping(values, bit, axis):
    place = ((lax.axis_index("expert") & bit) != 0).astype(jnp.int32)
    own = pick(values, place, axis)
    other = yield partner(pick(values, 1 - place, axis), bit)
    low = place == 0
    return jnp.stack([jnp.where(low, own, other), jnp.where(low, other, own)])


def march(*chains, jobs=()):
    results, found = [None] * len(chains), []
    live = {i: next(chain) for i, chain in enumerate(chains)}
    waiting = [operands for _, *operands in jobs]
    while live or len(found) < len(jobs):
        step = len(found)
        job = jobs[step][0](results, found, *waiting[step]) if step < len(jobs) else ()
        live, job, waiting = lax.optimization_barrier((live, job, waiting[step + 1 :]))
        waiting = [()] * (step + 1) + waiting
        found.append(job)
        following = {}
        for i, values in live.items():
            try:
                following[i] = chains[i].send(values)
            except StopIteration as stop:
                results[i] = stop.value
        live = following
    return results, found


def skip(results, found):
    return ()


def alone(chain, *markers):
    values = next(chain)
    step = 0
    while True:
        if step < len(markers):
            values = after(values, markers[step])
        step += 1
        try:
            values = chain.send(values)
        except StopIteration as stop:
            return stop.value


def after(values, *others):
    return lax.optimization_barrier((values, others))[0]


def thirds(width):
    side = width // 128 // 3 * 128
    return (0, side), (side, width - side), (width - side, width)


def whole_orders(bits, pair_bit):
    far, second, first = [bit for bit in bits if bit != pair_bit]
    return (
        (second, far, first, pair_bit),
        (far, first, pair_bit, second),
        (far, pair_bit, second, first),
    )


def lanes_dot(left, right):
    return lax.dot_general(left, right, (((1,), (1,)), ((), ())), preferred_element_type=f32)


def rows_dot(left, right):
    return lax.dot_general(left, right, (((0,), (0,)), ((), ())), preferred_element_type=f32)


def head_lanes(heads):
    lane = lax.broadcasted_iota(jnp.int32, (1, ROPE_LANES), 1) // (DR // 2)
    return [(lane == head).astype(f32) for head in range(heads)]


def attend_kernel(
    heads,
    x_ref,
    gain_ref,
    kv_gain_ref,
    down_ref,
    q_ref,
    up_ref,
    out_ref,
    cos_ref,
    sin_ref,
    column_ref,
    row_ref,
    normed_ref,
    joint_ref,
    kv_normed_ref,
    heads_ref,
    keys_ref,
    values_ref,
    probs_ref,
    attended_ref,
    sum_ref,
):
    nope = heads * DH
    rows = x_ref.shape[0]
    x = x_ref[...].astype(f32)
    scale = lax.rsqrt(jnp.mean(x * x, axis=-1, keepdims=True) + norm_eps)
    normed_ref[...] = (x * scale * gain_ref[...]).astype(bf16)
    joint_ref[...] = dot(normed_ref[...], down_ref[...])
    latent = joint_ref[:, :KVR]
    scale = lax.rsqrt(jnp.mean(latent * latent, axis=-1, keepdims=True) + norm_eps)
    kv_normed_ref[...] = (latent * scale * kv_gain_ref[...]).astype(bf16)
    copies = 2 * ROPE_LANES // DR
    cos, sin = [jnp.concatenate([ref[...]] * copies, axis=-1) for ref in (cos_ref, sin_ref)]
    front = jnp.concatenate([joint_ref[:, KVR : KVR + DR // 2]] * copies, axis=-1)
    back = jnp.concatenate([joint_ref[:, KVR + DR // 2 :]] * copies, axis=-1)
    keys_ref[:, nope : nope + ROPE_LANES] = (front * cos - back * sin).astype(bf16)
    keys_ref[:, nope + ROPE_LANES :] = (front * sin + back * cos).astype(bf16)
    q = dot(normed_ref[...], q_ref[:, : nope + 2 * ROPE_LANES])
    front = q[:, nope : nope + ROPE_LANES]
    back = q[:, nope + ROPE_LANES :]
    heads_ref[:, :nope] = q[:, :nope].astype(bf16)
    heads_ref[:, nope : nope + ROPE_LANES] = (front * cos - back * sin).astype(bf16)
    heads_ref[:, nope + ROPE_LANES :] = (front * sin + back * cos).astype(bf16)
    kv = dot(kv_normed_ref[...], up_ref[...])
    for head in range(heads):
        start = head * (DH + DV)
        keys_ref[:, head * DH : (head + 1) * DH] = kv[:, start : start + DH].astype(bf16)
        values_ref[:, head * DV : (head + 1) * DV] = kv[:, start + DH : start + DH + DV].astype(bf16)
    tile = probs_ref.shape[-1]
    causal = lax.broadcasted_iota(jnp.int32, (tile, tile), 0) >= lax.broadcasted_iota(
        jnp.int32, (tile, tile), 1
    )
    own = head_lanes(heads)
    for block in range(rows // tile):
        part = pl.ds(block * tile, tile)
        allowed = (column_ref[part, :] == row_ref[block]) & causal
        rotary = heads_ref[part, nope:].astype(f32)
        for head in range(heads):
            both = jnp.concatenate([own[head], own[head]], axis=-1)
            scores = lanes_dot(
                heads_ref[part, head * DH : (head + 1) * DH],
                keys_ref[part, head * DH : (head + 1) * DH],
            ) + lanes_dot((rotary * both).astype(bf16), keys_ref[part, nope:])
            scores = jnp.where(allowed, scores * (DH + DR) ** (-0.5), masked_score)
            weights = jnp.exp(scores - jnp.max(scores, axis=-1, keepdims=True))
            probs = weights / jnp.sum(weights, axis=-1, keepdims=True)
            probs_ref[block * heads + head] = probs
            attended_ref[part, head * DV : (head + 1) * DV] = dot(
                probs.astype(bf16), values_ref[part, head * DV : (head + 1) * DV]
            ).astype(bf16)
    sum_ref[...] = dot(attended_ref[...], out_ref[...]).astype(sum_ref.dtype)


def attend_back_kernel(
    heads,
    branch_ref,
    out_ref,
    probs_ref,
    heads_ref,
    keys_ref,
    values_ref,
    joint_ref,
    kv_gain_ref,
    up_ref,
    q_ref,
    down_ref,
    cos_ref,
    sin_ref,
    d_q_ref,
    d_kv_ref,
    d_joint_ref,
    d_gain_ref,
    sum_ref,
    d_key_ref,
):
    nope = heads * DH
    rows = branch_ref.shape[0]
    tile = probs_ref.shape[-1]
    factor = (DH + DR) ** (-0.5)
    d_attended = lanes_dot(branch_ref[...], out_ref[...]).astype(bf16)
    own = head_lanes(heads)
    for block in range(rows // tile):
        part = slice(block * tile, (block + 1) * tile)
        rotary = heads_ref[part, nope:].astype(f32)
        d_rotary = jnp.zeros((tile, 2 * ROPE_LANES), f32)
        d_key = jnp.zeros((tile, 2 * ROPE_LANES), f32)
        for head in range(heads):
            both = jnp.concatenate([own[head], own[head]], axis=-1)
            columns = slice(head * DH, (head + 1) * DH)
            start = head * (DH + DV)
            upstream = d_attended[part, head * DV : (head + 1) * DV]
            probs = probs_ref[block * heads + head]
            d_kv_ref[part, start + DH : start + DH + DV] = rows_dot(
                probs.astype(bf16), upstream
            ).astype(bf16)
            d_probs = lanes_dot(upstream, values_ref[part, head * DV : (head + 1) * DV])
            d_scores = probs * (d_probs - jnp.sum(d_probs * probs, axis=-1, keepdims=True))
            d_scores = d_scores.astype(bf16)
            d_q_ref[part, columns] = (dot(d_scores, keys_ref[part, columns]) * factor).astype(bf16)
            d_rotary = d_rotary + dot(d_scores, keys_ref[part, nope:]) * (factor * both)
            d_kv_ref[part, start : start + DH] = (
                rows_dot(d_scores, heads_ref[part, columns]) * factor
            ).astype(bf16)
            d_key = d_key + rows_dot(d_scores, (rotary * both).astype(bf16)) * factor
        narrow = cos_ref[part, :], sin_ref[part, :]
        cos, sin = [jnp.concatenate([table] * (2 * ROPE_LANES // DR), axis=-1) for table in narrow]
        front, back = d_rotary[:, :ROPE_LANES], d_rotary[:, ROPE_LANES:]
        d_q_ref[part, nope : nope + ROPE_LANES] = (front * cos + back * sin).astype(bf16)
        d_q_ref[part, nope + ROPE_LANES :] = (back * cos - front * sin).astype(bf16)
        front, back = [
            sum(half[:, at : at + DR // 2] for at in range(0, ROPE_LANES, DR // 2))
            for half in (d_key[:, :ROPE_LANES], d_key[:, ROPE_LANES:])
        ]
        cos, sin = narrow
        d_key_ref[part, : DR // 2] = front * cos + back * sin
        d_key_ref[part, DR // 2 :] = back * cos - front * sin
    d_kv_normed = lanes_dot(d_kv_ref[...], up_ref[...])
    latent = joint_ref[:, :KVR]
    scale = lax.rsqrt(jnp.mean(latent * latent, axis=-1, keepdims=True) + norm_eps)
    d_gain_ref[0] = jnp.sum(d_kv_normed * latent * scale, axis=0, keepdims=True)
    d_kv_normed = d_kv_normed * kv_gain_ref[...]
    fall = jnp.mean(d_kv_normed * latent, axis=-1, keepdims=True) * scale * scale * scale
    d_joint_ref[:, :KVR] = (d_kv_normed * scale - latent * fall).astype(bf16)
    d_joint_ref[:, KVR:] = d_key_ref[...].astype(bf16)
    sum_ref[...] = (
        lanes_dot(d_q_ref[...], q_ref[:, : nope + 2 * ROPE_LANES])
        + lanes_dot(d_joint_ref[...], down_ref[...])
    ).astype(sum_ref.dtype)


def by_rows_call(
    kernel, steps, order, streamed, fixed, outs, scratch=(), group=lambda i: i, scalars=(), half=None
):
    half = half or ()

    def spec(name, shape):
        rest = (0,) * (len(shape) - 1)
        if name in half:
            block = (shape[0] * 2 // steps,) + shape[1:]
            return pl.BlockSpec(block, lambda i, *unused: (i // 2,) + rest)
        block = (shape[0] // steps,) + shape[1:]
        return pl.BlockSpec(block, lambda i, *unused: (group(i),) + rest)

    operands, specs = [], []
    for name in order:
        if name in streamed:
            operands.append(streamed[name])
            specs.append(spec(name, streamed[name].shape))
        else:
            value = fixed[name]
            operands.append(value)
            specs.append(
                pl.BlockSpec(
                    value.shape,
                    lambda i, *unused, ndim=value.ndim: (0,) * ndim,
                    pipeline_mode=pl.Buffered(1),
                )
            )
    return pl.pallas_call(
        kernel,
        grid_spec=pltpu.PrefetchScalarGridSpec(
            num_scalar_prefetch=len(scalars),
            grid=(steps,),
            in_specs=specs,
            out_specs=[spec(name, shape) for name, shape, dtype in outs],
            scratch_shapes=scratch,
        ),
        out_shape=[jax.ShapeDtypeStruct(shape, dtype) for name, shape, dtype in outs],
        compiler_params=pltpu.CompilerParams(vmem_limit_bytes=60 * 2**20),
    )(*scalars, *operands)


def without(index, place):
    return (index >> (place + 1) << place) | (index & ((1 << place) - 1))


def assemble_kernel(shape, me_ref, *refs):
    places, pair_place, slice_rows, pieces = shape
    sources, (q_ref, up_ref, out_ref) = refs[:8], refs[8:]
    q_cols, up_cols = q_ref.shape[1], sources[0].shape[-1] - q_ref.shape[1]
    piece_rows = slice_rows // pieces
    count = 2 * sources[0].shape[0]
    start = 0
    for which, place in enumerate(places):
        held_ref, came_ref = sources[2 * which : 2 * which + 2]
        if which == 2:
            start = 0
        size = held_ref.shape[1]

        def put(mine, start=start, size=size, which=which, place=place, both=(held_ref, came_ref)):
            for e in range(count):
                source = both[(e >> place & 1) ^ mine]
                at = without(e, place)
                if which >= 2:
                    row = without(e, pair_place) * slice_rows + start
                    half = (e >> pair_place & 1) * source.shape[-1]
                    out_ref[row : row + size, half : half + source.shape[-1]] = source[at]
                    continue
                row = e * 2 * slice_rows + start
                q_ref[row : row + size, :] = source[at, :, :q_cols]
                for piece in range(start // piece_rows, (start + size) // piece_rows):
                    core, column = piece // pieces, piece % pieces
                    row = (core * count + e) * piece_rows
                    begin = piece * piece_rows - start
                    up_ref[row : row + piece_rows, column * up_cols : (column + 1) * up_cols] = (
                        source[at, begin : begin + piece_rows, q_cols:]
                    )

        pl.when(me_ref[which] == 0)(functools.partial(put, 0))
        pl.when(me_ref[which] == 1)(functools.partial(put, 1))
        start += size


def attention_gradients_kernel(
    shape,
    normed_ref,
    d_q_ref,
    kv_normed_ref,
    d_kv_ref,
    attended_ref,
    branch_ref,
    d_joint_ref,
    first_ref,
    last_ref,
    out_first_ref,
    out_last_ref,
    joint_ref,
):
    pair_place, slice_rows, pieces = shape
    count, cut, _ = first_ref.shape
    out_cut = out_first_ref.shape[1]
    q_cols, piece_rows = d_q_ref.shape[1], slice_rows // pieces
    up_cols = first_ref.shape[-1] - q_cols
    up = rows_dot(kv_normed_ref[...], d_kv_ref[...]).astype(bf16)
    for e in range(count):
        for piece in range(2 * pieces):
            core, column = piece // pieces, piece % pieces
            row = (core * count + e) * piece_rows
            found = up[row : row + piece_rows, column * up_cols : (column + 1) * up_cols]
            begin = piece * piece_rows
            if begin < cut:
                first_ref[e, begin : begin + piece_rows, q_cols:] = found
            else:
                last_ref[e, begin - cut : begin - cut + piece_rows, q_cols:] = found
    width = normed_ref.shape[1]
    per = 4
    for at in range(0, count, per):
        columns = slice(at * 2 * slice_rows, (at + per) * 2 * slice_rows)
        found = rows_dot(normed_ref[:, columns], d_q_ref[...]).astype(bf16)
        for e in range(per):
            row = e * 2 * slice_rows
            first_ref[at + e, :, :q_cols] = found[row : row + cut]
            last_ref[at + e, :, :q_cols] = found[row + cut : row + 2 * slice_rows]
        found = rows_dot(normed_ref[:, columns], d_joint_ref[...]).astype(bf16)
        for e in range(per):
            for core in range(2):
                row = (2 * e + core) * slice_rows
                joint_ref[core, at + e] = found[row : row + slice_rows]
    found = rows_dot(attended_ref[...], branch_ref[...]).astype(bf16)
    half = width // 2
    for e in range(count):
        row = without(e, pair_place) * slice_rows
        side = (e >> pair_place & 1) * half
        out_first_ref[e] = found[row : row + out_cut, side : side + half]
        out_last_ref[e] = found[row + out_cut : row + slice_rows, side : side + half]


def whole_call(kernel, operands, outs, scalars=()):
    return pl.pallas_call(
        kernel,
        grid_spec=pltpu.PrefetchScalarGridSpec(
            num_scalar_prefetch=len(scalars),
            grid=(1,),
            in_specs=[
                pl.BlockSpec(value.shape, lambda i, *unused, ndim=value.ndim: (0,) * ndim)
                for value in operands
            ],
            out_specs=[
                pl.BlockSpec(shape, lambda i, *unused, ndim=len(shape): (0,) * ndim)
                for shape, dtype in outs
            ],
        ),
        out_shape=[jax.ShapeDtypeStruct(shape, dtype) for shape, dtype in outs],
        compiler_params=pltpu.CompilerParams(vmem_limit_bytes=60 * 2**20),
    )(*scalars, *operands)


def one_hot(slot_ref, place, count):
    slots = slot_ref[place]
    return lax.broadcasted_iota(jnp.int32, (count, slots.shape[1]), 0) == slots


def swiglu_back(gate_part, up_part, upstream):
    sigmoid = jax.nn.sigmoid(gate_part)
    silu = gate_part * sigmoid
    slope = sigmoid + silu * (1.0 - sigmoid)
    return silu * up_part, upstream * up_part * slope, upstream * silu


def gradient_kernel(
    count, grad_ref, slot_ref, gate_ref, down_ref, shared_ref, picked_ref, d_hidden_ref, d_shared_ref
):
    span = slot_ref.shape[-1]
    for place in range(slot_ref.shape[0]):
        chosen = one_hot(slot_ref, place, count)
        gate = jnp.sum(jnp.where(chosen, gate_ref[place], 0.0), axis=1, keepdims=True)
        found = dot(chosen.astype(bf16), grad_ref[place * span : (place + 1) * span])
        picked_ref[place * count : (place + 1) * count] = (found * gate).astype(bf16)
    d_hidden_ref[...] = lanes_dot(picked_ref[...], down_ref[...])
    d_shared_ref[...] = lanes_dot(grad_ref[...], shared_ref[...])


def halves_in(me_ref, refs, x_ref, parts, span):
    for (start, stop), (held_ref, came_ref), mine in zip(parts, refs, my_places(me_ref)):
        if start == 0:
            here = lax.rem(pl.program_id(0), 2) == mine

            @pl.when(here)
            def _():
                x_ref[:, start:stop] = held_ref[...]

            @pl.when(jnp.logical_not(here))
            def _():
                x_ref[:, start:stop] = came_ref[...]

            continue
        size = span if start == parts[1][0] else span // 2
        for at in range(2 * span // size):
            turn, place = (at // 2, at % 2) if size < span else (0, at)
            source = slice(turn * size, (turn + 1) * size)
            x_ref[at * size : (at + 1) * size, start:stop] = jnp.where(
                mine == place, held_ref[source].astype(f32), came_ref[source].astype(f32)
            ).astype(bf16)


def halves_out(me_ref, refs, values, which, span):
    (kept_ref, sent_ref), mine = refs[which], my_places(me_ref)[which]
    if which == 0:
        here = lax.rem(pl.program_id(0), 2) == mine

        @pl.when(here)
        def _():
            kept_ref[...] = values.astype(bf16)

        @pl.when(jnp.logical_not(here))
        def _():
            sent_ref[...] = values.astype(bf16)

        return
    size = span if which == 1 else span // 2
    for turn in range(span // size):
        low = values[2 * turn * size : (2 * turn + 1) * size]
        high = values[(2 * turn + 1) * size : (2 * turn + 2) * size]
        target = slice(turn * size, (turn + 1) * size)
        kept_ref[target] = jnp.where(mine == 0, low, high).astype(bf16)
        sent_ref[target] = jnp.where(mine == 0, high, low).astype(bf16)


def my_places(me_ref):
    return me_ref[0], me_ref[1], me_ref[2]


def expert_kernel(
    count,
    me_ref,
    slot_ref,
    d_hidden_ref,
    d_shared_ref,
    pair_ref,
    shared_ref,
    left_ref,
    left_came_ref,
    middle_ref,
    middle_came_ref,
    right_ref,
    right_came_ref,
    x_ref,
    rows_ref,
    hidden_ref,
    d_pair_ref,
    shared_hidden_ref,
    d_shared_pair_ref,
    left_kept_ref,
    left_sent_ref,
    middle_kept_ref,
    middle_sent_ref,
    right_kept_ref,
    right_sent_ref,
):
    span = slot_ref.shape[-1]
    parts = thirds(x_ref.shape[-1])
    halves_in(
        me_ref,
        ((left_ref, left_came_ref), (middle_ref, middle_came_ref), (right_ref, right_came_ref)),
        x_ref,
        parts,
        span,
    )
    places = range(slot_ref.shape[0])
    chosen = [one_hot(slot_ref, place, count).astype(bf16) for place in places]
    for place in places:
        rows_ref[place * count : (place + 1) * count] = dot(
            chosen[place], x_ref[place * span : (place + 1) * span]
        ).astype(bf16)
    hidden = hidden_ref.shape[-1]
    units, d_gate, d_up = swiglu_back(
        dot(rows_ref[...], pair_ref[:, :hidden]),
        dot(rows_ref[...], pair_ref[:, hidden:]),
        d_hidden_ref[...],
    )
    hidden_ref[...] = units.astype(bf16)
    d_pair_ref[:, :hidden] = d_gate.astype(bf16)
    d_pair_ref[:, hidden:] = d_up.astype(bf16)
    padded = shared_hidden_ref.shape[-1]
    units, d_gate, d_up = swiglu_back(
        dot(x_ref[...], shared_ref[:, :padded]),
        dot(x_ref[...], shared_ref[:, padded:]),
        d_shared_ref[...],
    )
    shared_hidden_ref[...] = units.astype(bf16)
    d_shared_pair_ref[:, :padded] = d_gate.astype(bf16)
    d_shared_pair_ref[:, padded:] = d_up.astype(bf16)
    refs = (
        (left_kept_ref, left_sent_ref),
        (middle_kept_ref, middle_sent_ref),
        (right_kept_ref, right_sent_ref),
    )
    for which, (start, stop) in enumerate(parts):
        back = lanes_dot(d_pair_ref[...], pair_ref[start:stop]).astype(bf16)
        found = [
            rows_dot(chosen[place], back[place * count : (place + 1) * count])
            + lanes_dot(d_shared_pair_ref[place * span : (place + 1) * span], shared_ref[start:stop])
            for place in places
        ]
        halves_out(me_ref, refs, jnp.concatenate(found, axis=0), which, span)


def output_kernel(
    count,
    me_ref,
    hidden_ref,
    shared_hidden_ref,
    slot_ref,
    gate_ref,
    down_ref,
    shared_ref,
    left_kept_ref,
    left_sent_ref,
    middle_kept_ref,
    middle_sent_ref,
    right_kept_ref,
    right_sent_ref,
    rows_ref,
):
    span = slot_ref.shape[-1]
    places = range(slot_ref.shape[0])
    chosen = [one_hot(slot_ref, place, count) for place in places]
    found = dot(hidden_ref[...], down_ref[...])
    for place in places:
        at = slice(place * count, (place + 1) * count)
        gate = jnp.sum(jnp.where(chosen[place], gate_ref[place], 0.0), axis=1, keepdims=True)
        rows_ref[at] = (found[at] * gate).astype(bf16)
    refs = (
        (left_kept_ref, left_sent_ref),
        (middle_kept_ref, middle_sent_ref),
        (right_kept_ref, right_sent_ref),
    )
    for which, (start, stop) in enumerate(thirds(down_ref.shape[-1])):
        found = [
            rows_dot(
                chosen[place].astype(bf16),
                rows_ref[place * count : (place + 1) * count, start:stop],
            )
            + dot(shared_hidden_ref[place * span : (place + 1) * span], shared_ref[:, start:stop])
            for place in places
        ]
        halves_out(me_ref, refs, jnp.concatenate(found, axis=0), which, span)


def columns_kernel(place_ref, left_ref, right_ref, out_ref):
    out_ref[...] = rows_dot(left_ref[...], right_ref[...]).astype(out_ref.dtype)


def columns_sum_kernel(place_ref, left_ref, right_ref, came_ref, out_ref):
    found = rows_dot(left_ref[...], right_ref[...]) + came_ref[...].astype(f32)
    hidden = found.shape[1] // 2
    out_ref[:, 0, :] = found[:, :hidden]
    out_ref[:, 1, :] = found[:, hidden:]


def columns_sum(left, right, came, place):
    width, block = left.shape[1] // 2, 256
    steps = width // block
    hidden = right.shape[1] // 2
    return pl.pallas_call(
        columns_sum_kernel,
        grid_spec=pltpu.PrefetchScalarGridSpec(
            num_scalar_prefetch=1,
            grid=(steps,),
            in_specs=[
                pl.BlockSpec((left.shape[0], block), lambda i, place: (0, place[0] * steps + i)),
                pl.BlockSpec(right.shape, lambda i, place: (0, 0), pipeline_mode=pl.Buffered(1)),
                pl.BlockSpec((block, right.shape[1]), lambda i, place: (i, 0)),
            ],
            out_specs=pl.BlockSpec((block, 2, hidden), lambda i, place: (i, 0, 0)),
        ),
        out_shape=jax.ShapeDtypeStruct((width, 2, hidden), f32),
        compiler_params=pltpu.CompilerParams(vmem_limit_bytes=60 * 2**20),
    )(jnp.reshape(place, (1,)).astype(jnp.int32), left, right, came)


def columns_product(left, right, place, parts, dtype):
    width = left.shape[1] // parts
    block = 256 if width % 256 == 0 else 128
    steps = width // block
    return pl.pallas_call(
        columns_kernel,
        grid_spec=pltpu.PrefetchScalarGridSpec(
            num_scalar_prefetch=1,
            grid=(steps,),
            in_specs=[
                pl.BlockSpec((left.shape[0], block), lambda i, place: (0, place[0] * steps + i)),
                pl.BlockSpec(right.shape, lambda i, place: (0, 0), pipeline_mode=pl.Buffered(1)),
            ],
            out_specs=pl.BlockSpec((block, right.shape[1]), lambda i, place: (i, 0)),
        ),
        out_shape=jax.ShapeDtypeStruct((width, right.shape[1]), dtype),
        compiler_params=pltpu.CompilerParams(vmem_limit_bytes=56 * 2**20),
    )(jnp.reshape(place, (1,)).astype(jnp.int32), left, right)


def shards(
    tokens,
    attn_gain,
    kv_gain,
    ffn_gain,
    q_weight,
    kv_down_weight,
    kv_up_weight,
    out_weight,
    shared_gate_up,
    shared_down,
    expert_gate_up,
    expert_down,
    routes,
    gates,
    lengths,
    out_grad,
):
    row_count, width = tokens.shape
    dp_count = lax.axis_size("dp")
    expert_count = lax.axis_size("expert")
    core = lax.axis_index("dp")
    me = lax.axis_index("expert")
    scale_factor = (DH + DR) ** (-0.5)
    slice_rows = kv_down_weight.shape[0]
    joint_width = KVR + DR
    n_gain, n_kv_gain = attn_gain.shape[0], kv_gain.shape[0]

    bits = bits_of(expert_count)
    head_step = expert_count * dp_count // H
    pair_bit = max(4, head_step)
    rest = [bit for bit in bits if bit != pair_bit]
    head_low = pair_bit // head_step
    head_high = H // (dp_count * 2 * head_low)
    heads = head_high * head_low
    blocks = 2 * dp_count
    pair_rows = blocks * row_count

    far, second, first = rest
    orders = whole_orders(bits, pair_bit)
    parts = thirds(width)

    def column_parts(values):
        return [values[..., low:high] for low, high in parts]

    combined = jnp.sum(
        jnp.where(
            routes[:, :, None] == jnp.arange(expert_count, dtype=jnp.int32),
            gates[:, :, None],
            0.0,
        ),
        axis=1,
    ).T
    gates_high = lax.reduce_precision(combined, 8, 7)
    gates_low = (combined - gates_high).astype(bf16)
    gates_both = jnp.stack([gates_high.astype(bf16), gates_low], axis=1)
    gate_cols = 4 * row_count
    gates_both = gates_both.reshape(-1, gate_cols)
    gate_rows = gates_both.shape[0]
    gates_both = jnp.pad(gates_both, ((0, 0), (0, joint_width - gate_cols)))
    gains = jnp.concatenate([attn_gain, ffn_gain, kv_gain, lengths[0].astype(bf16)])
    gains = jnp.pad(gains, (0, joint_width - gains.shape[0]))[None]
    gain_row = slice_rows + gate_rows
    spare = -(gain_row + 1) % 16
    small = jnp.concatenate(
        [kv_down_weight, gates_both, jnp.pad(gains, ((0, spare), (0, 0)))], axis=0
    )

    def turned(values):
        split = values.reshape(values.shape[0], dp_count, expert_count, slice_rows)
        return split.transpose(0, 2, 1, 3).reshape(values.shape)

    def turned_back(values):
        split = values.reshape(values.shape[0], expert_count, dp_count, slice_rows)
        return split.transpose(0, 2, 1, 3).reshape(values.shape)

    q_cols = heads * (DH + DR)
    up_cols = heads * (DH + DV) * n_kv_gain // slice_rows
    head_cols = q_cols + up_cols
    head_rows = dp_count * slice_rows

    def by_pair(weight, head_width, *cuts):
        split = weight.reshape(-1, dp_count, head_high, 2, head_low, head_width)
        split = split.transpose(1, 3, 0, 2, 4, 5)
        lead = (dp_count, 2, weight.shape[0], -1)
        return [part.reshape(lead) for part in jnp.split(split, cuts, axis=-1)]

    pieces = slice_rows // n_kv_gain

    def in_pieces(found):
        found = found.reshape(found.shape[:-2] + (n_kv_gain, pieces, -1))
        return jnp.swapaxes(found, -3, -2).reshape(found.shape[:-3] + (slice_rows, -1))

    def of_pieces(found):
        found = found.reshape(found.shape[:-2] + (pieces, n_kv_gain, -1))
        return jnp.swapaxes(found, -3, -2).reshape(found.shape[:-3] + (n_kv_gain, -1))

    by_head = dp_swap(
        jnp.concatenate(
            by_pair(q_weight, DH + DR, DH, DH + DR // 2)
            + [in_pieces(part) for part in by_pair(kv_up_weight, DH + DV)],
            axis=-1,
        )
    )
    nope_cols = heads * DH
    rope_cols = heads * DR // 2

    def spread(columns):
        if rope_cols == ROPE_LANES:
            return columns
        parts = jnp.split(columns[:, :q_cols], (nope_cols, nope_cols + rope_cols), axis=-1)
        room = ((0, 0), (0, ROPE_LANES - rope_cols))
        return jnp.concatenate([parts[0], jnp.pad(parts[1], room), jnp.pad(parts[2], room)], axis=-1)

    def unspread(columns):
        if rope_cols == ROPE_LANES:
            return columns
        parts = jnp.split(columns, (nope_cols, nope_cols + ROPE_LANES), axis=-1)
        return jnp.concatenate([parts[0], parts[1][:, :rope_cols], parts[2][:, :rope_cols]], axis=-1)

    out_cut = out_weight.reshape(slice_rows, -1, 2, head_cols).transpose(2, 1, 0, 3)
    out_cut = out_cut.reshape(2, -1, head_cols)
    head_cut = head_rows * 3 // 8
    out_mid = out_cut.shape[1] // 2

    share = shared_down.shape[0]
    units = dp_count * share
    padded = -(-units // 128) * 128

    def shared_by_unit(results, found, weight):
        split = weight.reshape(slice_rows, 2, dp_count, expert_count, share)
        split = split.transpose(3, 0, 1, 2, 4).reshape(expert_count, slice_rows, 2, units)
        split = jnp.pad(split, ((0, 0), (0, 0), (0, 0), (0, padded - units)))
        return split.reshape(expert_count, slice_rows, 2 * padded)

    pair_w = lax.all_gather(expert_gate_up[0].reshape(width // dp_count, -1), "dp", tiled=True)
    down_w = lax.all_gather(expert_down[0], "dp", tiled=True)
    def shared_weights(split, shared_down):
        split = lax.all_to_all(split, "expert", split_axis=0, concat_axis=0, tiled=True)
        down = dp_gather(shared_down).reshape(units, width)
        down = jnp.pad(down, ((0, padded - units), (0, 0)))
        return dp_gather(split).reshape(width, 2 * padded), down

    def attend(all_rows, small_all, by_head, out_parts):
        joint_all = dp_gather(small_all[:, :slice_rows])
        kv_down = joint_all.transpose(1, 0, 2, 3).reshape(width, joint_width)
        gains_all = dp_gather(small_all[:, gain_row])
        attn_scale = gains_all[..., :n_gain].transpose(1, 0, 2).reshape(-1)
        ffn_scale = gains_all[..., n_gain : 2 * n_gain].reshape(-1)
        n_gains = 2 * n_gain + n_kv_gain
        kv_scale = gains_all[..., 2 * n_gain : n_gains].reshape(-1)
        all_lengths = gains_all[..., n_gains : n_gains + lengths.shape[1]].astype(jnp.int32)
        low = me & ~pair_bit
        all_lengths = jnp.stack([pick(all_lengths, low, 1), pick(all_lengths, low | pair_bit, 1)])
        all_lengths = all_lengths.reshape(blocks, -1)
        doc_ids, offsets = jax.vmap(lambda row: layout(row, row_count))(all_lengths)
        cos, sin = [table.reshape(pair_rows, DR // 2) for table in angles(offsets, DR)]
        all_rows = dp_gather(all_rows).transpose(1, 0, 2, 3).reshape(pair_rows, width)
        if dp_count == 2:
            last = (first, second, far, first)
            places = jnp.stack([((me & bit) != 0).astype(jnp.int32) for bit in last])
            q_full, kv_up, out_full = whole_call(
                functools.partial(
                    assemble_kernel,
                    (
                        [bit.bit_length() - 1 for bit in last],
                        pair_bit.bit_length() - 1,
                        slice_rows,
                        pieces,
                    ),
                ),
                [part for both in by_head + out_parts for part in both],
                (
                    ((width, q_cols), bf16),
                    ((KVR, heads * (DH + DV)), bf16),
                    ((heads * DV, width), bf16),
                ),
                scalars=(places,),
            )
        else:
            by_head = jnp.concatenate(by_head, axis=1)
            q_full = spread(by_head.reshape(width, head_cols))
            kv_up = by_head[..., q_cols:].reshape(expert_count, dp_count, slice_rows, -1)
            kv_up = of_pieces(kv_up).transpose(1, 0, 2, 3).reshape(KVR, heads * (DH + DV))
            out_full = jnp.concatenate(out_parts, axis=1)
            at = bits.index(pair_bit)
            out_full = out_full.reshape((2,) * len(bits) + (-1, slice_rows, head_cols))
            out_full = jnp.moveaxis(out_full, (len(bits), at), (-3, -2)).reshape(heads * DV, width)
        wide = nope_cols + 2 * ROPE_LANES
        outs = by_rows_call(
            functools.partial(attend_kernel, heads),
            pair_rows // (4 * row_count),
            ("x", "gain", "kv_gain", "down", "q", "up", "out", "cos", "sin", "column", "row"),
            dict(
                x=all_rows,
                cos=cos,
                sin=sin,
                column=doc_ids.reshape(pair_rows, 1),
                row=doc_ids.reshape(blocks, 1, row_count),
            ),
            dict(
                gain=attn_scale.astype(f32)[None],
                kv_gain=kv_scale.astype(f32)[None],
                down=kv_down,
                q=q_full,
                up=kv_up,
                out=out_full,
            ),
            (
                ("normed", (pair_rows, width), bf16),
                ("joint", (pair_rows, joint_width), f32),
                ("kv_normed", (pair_rows, KVR), bf16),
                ("heads", (pair_rows, wide), bf16),
                ("keys", (pair_rows, wide), bf16),
                ("values", (pair_rows, heads * DV), bf16),
                ("probs", (blocks * heads, row_count, row_count), f32),
                ("attended", (pair_rows, heads * DV), bf16),
                ("sum", (pair_rows, width), bf16),
            ),
        )
        return outs, (q_full, kv_up, out_full, kv_down), (attn_scale, kv_scale, ffn_scale), (cos, sin)

    def cut_out(found):
        at = bits.index(pair_bit)
        found = found.reshape((2,) * len(rest) + (slice_rows, -1, 2, head_cols))
        found = jnp.moveaxis(found, (-3, -2), (len(bits), at))
        return found.reshape(expert_count, -1, head_cols)

    def by_owner(found):
        found = found.reshape(2, dp_count, row_count, -1).transpose(1, 0, 2, 3)
        return dp_scatter(found, bf16).astype(bf16)

    (all_rows, by_head, small), (shared_split,) = march(
        gathering(turned(tokens), [pair_bit]),
        pair_swapping(by_head, pair_bit, 1),
        gathering(small, [far]),
        jobs=((shared_by_unit, shared_gate_up),),
    )
    by_head = by_head.reshape(2, head_rows, head_cols)
    held_grad = []
    results, found = march(
        *(
            gathering(part, order, [pair_bit], whole=dp_count != 2)
            for part, order in (
                (by_head[:, :head_cut], (second, far, first)),
                (by_head[:, head_cut:], (far, first, second)),
                (out_cut[:, :out_mid], (second, first, far)),
                (out_cut[:, out_mid:], (far, second, first)),
            )
        ),
        gathering(small, (first, second, pair_bit), [far]),
        jobs=((skip,), (skip,), (lambda results, found, part: held_grad.append(part), out_grad)),
    )

    grad_all = lax.all_gather(held_grad[0], "expert")
    outs, weights, scales, tables = attend(all_rows, results[4], results[:2], results[2:4])
    normed, joint, kv_normed, query_parts, key_parts, values, probs, attended, attended_sum = outs
    q_full, kv_up, out_full, kv_down = weights
    attn_scale, kv_scale, ffn_scale = scales
    attended_sum = by_owner(attended_sum)
    shared_w, shared_out = shared_weights(shared_split, shared_down)
    hidden = down_w.shape[0]
    gates_all = results[4][:, slice_rows:gain_row, :gate_cols]
    gates_all = gates_all.reshape(expert_count, expert_count, 2, row_count)
    own_gate = pick(gates_all, me, 1).astype(f32).sum(axis=1)

    capacity = min(row_count, 3 * row_count * TOP // (2 * expert_count))
    slots = expert_count * capacity
    group_rows = expert_count * row_count
    grad_rows = grad_all.reshape(group_rows, width)
    live = own_gate > 0.0
    slot = jnp.cumsum(live.astype(jnp.int32), axis=1) - 1
    slot = slot + capacity * (jnp.arange(expert_count, dtype=jnp.int32) % 2)[:, None]
    slot = jnp.where(live, slot, -1).reshape(expert_count // 2, 1, 2 * row_count)
    gate = own_gate.reshape(expert_count // 2, 1, 2 * row_count)
    chunk = 4 * row_count

    steps = group_rows // chunk
    my_place = [((me & bit) != 0).astype(jnp.int32) for bit in (pair_bit, second, first)]
    my_place = jnp.stack(my_place)

    def group(i):
        return i if pair_bit == 4 else (i % 2) * (steps // 2) + i // 2

    def halves_of(name):
        return [
            (f"{name}{i}{kind}", (group_rows // 2, high - low), bf16)
            for i, (low, high) in enumerate(parts)
            for kind in ("kept", "sent")
        ]

    def from_gradient(results, found, grad_rows):
        return by_rows_call(
            functools.partial(gradient_kernel, 2 * capacity),
            steps,
            ("grad", "slot", "gate", "down", "shared"),
            dict(grad=grad_rows, slot=slot, gate=gate),
            dict(down=down_w, shared=shared_out),
            (
                ("picked", (slots, width), bf16),
                ("d_hidden", (slots, hidden), f32),
                ("d_shared", (group_rows, padded), f32),
            ),
        )

    attended_sum = alone(scattering(attended_sum, [pair_bit], [pair_bit]))
    resid_in = tokens.astype(f32)
    upstream = out_grad.astype(f32)
    resid = resid_in + attended_sum
    ffn_in = norm_apply(resid, ffn_scale).astype(bf16)

    ffn_parts, ((slot_grad, d_hidden, d_shared_hidden), *unused) = march(
        *(gathering(part, order, whole=False) for part, order in zip(column_parts(ffn_in), orders)),
        jobs=((from_gradient, grad_rows),),
    )
    names = [f"in{i}{kind}" for i in range(3) for kind in ("held", "came")]
    ffn_parts = [part.reshape(group_rows // 2, -1) for both in ffn_parts for part in both]
    ffn_rows, rows, expert_hidden, d_pair, shared_hidden, d_shared_pair, *d_parts = by_rows_call(
        functools.partial(expert_kernel, 2 * capacity),
        steps,
        ["slot", "d_hidden", "d_shared", "pair", "shared"] + names,
        dict(zip(names, ffn_parts), slot=slot, d_hidden=d_hidden, d_shared=d_shared_hidden),
        dict(pair=pair_w, shared=shared_w),
        [
            ("x", (group_rows, width), bf16),
            ("rows", (slots, width), bf16),
            ("hidden", (slots, hidden), bf16),
            ("d_pair", (slots, 2 * hidden), bf16),
            ("shared_hidden", (group_rows, padded), bf16),
            ("d_shared_pair", (group_rows, 2 * padded), bf16),
        ]
        + halves_of("out"),
        group=group,
        scalars=(my_place,),
        half=("in0held", "in0came", "out0kept", "out0sent"),
    )
    d_parts = [(d_parts[2 * i], d_parts[2 * i + 1]) for i in range(3)]

    def output_part(results, found, expert_hidden, shared_hidden):
        return by_rows_call(
            functools.partial(output_kernel, 2 * capacity),
            steps,
            ("hidden", "shared_hidden", "slot", "gate", "down", "shared"),
            dict(hidden=expert_hidden, shared_hidden=shared_hidden, slot=slot, gate=gate),
            dict(down=down_w, shared=shared_out),
            halves_of("out"),
            scratch=[pltpu.VMEM((slots // steps, width), bf16)],
            group=group,
            scalars=(my_place,),
            half=("out0kept", "out0sent"),
        )

    def halves(found):
        if dp_count != 2:
            return lax.psum_scatter(found.astype(bf16), "dp", scatter_dimension=0), ()
        return pick(found, core, 0), pick(found, 1 - core, 0).astype(bf16)

    def exchanged(kept, sent):
        if dp_count != 2:
            return kept.astype(f32)
        return kept + lax.ppermute(sent, "dp", [(0, 1), (1, 0)]).astype(f32)

    def pair_sent(results, found, rows, d_pair, expert_hidden, shared_hidden):
        out_part = output_part(results, found, expert_hidden, shared_hidden)
        if dp_count != 2:
            return (), out_part
        return columns_product(rows, d_pair, 1 - core, dp_count, bf16), out_part

    def pair_kept(results, found, rows, d_pair):
        if dp_count != 2:
            whole = dot(rows.T, d_pair).astype(bf16).reshape(dp_count, width // dp_count, -1)
            whole = lax.psum_scatter(whole, "dp", scatter_dimension=0).astype(f32)
            return whole.reshape(-1, 2, hidden)
        came = lax.ppermute(found[0][0], "dp", [(0, 1), (1, 0)])
        return columns_sum(rows, d_pair, came, core)

    def down_gradient(results, found, expert_hidden, slot_grad):
        return halves(
            dot(expert_hidden.T, slot_grad).reshape(dp_count, hidden // dp_count, width)
        )

    def shared_gradient(results, found, shared_hidden, d_shared_pair):
        down = columns_product(shared_hidden, grad_rows, jnp.int32(0), 1, f32)
        down = down[:units].reshape(dp_count, share, width)
        both = columns_product(ffn_rows, d_shared_pair, jnp.int32(0), 1, bf16)
        both = both.reshape(dp_count, expert_count, slice_rows, 2 * padded)
        return dp_scatter(down, bf16), dp_scatter(both, bf16).astype(bf16)

    d_sums, found = march(
        *(scattering(part, order[::-1], bits) for part, order in zip(d_parts, orders)),
        jobs=(
            (pair_sent, rows, d_pair, expert_hidden, shared_hidden),
            (pair_kept, rows, d_pair),
        ),
    )
    (unused, out_part), grad_pair, *unused = found
    d_ffn_in = jnp.concatenate(d_sums, axis=-1)

    d_norm_resid, grad_ffn_scale = norm_back(resid, ffn_scale, d_ffn_in)
    d_resid = upstream + d_norm_resid
    out_part = [(out_part[2 * i], out_part[2 * i + 1]) for i in range(3)]

    def attend_back(results, found, d_branch):
        d_branch = dp_gather(d_branch).transpose(1, 0, 2, 3).reshape(pair_rows, width)
        steps = pair_rows // (4 * row_count)
        wide = nope_cols + 2 * ROPE_LANES
        outs = by_rows_call(
            functools.partial(attend_back_kernel, heads),
            steps,
            (
                "branch", "out", "probs", "heads", "keys", "values", "joint", "kv_gain", "up", "q",
                "down", "cos", "sin",
            ),
            dict(
                branch=d_branch,
                probs=probs,
                heads=query_parts,
                keys=key_parts,
                values=values,
                joint=joint,
                cos=tables[0],
                sin=tables[1],
            ),
            dict(
                out=out_full,
                kv_gain=kv_scale.astype(f32)[None],
                up=kv_up,
                q=q_full,
                down=kv_down,
            ),
            (
                ("d_q", (pair_rows, wide), bf16),
                ("d_kv", (pair_rows, heads * (DH + DV)), bf16),
                ("d_joint", (pair_rows, joint_width), bf16),
                ("d_gain", (steps, 1, KVR), f32),
                ("sum", (pair_rows, width), bf16),
            ),
            scratch=[pltpu.VMEM((4 * row_count, DR), f32)],
        )
        return d_branch, outs

    def weight_gradients(results, found):
        d_branch, (d_q_heads, d_kv_heads, d_joint, unused, unused) = found[0]
        if dp_count == 2:
            *parts, grad_kvdown = whole_call(
                functools.partial(
                    attention_gradients_kernel, (pair_bit.bit_length() - 1, slice_rows, pieces)
                ),
                (normed, d_q_heads, kv_normed, d_kv_heads, attended, d_branch, d_joint),
                (
                    ((expert_count, head_cut, head_cols), bf16),
                    ((expert_count, head_rows - head_cut, head_cols), bf16),
                    ((expert_count, out_mid, head_cols), bf16),
                    ((expert_count, slice_rows - out_mid, head_cols), bf16),
                    ((dp_count, expert_count, slice_rows, joint_width), bf16),
                ),
            )
            return *parts, dp_scatter(grad_kvdown, bf16)
        grad_q = unspread(dot(normed.T, d_q_heads)).astype(bf16)
        grad_q = grad_q.reshape(expert_count, head_rows, q_cols)
        grad_up = dot(kv_normed.T, d_kv_heads).astype(bf16)
        grad_up = grad_up.reshape(dp_count, expert_count, n_kv_gain, -1).transpose(1, 0, 2, 3)
        grad_up = in_pieces(grad_up).reshape(expert_count, head_rows, up_cols)
        by_head = jnp.concatenate([grad_q, grad_up], axis=-1)
        grad_out = cut_out(dot(attended.T, d_branch).astype(bf16))
        grad_kvdown = dot(normed.T, d_joint)
        grad_kvdown = grad_kvdown.reshape(expert_count, dp_count, slice_rows, joint_width)
        parts = (
            by_head[:, :head_cut], by_head[:, head_cut:], grad_out[:, :out_mid], grad_out[:, out_mid:]
        )
        return *parts, dp_scatter(grad_kvdown.transpose(1, 0, 2, 3), bf16)

    sums = []

    def back_of(results, found):
        return attend_back(results, found, results[0])

    def sum_and_gradients(results, found):
        sums.append(by_owner(found[1][1][4]))
        return weight_gradients(results, found[1:])

    (unused, d_normed, *results), found = march(
        gathering(d_resid.astype(bf16), [pair_bit]),
        deferred(3, lambda: scattering(sums[0], [pair_bit], [pair_bit])),
        *(
            scattering(after(part, d_resid), order[::-1], bits)
            for part, order in zip(out_part, orders)
        ),
        jobs=(
            (skip,),
            (back_of,),
            (sum_and_gradients,),
            (shared_gradient, shared_hidden, d_shared_pair),
        ),
    )
    *grad_parts, grad_kvdown = found[2]
    grad_shared_out, grad_shared = found[3]
    output = (resid + jnp.concatenate(results, axis=-1)).astype(bf16)
    grad_kv_scale = found[1][1][3].sum(axis=0)
    d_norm_in, grad_attn_scale = norm_back(turned(resid_in), attn_scale, d_normed)
    grad_in = (d_resid + turned_back(d_norm_in)).astype(bf16)
    scale_sums = jnp.concatenate(
        [
            grad_attn_scale.reshape(expert_count, dp_count, n_gain).transpose(1, 0, 2),
            grad_ffn_scale.reshape(dp_count, expert_count, n_gain),
            grad_kv_scale.reshape(dp_count, expert_count, n_kv_gain),
        ],
        axis=-1,
    )
    scale_sums = jnp.pad(scale_sums, ((0, 0), (0, 0), (0, joint_width - scale_sums.shape[-1])))
    scale_sums = dp_scatter(scale_sums)[:, None]
    small_sums = jnp.concatenate([grad_kvdown, scale_sums], axis=1).astype(bf16)

    def start_down(results, found, expert_hidden, slot_grad, shared):
        shared = lax.all_to_all(shared, "expert", split_axis=0, concat_axis=0, tiled=True)
        return down_gradient(results, found, expert_hidden, slot_grad), shared

    def finish_down(results, found):
        return exchanged(*found[0][0]).reshape(expert_down.shape)

    def finish_shared(results, found):
        both = found[0][1].reshape(expert_count, slice_rows, 2, padded)[..., :units]
        both = both.reshape(expert_count, slice_rows, 2, dp_count, share)
        return both.transpose(1, 2, 3, 0, 4).reshape(shared_gate_up.shape).astype(f32)

    def whole_heads(found, rows, *widths):
        cuts = [heads * sum(widths[: i + 1]) for i in range(len(widths) - 1)]
        lead = (dp_count, 2, rows, head_high, head_low, -1)
        found = jnp.concatenate(
            [part.reshape(lead) for part in jnp.split(found, cuts, axis=-1)], axis=-1
        )
        return found.transpose(2, 0, 3, 1, 4, 5).reshape(rows, -1).astype(f32)

    summed, found = march(
        scattering(small_sums, (pair_bit, second, first, far), bits),
        *(
            scattering(part, order, bits, bf16)
            for part, order in (
                (grad_parts[0], (first, far, second)),
                (grad_parts[1], (second, first, far)),
                (grad_parts[2], (far, first, second)),
                (grad_parts[3], (first, second, far)),
            )
        ),
        jobs=(
            (start_down, *after((expert_hidden, slot_grad, grad_shared), results)),
            (finish_down,),
            (finish_shared,),
        ),
    )
    unused, grad_down, grad_shared = found[:3]
    by_head = jnp.concatenate(summed[1:3], axis=1)
    by_head = alone(pair_swapping(by_head, pair_bit, 0)).reshape(2, dp_count, slice_rows, head_cols)
    by_head = dp_swap(by_head.transpose(1, 0, 2, 3))
    grad_q = whole_heads(by_head[..., :q_cols], slice_rows, DH, DR // 2, DR // 2)
    grad_up = of_pieces(by_head[..., q_cols:])
    grad_up = whole_heads(grad_up, n_kv_gain, DH + DV)
    grad_out = jnp.concatenate(summed[3:5], axis=1).reshape(2, -1, slice_rows, head_cols)
    grad_out = grad_out.transpose(2, 1, 0, 3).reshape(out_weight.shape).astype(f32)
    small_sums = summed[0]
    grad_kvdown = small_sums[:slice_rows]
    scale_sums = small_sums[slice_rows]

    return (
        output,
        grad_in,
        scale_sums[:n_gain],
        scale_sums[2 * n_gain : 2 * n_gain + n_kv_gain],
        scale_sums[n_gain : 2 * n_gain],
        grad_q,
        grad_kvdown,
        grad_up,
        grad_out,
        grad_shared,
        grad_shared_out,
        grad_pair.reshape(expert_gate_up.shape),
        grad_down,
    )


def solution(mesh):
    rows = P(SPLIT, None)
    each = P(SPLIT)
    cube = P(SPLIT, None, None)
    pair = P("expert", "dp", None, None)
    down = P("expert", "dp", None)
    dense = (rows, rows, rows, rows, cube, rows)
    return jax.shard_map(
        shards,
        mesh=mesh,
        in_specs=(rows, each, each, each) + dense + (pair, down, rows, rows, rows, rows),
        out_specs=(rows, rows, each, each, each) + dense + (pair, down),
        check_vma=False,
    )
```

```python
import functools

import jax
import jax.numpy as jnp
from jax import lax
from jax.experimental import pallas as pl
from jax.experimental.pallas import tpu as pltpu
from jax.sharding import PartitionSpec as P

H = 16
DH = 128
DR = 64
DV = 128
KVR = 512
TOP = 6
SPLIT = ("dp", "expert")
ROPE_LANES = 128

f32 = jnp.float32
bf16 = jnp.bfloat16

norm_eps = 1e-06
rope_base = 50000.0
masked_score = -1e30


def norm_apply(values, scales):
    return values * lax.rsqrt(jnp.mean(values * values, axis=-1, keepdims=True) + norm_eps) * scales


def norm_back(values, scales, upstream):
    unused, pullback = jax.vjp(norm_apply, values, scales.astype(f32))
    return pullback(upstream)


def rotate(values, cosine_table, sine_table):
    half_width = values.shape[-1] // 2
    front_half = values[..., :half_width]
    back_half = values[..., half_width:]
    return jnp.concatenate(
        [
            front_half * cosine_table - back_half * sine_table,
            front_half * sine_table + back_half * cosine_table,
        ],
        axis=-1,
    )


def swish_gate(gate_part, up_part):
    return gate_part * jax.nn.sigmoid(gate_part) * up_part


def swish_back(gate_part, up_part, upstream):
    unused, pullback = jax.vjp(swish_gate, gate_part, up_part)
    return jnp.concatenate(pullback(upstream), axis=-1)


def layout(lengths_row, row_count):
    doc_ends = jnp.cumsum(lengths_row)
    places = jnp.arange(row_count, dtype=jnp.int32)
    passed_end = (places[:, None] >= doc_ends[None, :]).astype(jnp.int32)
    doc_ids = jnp.sum(passed_end, axis=1)
    starts = jnp.sum(passed_end * lengths_row[None, :], axis=1)
    return (doc_ids, places - starts)


def angles(offsets, rope_width):
    frequency = rope_base ** (-2.0 * jnp.arange(rope_width // 2, dtype=f32) / rope_width)
    turned = offsets.astype(f32)[..., None] * frequency
    return (jnp.cos(turned), jnp.sin(turned))


def dot(left, right):
    return jnp.dot(left, right, preferred_element_type=f32)


def pick(values, place, axis):
    return lax.dynamic_index_in_dim(values, place, axis, keepdims=False)


def dp_gather(values):
    if lax.axis_size("dp") != 2:
        return lax.all_gather(values, "dp")
    other = lax.ppermute(values, "dp", [(0, 1), (1, 0)])
    first = lax.axis_index("dp") == 0
    return jnp.stack([jnp.where(first, values, other), jnp.where(first, other, values)])


def dp_swap(values):
    if lax.axis_size("dp") != 2:
        return lax.all_to_all(values, "dp", split_axis=0, concat_axis=0)
    core = lax.axis_index("dp")
    own = pick(values, core, 0)
    other = lax.ppermute(pick(values, 1 - core, 0), "dp", [(0, 1), (1, 0)])
    first = core == 0
    return jnp.stack([jnp.where(first, own, other), jnp.where(first, other, own)])


def dp_scatter(values, sent=f32):
    if lax.axis_size("dp") != 2:
        return lax.psum_scatter(values.astype(sent), "dp", scatter_dimension=0).astype(f32)
    core = lax.axis_index("dp")
    other = lax.ppermute(pick(values, 1 - core, 0).astype(sent), "dp", [(0, 1), (1, 0)])
    return pick(values, core, 0).astype(f32) + other.astype(f32)


def dp_sum(values):
    if lax.axis_size("dp") != 2:
        return lax.psum(values, "dp")
    return values + lax.ppermute(values, "dp", [(0, 1), (1, 0)])


def bits_of(count):
    return [1 << place for place in reversed(range(count.bit_length() - 1))]


def partner(values, bit):
    count = lax.axis_size("expert")
    return lax.ppermute(values, "expert", [(i, i ^ bit) for i in range(count)])


def gathering(values, order, held=(), lead=0, whole=True):
    me = lax.axis_index("expert")
    held = list(held)
    for step, bit in enumerate(order):
        if not whole and step + 1 == len(order):
            values = values.reshape((-1,) + values.shape[lead + len(held) :])
            if values.shape[1] % 128 == 0:
                values = values.reshape(-1, values.shape[-1])
            return values, (yield partner(values, bit))
        other = yield partner(values, bit)
        low = (me & bit) == 0
        values = jnp.stack(
            [jnp.where(low, values, other), jnp.where(low, other, values)],
            axis=lead + sum(1 for known in held if known > bit),
        )
        held.append(bit)
    return values.reshape(values.shape[:lead] + (-1,) + values.shape[lead + len(held) :])


def scattering(values, order, bits, kept=f32, lead=0):
    me = lax.axis_index("expert")
    bits = list(bits)
    split = isinstance(values, tuple)
    if not split:
        values = values.reshape(values.shape[:lead] + (2,) * len(bits) + values.shape[lead + 1 :])
    for step, bit in enumerate(order):
        axis = lead + bits.index(bit)
        bits.remove(bit)
        place = ((me & bit) != 0).astype(jnp.int32)
        if split and step == 0:
            own, sent = values
        else:
            own, sent = pick(values, place, axis), pick(values, 1 - place, axis)
        other = yield partner(sent, bit)
        if step + 1 < len(order):
            values = own + other
        else:
            values = (own.astype(f32) + other.astype(f32)).astype(kept)
        if split and step == 0:
            values = values.reshape((2,) * len(bits) + (-1,) + values.shape[-1:])
    if bits:
        values = values.reshape(values.shape[:lead] + (-1,) + values.shape[lead + len(bits) :])
    return values


def later(steps, values, chain):
    for _ in range(steps):
        values = yield values
    return (yield from chain(values))


def begun(chain, values):
    while True:
        try:
            values = chain.send(values)
        except StopIteration as stop:
            return stop.value
        values = yield values


def last_of(chain, values):
    try:
        chain.send(values)
    except StopIteration as stop:
        return stop.value


def deferred(steps, make):
    for _ in range(steps):
        yield ()
    return (yield from make())


def pair_swapping(values, bit, axis):
    place = ((lax.axis_index("expert") & bit) != 0).astype(jnp.int32)
    own = pick(values, place, axis)
    other = yield partner(pick(values, 1 - place, axis), bit)
    low = place == 0
    return jnp.stack([jnp.where(low, own, other), jnp.where(low, other, own)])


def march(*chains, jobs=()):
    results, found = [None] * len(chains), []
    live = {i: next(chain) for i, chain in enumerate(chains)}
    waiting = [operands for _, *operands in jobs]
    while live or len(found) < len(jobs):
        step = len(found)
        job = jobs[step][0](results, found, *waiting[step]) if step < len(jobs) else ()
        live, job, waiting = lax.optimization_barrier((live, job, waiting[step + 1 :]))
        waiting = [()] * (step + 1) + waiting
        found.append(job)
        following = {}
        for i, values in live.items():
            try:
                following[i] = chains[i].send(values)
            except StopIteration as stop:
                results[i] = stop.value
        live = following
    return results, found


def skip(results, found):
    return ()


def alone(chain, *markers):
    values = next(chain)
    step = 0
    while True:
        if step < len(markers):
            values = after(values, markers[step])
        step += 1
        try:
            values = chain.send(values)
        except StopIteration as stop:
            return stop.value


def after(values, *others):
    return lax.optimization_barrier((values, others))[0]


def thirds(width):
    side = width // 128 // 3 * 128
    return (0, side), (side, width - side), (width - side, width)


def whole_orders(bits, pair_bit):
    far, second, first = [bit for bit in bits if bit != pair_bit]
    return (
        (second, far, first, pair_bit),
        (far, first, pair_bit, second),
        (far, pair_bit, second, first),
    )


def lanes_dot(left, right):
    return lax.dot_general(left, right, (((1,), (1,)), ((), ())), preferred_element_type=f32)


def rows_dot(left, right):
    return lax.dot_general(left, right, (((0,), (0,)), ((), ())), preferred_element_type=f32)


def head_lanes(heads):
    lane = lax.broadcasted_iota(jnp.int32, (1, ROPE_LANES), 1) // (DR // 2)
    return [(lane == head).astype(f32) for head in range(heads)]


def attend_kernel(
    heads,
    x_ref,
    gain_ref,
    kv_gain_ref,
    down_ref,
    q_ref,
    up_ref,
    out_ref,
    cos_ref,
    sin_ref,
    column_ref,
    row_ref,
    normed_ref,
    joint_ref,
    kv_normed_ref,
    heads_ref,
    keys_ref,
    values_ref,
    probs_ref,
    attended_ref,
    sum_ref,
):
    nope = heads * DH
    rows = x_ref.shape[0]
    x = x_ref[...].astype(f32)
    scale = lax.rsqrt(jnp.mean(x * x, axis=-1, keepdims=True) + norm_eps)
    normed_ref[...] = (x * scale * gain_ref[...]).astype(bf16)
    joint_ref[...] = dot(normed_ref[...], down_ref[...])
    latent = joint_ref[:, :KVR]
    scale = lax.rsqrt(jnp.mean(latent * latent, axis=-1, keepdims=True) + norm_eps)
    kv_normed_ref[...] = (latent * scale * kv_gain_ref[...]).astype(bf16)
    copies = 2 * ROPE_LANES // DR
    cos, sin = [jnp.concatenate([ref[...]] * copies, axis=-1) for ref in (cos_ref, sin_ref)]
    front = jnp.concatenate([joint_ref[:, KVR : KVR + DR // 2]] * copies, axis=-1)
    back = jnp.concatenate([joint_ref[:, KVR + DR // 2 :]] * copies, axis=-1)
    keys_ref[:, nope : nope + ROPE_LANES] = (front * cos - back * sin).astype(bf16)
    keys_ref[:, nope + ROPE_LANES :] = (front * sin + back * cos).astype(bf16)
    q = dot(normed_ref[...], q_ref[:, : nope + 2 * ROPE_LANES])
    front = q[:, nope : nope + ROPE_LANES]
    back = q[:, nope + ROPE_LANES :]
    heads_ref[:, :nope] = q[:, :nope].astype(bf16)
    heads_ref[:, nope : nope + ROPE_LANES] = (front * cos - back * sin).astype(bf16)
    heads_ref[:, nope + ROPE_LANES :] = (front * sin + back * cos).astype(bf16)
    kv = dot(kv_normed_ref[...], up_ref[...])
    for head in range(heads):
        start = head * (DH + DV)
        keys_ref[:, head * DH : (head + 1) * DH] = kv[:, start : start + DH].astype(bf16)
        values_ref[:, head * DV : (head + 1) * DV] = kv[:, start + DH : start + DH + DV].astype(bf16)
    tile = probs_ref.shape[-1]
    causal = lax.broadcasted_iota(jnp.int32, (tile, tile), 0) >= lax.broadcasted_iota(
        jnp.int32, (tile, tile), 1
    )
    own = head_lanes(heads)
    for block in range(rows // tile):
        part = pl.ds(block * tile, tile)
        allowed = (column_ref[part, :] == row_ref[block]) & causal
        rotary = heads_ref[part, nope:].astype(f32)
        for head in range(heads):
            both = jnp.concatenate([own[head], own[head]], axis=-1)
            scores = lanes_dot(
                heads_ref[part, head * DH : (head + 1) * DH],
                keys_ref[part, head * DH : (head + 1) * DH],
            ) + lanes_dot((rotary * both).astype(bf16), keys_ref[part, nope:])
            scores = jnp.where(allowed, scores * (DH + DR) ** (-0.5), masked_score)
            weights = jnp.exp(scores - jnp.max(scores, axis=-1, keepdims=True))
            probs = weights / jnp.sum(weights, axis=-1, keepdims=True)
            probs_ref[block * heads + head] = probs
            attended_ref[part, head * DV : (head + 1) * DV] = dot(
                probs.astype(bf16), values_ref[part, head * DV : (head + 1) * DV]
            ).astype(bf16)
    sum_ref[...] = dot(attended_ref[...], out_ref[...]).astype(sum_ref.dtype)


def attend_back_kernel(
    heads,
    x_ref,
    branch_ref,
    out_ref,
    probs_ref,
    heads_ref,
    keys_ref,
    values_ref,
    joint_ref,
    kv_gain_ref,
    up_ref,
    q_ref,
    down_ref,
    cos_ref,
    sin_ref,
    d_q_ref,
    d_kv_ref,
    d_joint_ref,
    d_gain_ref,
    d_first_gain_ref,
    sum_ref,
    d_key_ref,
):
    nope = heads * DH
    rows = branch_ref.shape[0]
    tile = probs_ref.shape[-1]
    factor = (DH + DR) ** (-0.5)
    d_attended = lanes_dot(branch_ref[...], out_ref[...]).astype(bf16)
    own = head_lanes(heads)
    for block in range(rows // tile):
        part = slice(block * tile, (block + 1) * tile)
        rotary = heads_ref[part, nope:].astype(f32)
        d_rotary = jnp.zeros((tile, 2 * ROPE_LANES), f32)
        d_key = jnp.zeros((tile, 2 * ROPE_LANES), f32)
        for head in range(heads):
            both = jnp.concatenate([own[head], own[head]], axis=-1)
            columns = slice(head * DH, (head + 1) * DH)
            start = head * (DH + DV)
            upstream = d_attended[part, head * DV : (head + 1) * DV]
            probs = probs_ref[block * heads + head]
            d_kv_ref[part, start + DH : start + DH + DV] = rows_dot(
                probs.astype(bf16), upstream
            ).astype(bf16)
            d_probs = lanes_dot(upstream, values_ref[part, head * DV : (head + 1) * DV])
            d_scores = probs * (d_probs - jnp.sum(d_probs * probs, axis=-1, keepdims=True))
            d_scores = d_scores.astype(bf16)
            d_q_ref[part, columns] = (dot(d_scores, keys_ref[part, columns]) * factor).astype(bf16)
            d_rotary = d_rotary + dot(d_scores, keys_ref[part, nope:]) * (factor * both)
            d_kv_ref[part, start : start + DH] = (
                rows_dot(d_scores, heads_ref[part, columns]) * factor
            ).astype(bf16)
            d_key = d_key + rows_dot(d_scores, (rotary * both).astype(bf16)) * factor
        narrow = cos_ref[part, :], sin_ref[part, :]
        cos, sin = [jnp.concatenate([table] * (2 * ROPE_LANES // DR), axis=-1) for table in narrow]
        front, back = d_rotary[:, :ROPE_LANES], d_rotary[:, ROPE_LANES:]
        d_q_ref[part, nope : nope + ROPE_LANES] = (front * cos + back * sin).astype(bf16)
        d_q_ref[part, nope + ROPE_LANES :] = (back * cos - front * sin).astype(bf16)
        front, back = [
            sum(half[:, at : at + DR // 2] for at in range(0, ROPE_LANES, DR // 2))
            for half in (d_key[:, :ROPE_LANES], d_key[:, ROPE_LANES:])
        ]
        cos, sin = narrow
        d_key_ref[part, : DR // 2] = front * cos + back * sin
        d_key_ref[part, DR // 2 :] = back * cos - front * sin
    d_kv_normed = lanes_dot(d_kv_ref[...], up_ref[...])
    latent = joint_ref[:, :KVR]
    scale = lax.rsqrt(jnp.mean(latent * latent, axis=-1, keepdims=True) + norm_eps)
    d_gain_ref[0] = jnp.sum(d_kv_normed * latent * scale, axis=0, keepdims=True)
    d_kv_normed = d_kv_normed * kv_gain_ref[...]
    fall = jnp.mean(d_kv_normed * latent, axis=-1, keepdims=True) * scale * scale * scale
    d_joint_ref[:, :KVR] = (d_kv_normed * scale - latent * fall).astype(bf16)
    d_joint_ref[:, KVR:] = d_key_ref[...].astype(bf16)
    total = lanes_dot(d_q_ref[...], q_ref[:, : nope + 2 * ROPE_LANES]) + lanes_dot(
        d_joint_ref[...], down_ref[...]
    )
    sum_ref[...] = total.astype(sum_ref.dtype)
    x = x_ref[...].astype(f32)
    scale = lax.rsqrt(jnp.mean(x * x, axis=-1, keepdims=True) + norm_eps)
    d_first_gain_ref[0] = jnp.sum(total * (x * scale), axis=0, keepdims=True)


def by_rows_call(
    kernel, steps, order, streamed, fixed, outs, scratch=(), group=lambda i: i, scalars=(), half=None
):
    half = half or ()

    def spec(name, shape):
        rest = (0,) * (len(shape) - 1)
        if name in half:
            block = (shape[0] * 2 // steps,) + shape[1:]
            return pl.BlockSpec(block, lambda i, *unused: (i // 2,) + rest)
        block = (shape[0] // steps,) + shape[1:]
        return pl.BlockSpec(block, lambda i, *unused: (group(i),) + rest)

    operands, specs = [], []
    for name in order:
        if name in streamed:
            operands.append(streamed[name])
            specs.append(spec(name, streamed[name].shape))
        else:
            value = fixed[name]
            operands.append(value)
            specs.append(
                pl.BlockSpec(
                    value.shape,
                    lambda i, *unused, ndim=value.ndim: (0,) * ndim,
                    pipeline_mode=pl.Buffered(1),
                )
            )
    return pl.pallas_call(
        kernel,
        grid_spec=pltpu.PrefetchScalarGridSpec(
            num_scalar_prefetch=len(scalars),
            grid=(steps,),
            in_specs=specs,
            out_specs=[spec(name, shape) for name, shape, dtype in outs],
            scratch_shapes=scratch,
        ),
        out_shape=[jax.ShapeDtypeStruct(shape, dtype) for name, shape, dtype in outs],
        compiler_params=pltpu.CompilerParams(vmem_limit_bytes=60 * 2**20),
    )(*scalars, *operands)


def without(index, place):
    return (index >> (place + 1) << place) | (index & ((1 << place) - 1))


def assemble_kernel(shape, me_ref, *refs):
    places, pair_place, slice_rows, pieces = shape
    sources, (q_ref, up_ref, out_ref) = refs[:8], refs[8:]
    q_cols, up_cols = q_ref.shape[1], sources[0].shape[-1] - q_ref.shape[1]
    piece_rows = slice_rows // pieces
    count = 2 * sources[0].shape[0]
    start = 0
    for which, place in enumerate(places):
        held_ref, came_ref = sources[2 * which : 2 * which + 2]
        if which == 2:
            start = 0
        size = held_ref.shape[1]

        def put(mine, start=start, size=size, which=which, place=place, both=(held_ref, came_ref)):
            for e in range(count):
                source = both[(e >> place & 1) ^ mine]
                at = without(e, place)
                if which >= 2:
                    row = without(e, pair_place) * slice_rows + start
                    half = (e >> pair_place & 1) * source.shape[-1]
                    out_ref[row : row + size, half : half + source.shape[-1]] = source[at]
                    continue
                row = e * 2 * slice_rows + start
                q_ref[row : row + size, :] = source[at, :, :q_cols]
                for piece in range(start // piece_rows, (start + size) // piece_rows):
                    core, column = piece // pieces, piece % pieces
                    row = (core * count + e) * piece_rows
                    begin = piece * piece_rows - start
                    up_ref[row : row + piece_rows, column * up_cols : (column + 1) * up_cols] = (
                        source[at, begin : begin + piece_rows, q_cols:]
                    )

        pl.when(me_ref[which] == 0)(functools.partial(put, 0))
        pl.when(me_ref[which] == 1)(functools.partial(put, 1))
        start += size


def attention_gradients_kernel(
    shape,
    normed_ref,
    d_q_ref,
    kv_normed_ref,
    d_kv_ref,
    attended_ref,
    branch_ref,
    d_joint_ref,
    first_ref,
    last_ref,
    out_first_ref,
    out_last_ref,
    joint_ref,
):
    pair_place, slice_rows, pieces = shape
    count, cut, _ = first_ref.shape
    out_cut = out_first_ref.shape[1]
    q_cols, piece_rows = d_q_ref.shape[1], slice_rows // pieces
    up_cols = first_ref.shape[-1] - q_cols
    up = rows_dot(kv_normed_ref[...], d_kv_ref[...]).astype(bf16)
    for e in range(count):
        for piece in range(2 * pieces):
            core, column = piece // pieces, piece % pieces
            row = (core * count + e) * piece_rows
            found = up[row : row + piece_rows, column * up_cols : (column + 1) * up_cols]
            begin = piece * piece_rows
            if begin < cut:
                first_ref[e, begin : begin + piece_rows, q_cols:] = found
            else:
                last_ref[e, begin - cut : begin - cut + piece_rows, q_cols:] = found
    width = normed_ref.shape[1]
    per = 4
    for at in range(0, count, per):
        columns = slice(at * 2 * slice_rows, (at + per) * 2 * slice_rows)
        found = rows_dot(normed_ref[:, columns], d_q_ref[...]).astype(bf16)
        for e in range(per):
            row = e * 2 * slice_rows
            first_ref[at + e, :, :q_cols] = found[row : row + cut]
            last_ref[at + e, :, :q_cols] = found[row + cut : row + 2 * slice_rows]
        found = rows_dot(normed_ref[:, columns], d_joint_ref[...]).astype(bf16)
        for e in range(per):
            for core in range(2):
                row = (2 * e + core) * slice_rows
                joint_ref[core, at + e] = found[row : row + slice_rows]
    found = rows_dot(attended_ref[...], branch_ref[...]).astype(bf16)
    half = width // 2
    for e in range(count):
        row = without(e, pair_place) * slice_rows
        side = (e >> pair_place & 1) * half
        out_first_ref[e] = found[row : row + out_cut, side : side + half]
        out_last_ref[e] = found[row + out_cut : row + slice_rows, side : side + half]


def whole_call(kernel, operands, outs, scalars=()):
    return pl.pallas_call(
        kernel,
        grid_spec=pltpu.PrefetchScalarGridSpec(
            num_scalar_prefetch=len(scalars),
            grid=(1,),
            in_specs=[
                pl.BlockSpec(value.shape, lambda i, *unused, ndim=value.ndim: (0,) * ndim)
                for value in operands
            ],
            out_specs=[
                pl.BlockSpec(shape, lambda i, *unused, ndim=len(shape): (0,) * ndim)
                for shape, dtype in outs
            ],
        ),
        out_shape=[jax.ShapeDtypeStruct(shape, dtype) for shape, dtype in outs],
        compiler_params=pltpu.CompilerParams(vmem_limit_bytes=60 * 2**20),
    )(*scalars, *operands)


def one_hot(slot_ref, place, count):
    slots = slot_ref[place]
    return lax.broadcasted_iota(jnp.int32, (count, slots.shape[1]), 0) == slots


def swiglu_back(gate_part, up_part, upstream):
    sigmoid = jax.nn.sigmoid(gate_part)
    silu = gate_part * sigmoid
    slope = sigmoid + silu * (1.0 - sigmoid)
    return silu * up_part, upstream * up_part * slope, upstream * silu


def gradient_kernel(
    count, grad_ref, slot_ref, gate_ref, down_ref, shared_ref, picked_ref, d_hidden_ref, d_shared_ref
):
    span = slot_ref.shape[-1]
    for place in range(slot_ref.shape[0]):
        chosen = one_hot(slot_ref, place, count)
        gate = jnp.sum(jnp.where(chosen, gate_ref[place], 0.0), axis=1, keepdims=True)
        found = dot(chosen.astype(bf16), grad_ref[place * span : (place + 1) * span])
        picked_ref[place * count : (place + 1) * count] = (found * gate).astype(bf16)
    d_hidden_ref[...] = lanes_dot(picked_ref[...], down_ref[...])
    d_shared_ref[...] = lanes_dot(grad_ref[...], shared_ref[...])


def halves_in(me_ref, refs, x_ref, parts, span):
    for (start, stop), (held_ref, came_ref), mine in zip(parts, refs, my_places(me_ref)):
        if start == 0:
            here = lax.rem(pl.program_id(0), 2) == mine

            @pl.when(here)
            def _():
                x_ref[:, start:stop] = held_ref[...]

            @pl.when(jnp.logical_not(here))
            def _():
                x_ref[:, start:stop] = came_ref[...]

            continue
        size = span if start == parts[1][0] else span // 2
        for at in range(2 * span // size):
            turn, place = (at // 2, at % 2) if size < span else (0, at)
            source = slice(turn * size, (turn + 1) * size)
            x_ref[at * size : (at + 1) * size, start:stop] = jnp.where(
                mine == place, held_ref[source].astype(f32), came_ref[source].astype(f32)
            ).astype(bf16)


def halves_out(me_ref, refs, values, which, span):
    (kept_ref, sent_ref), mine = refs[which], my_places(me_ref)[which]
    if which == 0:
        here = lax.rem(pl.program_id(0), 2) == mine

        @pl.when(here)
        def _():
            kept_ref[...] = values.astype(bf16)

        @pl.when(jnp.logical_not(here))
        def _():
            sent_ref[...] = values.astype(bf16)

        return
    size = span if which == 1 else span // 2
    for turn in range(span // size):
        low = values[2 * turn * size : (2 * turn + 1) * size]
        high = values[(2 * turn + 1) * size : (2 * turn + 2) * size]
        target = slice(turn * size, (turn + 1) * size)
        kept_ref[target] = jnp.where(mine == 0, low, high).astype(bf16)
        sent_ref[target] = jnp.where(mine == 0, high, low).astype(bf16)


def my_places(me_ref):
    return me_ref[0], me_ref[1], me_ref[2]


def expert_kernel(
    count,
    me_ref,
    slot_ref,
    d_hidden_ref,
    d_shared_ref,
    pair_ref,
    shared_ref,
    left_ref,
    left_came_ref,
    middle_ref,
    middle_came_ref,
    right_ref,
    right_came_ref,
    x_ref,
    rows_ref,
    hidden_ref,
    d_pair_ref,
    shared_hidden_ref,
    d_shared_pair_ref,
    left_kept_ref,
    left_sent_ref,
    middle_kept_ref,
    middle_sent_ref,
    right_kept_ref,
    right_sent_ref,
):
    span = slot_ref.shape[-1]
    parts = thirds(x_ref.shape[-1])
    halves_in(
        me_ref,
        ((left_ref, left_came_ref), (middle_ref, middle_came_ref), (right_ref, right_came_ref)),
        x_ref,
        parts,
        span,
    )
    places = range(slot_ref.shape[0])
    chosen = [one_hot(slot_ref, place, count).astype(bf16) for place in places]
    for place in places:
        rows_ref[place * count : (place + 1) * count] = dot(
            chosen[place], x_ref[place * span : (place + 1) * span]
        ).astype(bf16)
    hidden = hidden_ref.shape[-1]
    units, d_gate, d_up = swiglu_back(
        dot(rows_ref[...], pair_ref[:, :hidden]),
        dot(rows_ref[...], pair_ref[:, hidden:]),
        d_hidden_ref[...],
    )
    hidden_ref[...] = units.astype(bf16)
    d_pair_ref[:, :hidden] = d_gate.astype(bf16)
    d_pair_ref[:, hidden:] = d_up.astype(bf16)
    padded = shared_hidden_ref.shape[-1]
    units, d_gate, d_up = swiglu_back(
        dot(x_ref[...], shared_ref[:, :padded]),
        dot(x_ref[...], shared_ref[:, padded:]),
        d_shared_ref[...],
    )
    shared_hidden_ref[...] = units.astype(bf16)
    d_shared_pair_ref[:, :padded] = d_gate.astype(bf16)
    d_shared_pair_ref[:, padded:] = d_up.astype(bf16)
    refs = (
        (left_kept_ref, left_sent_ref),
        (middle_kept_ref, middle_sent_ref),
        (right_kept_ref, right_sent_ref),
    )
    for which, (start, stop) in enumerate(parts):
        back = lanes_dot(d_pair_ref[...], pair_ref[start:stop]).astype(bf16)
        found = [
            rows_dot(chosen[place], back[place * count : (place + 1) * count])
            + lanes_dot(d_shared_pair_ref[place * span : (place + 1) * span], shared_ref[start:stop])
            for place in places
        ]
        halves_out(me_ref, refs, jnp.concatenate(found, axis=0), which, span)


def output_kernel(
    count,
    me_ref,
    hidden_ref,
    shared_hidden_ref,
    slot_ref,
    gate_ref,
    down_ref,
    shared_ref,
    left_kept_ref,
    left_sent_ref,
    middle_kept_ref,
    middle_sent_ref,
    right_kept_ref,
    right_sent_ref,
    rows_ref,
):
    span = slot_ref.shape[-1]
    places = range(slot_ref.shape[0])
    chosen = [one_hot(slot_ref, place, count) for place in places]
    found = dot(hidden_ref[...], down_ref[...])
    for place in places:
        at = slice(place * count, (place + 1) * count)
        gate = jnp.sum(jnp.where(chosen[place], gate_ref[place], 0.0), axis=1, keepdims=True)
        rows_ref[at] = (found[at] * gate).astype(bf16)
    refs = (
        (left_kept_ref, left_sent_ref),
        (middle_kept_ref, middle_sent_ref),
        (right_kept_ref, right_sent_ref),
    )
    for which, (start, stop) in enumerate(thirds(down_ref.shape[-1])):
        found = [
            rows_dot(
                chosen[place].astype(bf16),
                rows_ref[place * count : (place + 1) * count, start:stop],
            )
            + dot(shared_hidden_ref[place * span : (place + 1) * span], shared_ref[:, start:stop])
            for place in places
        ]
        halves_out(me_ref, refs, jnp.concatenate(found, axis=0), which, span)


def columns_kernel(place_ref, left_ref, right_ref, out_ref):
    out_ref[...] = rows_dot(left_ref[...], right_ref[...]).astype(out_ref.dtype)


def columns_sum_kernel(place_ref, left_ref, right_ref, came_ref, out_ref):
    found = rows_dot(left_ref[...], right_ref[...]) + came_ref[...].astype(f32)
    hidden = found.shape[1] // 2
    out_ref[:, 0, :] = found[:, :hidden]
    out_ref[:, 1, :] = found[:, hidden:]


def columns_sum(left, right, came, place):
    width, block = left.shape[1] // 2, 256
    steps = width // block
    hidden = right.shape[1] // 2
    return pl.pallas_call(
        columns_sum_kernel,
        grid_spec=pltpu.PrefetchScalarGridSpec(
            num_scalar_prefetch=1,
            grid=(steps,),
            in_specs=[
                pl.BlockSpec((left.shape[0], block), lambda i, place: (0, place[0] * steps + i)),
                pl.BlockSpec(right.shape, lambda i, place: (0, 0), pipeline_mode=pl.Buffered(1)),
                pl.BlockSpec((block, right.shape[1]), lambda i, place: (i, 0)),
            ],
            out_specs=pl.BlockSpec((block, 2, hidden), lambda i, place: (i, 0, 0)),
        ),
        out_shape=jax.ShapeDtypeStruct((width, 2, hidden), f32),
        compiler_params=pltpu.CompilerParams(vmem_limit_bytes=60 * 2**20),
    )(jnp.reshape(place, (1,)).astype(jnp.int32), left, right, came)


def columns_product(left, right, place, parts, dtype):
    width = left.shape[1] // parts
    block = 256 if width % 256 == 0 else 128
    steps = width // block
    return pl.pallas_call(
        columns_kernel,
        grid_spec=pltpu.PrefetchScalarGridSpec(
            num_scalar_prefetch=1,
            grid=(steps,),
            in_specs=[
                pl.BlockSpec((left.shape[0], block), lambda i, place: (0, place[0] * steps + i)),
                pl.BlockSpec(right.shape, lambda i, place: (0, 0), pipeline_mode=pl.Buffered(1)),
            ],
            out_specs=pl.BlockSpec((block, right.shape[1]), lambda i, place: (i, 0)),
        ),
        out_shape=jax.ShapeDtypeStruct((width, right.shape[1]), dtype),
        compiler_params=pltpu.CompilerParams(vmem_limit_bytes=56 * 2**20),
    )(jnp.reshape(place, (1,)).astype(jnp.int32), left, right)


def shards(
    tokens,
    attn_gain,
    kv_gain,
    ffn_gain,
    q_weight,
    kv_down_weight,
    kv_up_weight,
    out_weight,
    shared_gate_up,
    shared_down,
    expert_gate_up,
    expert_down,
    routes,
    gates,
    lengths,
    out_grad,
):
    row_count, width = tokens.shape
    dp_count = lax.axis_size("dp")
    expert_count = lax.axis_size("expert")
    core = lax.axis_index("dp")
    me = lax.axis_index("expert")
    scale_factor = (DH + DR) ** (-0.5)
    slice_rows = kv_down_weight.shape[0]
    joint_width = KVR + DR
    n_gain, n_kv_gain = attn_gain.shape[0], kv_gain.shape[0]

    bits = bits_of(expert_count)
    head_step = expert_count * dp_count // H
    pair_bit = max(4, head_step)
    rest = [bit for bit in bits if bit != pair_bit]
    head_low = pair_bit // head_step
    head_high = H // (dp_count * 2 * head_low)
    heads = head_high * head_low
    blocks = 2 * dp_count
    pair_rows = blocks * row_count

    far, second, first = rest
    orders = whole_orders(bits, pair_bit)
    parts = thirds(width)

    def column_parts(values):
        return [values[..., low:high] for low, high in parts]

    combined = jnp.sum(
        jnp.where(
            routes[:, :, None] == jnp.arange(expert_count, dtype=jnp.int32),
            gates[:, :, None],
            0.0,
        ),
        axis=1,
    ).T
    gates_high = lax.reduce_precision(combined, 8, 7)
    gates_low = (combined - gates_high).astype(bf16)
    gates_both = jnp.stack([gates_high.astype(bf16), gates_low], axis=1)
    gate_cols = 4 * row_count
    gates_both = gates_both.reshape(-1, gate_cols)
    gate_rows = gates_both.shape[0]
    gates_both = jnp.pad(gates_both, ((0, 0), (0, joint_width - gate_cols)))
    gains = jnp.concatenate([attn_gain, ffn_gain, kv_gain, lengths[0].astype(bf16)])
    gains = jnp.pad(gains, (0, joint_width - gains.shape[0]))[None]
    gain_row = slice_rows + gate_rows
    spare = -(gain_row + 1) % 16
    small = jnp.concatenate(
        [kv_down_weight, gates_both, jnp.pad(gains, ((0, spare), (0, 0)))], axis=0
    )

    def turned(values):
        split = values.reshape(values.shape[0], dp_count, expert_count, slice_rows)
        return split.transpose(0, 2, 1, 3).reshape(values.shape)

    def turned_back(values):
        split = values.reshape(values.shape[0], expert_count, dp_count, slice_rows)
        return split.transpose(0, 2, 1, 3).reshape(values.shape)

    q_cols = heads * (DH + DR)
    up_cols = heads * (DH + DV) * n_kv_gain // slice_rows
    head_cols = q_cols + up_cols
    head_rows = dp_count * slice_rows

    def by_pair(weight, head_width, *cuts):
        split = weight.reshape(-1, dp_count, head_high, 2, head_low, head_width)
        split = split.transpose(1, 3, 0, 2, 4, 5)
        lead = (dp_count, 2, weight.shape[0], -1)
        return [part.reshape(lead) for part in jnp.split(split, cuts, axis=-1)]

    pieces = slice_rows // n_kv_gain

    def in_pieces(found):
        found = found.reshape(found.shape[:-2] + (n_kv_gain, pieces, -1))
        return jnp.swapaxes(found, -3, -2).reshape(found.shape[:-3] + (slice_rows, -1))

    def of_pieces(found):
        found = found.reshape(found.shape[:-2] + (pieces, n_kv_gain, -1))
        return jnp.swapaxes(found, -3, -2).reshape(found.shape[:-3] + (n_kv_gain, -1))

    by_head = dp_swap(
        jnp.concatenate(
            by_pair(q_weight, DH + DR, DH, DH + DR // 2)
            + [in_pieces(part) for part in by_pair(kv_up_weight, DH + DV)],
            axis=-1,
        )
    )
    nope_cols = heads * DH
    rope_cols = heads * DR // 2

    def spread(columns):
        if rope_cols == ROPE_LANES:
            return columns
        parts = jnp.split(columns[:, :q_cols], (nope_cols, nope_cols + rope_cols), axis=-1)
        room = ((0, 0), (0, ROPE_LANES - rope_cols))
        return jnp.concatenate([parts[0], jnp.pad(parts[1], room), jnp.pad(parts[2], room)], axis=-1)

    def unspread(columns):
        if rope_cols == ROPE_LANES:
            return columns
        parts = jnp.split(columns, (nope_cols, nope_cols + ROPE_LANES), axis=-1)
        return jnp.concatenate([parts[0], parts[1][:, :rope_cols], parts[2][:, :rope_cols]], axis=-1)

    out_cut = out_weight.reshape(slice_rows, -1, 2, head_cols).transpose(2, 1, 0, 3)
    out_cut = out_cut.reshape(2, -1, head_cols)
    head_cut = head_rows * 3 // 8
    out_mid = out_cut.shape[1] // 2

    share = shared_down.shape[0]
    units = dp_count * share
    padded = -(-units // 128) * 128

    def shared_by_unit(results, found, weight):
        split = weight.reshape(slice_rows, 2, dp_count, expert_count, share)
        split = split.transpose(3, 0, 1, 2, 4).reshape(expert_count, slice_rows, 2, units)
        split = jnp.pad(split, ((0, 0), (0, 0), (0, 0), (0, padded - units)))
        return split.reshape(expert_count, slice_rows, 2 * padded)

    pair_w = lax.all_gather(expert_gate_up[0].reshape(width // dp_count, -1), "dp", tiled=True)
    down_w = lax.all_gather(expert_down[0], "dp", tiled=True)
    def shared_weights(split, shared_down):
        split = lax.all_to_all(split, "expert", split_axis=0, concat_axis=0, tiled=True)
        down = dp_gather(shared_down).reshape(units, width)
        down = jnp.pad(down, ((0, padded - units), (0, 0)))
        return dp_gather(split).reshape(width, 2 * padded), down

    def attend(all_rows, small_all, by_head, out_parts):
        joint_all = dp_gather(small_all[:, :slice_rows])
        kv_down = joint_all.transpose(1, 0, 2, 3).reshape(width, joint_width)
        gains_all = dp_gather(small_all[:, gain_row])
        attn_scale = gains_all[..., :n_gain].transpose(1, 0, 2).reshape(-1)
        ffn_scale = gains_all[..., n_gain : 2 * n_gain].reshape(-1)
        n_gains = 2 * n_gain + n_kv_gain
        kv_scale = gains_all[..., 2 * n_gain : n_gains].reshape(-1)
        all_lengths = gains_all[..., n_gains : n_gains + lengths.shape[1]].astype(jnp.int32)
        low = me & ~pair_bit
        all_lengths = jnp.stack([pick(all_lengths, low, 1), pick(all_lengths, low | pair_bit, 1)])
        all_lengths = all_lengths.reshape(blocks, -1)
        doc_ids, offsets = jax.vmap(lambda row: layout(row, row_count))(all_lengths)
        cos, sin = [table.reshape(pair_rows, DR // 2) for table in angles(offsets, DR)]
        all_rows = dp_gather(all_rows).transpose(1, 0, 2, 3).reshape(pair_rows, width)
        if dp_count == 2:
            last = (first, second, far, first)
            places = jnp.stack([((me & bit) != 0).astype(jnp.int32) for bit in last])
            q_full, kv_up, out_full = whole_call(
                functools.partial(
                    assemble_kernel,
                    (
                        [bit.bit_length() - 1 for bit in last],
                        pair_bit.bit_length() - 1,
                        slice_rows,
                        pieces,
                    ),
                ),
                [part for both in by_head + out_parts for part in both],
                (
                    ((width, q_cols), bf16),
                    ((KVR, heads * (DH + DV)), bf16),
                    ((heads * DV, width), bf16),
                ),
                scalars=(places,),
            )
        else:
            by_head = jnp.concatenate(by_head, axis=1)
            q_full = spread(by_head.reshape(width, head_cols))
            kv_up = by_head[..., q_cols:].reshape(expert_count, dp_count, slice_rows, -1)
            kv_up = of_pieces(kv_up).transpose(1, 0, 2, 3).reshape(KVR, heads * (DH + DV))
            out_full = jnp.concatenate(out_parts, axis=1)
            at = bits.index(pair_bit)
            out_full = out_full.reshape((2,) * len(bits) + (-1, slice_rows, head_cols))
            out_full = jnp.moveaxis(out_full, (len(bits), at), (-3, -2)).reshape(heads * DV, width)
        wide = nope_cols + 2 * ROPE_LANES
        outs = by_rows_call(
            functools.partial(attend_kernel, heads),
            pair_rows // (4 * row_count),
            ("x", "gain", "kv_gain", "down", "q", "up", "out", "cos", "sin", "column", "row"),
            dict(
                x=all_rows,
                cos=cos,
                sin=sin,
                column=doc_ids.reshape(pair_rows, 1),
                row=doc_ids.reshape(blocks, 1, row_count),
            ),
            dict(
                gain=attn_scale.astype(f32)[None],
                kv_gain=kv_scale.astype(f32)[None],
                down=kv_down,
                q=q_full,
                up=kv_up,
                out=out_full,
            ),
            (
                ("normed", (pair_rows, width), bf16),
                ("joint", (pair_rows, joint_width), f32),
                ("kv_normed", (pair_rows, KVR), bf16),
                ("heads", (pair_rows, wide), bf16),
                ("keys", (pair_rows, wide), bf16),
                ("values", (pair_rows, heads * DV), bf16),
                ("probs", (blocks * heads, row_count, row_count), f32),
                ("attended", (pair_rows, heads * DV), bf16),
                ("sum", (pair_rows, width), bf16),
            ),
        )
        weights = (q_full, kv_up, out_full, kv_down)
        return outs, weights, (attn_scale, kv_scale, ffn_scale), (cos, sin), all_rows

    def cut_out(found):
        at = bits.index(pair_bit)
        found = found.reshape((2,) * len(rest) + (slice_rows, -1, 2, head_cols))
        found = jnp.moveaxis(found, (-3, -2), (len(bits), at))
        return found.reshape(expert_count, -1, head_cols)

    def by_owner(found):
        found = found.reshape(2, dp_count, row_count, -1).transpose(1, 0, 2, 3)
        return dp_scatter(found, bf16).astype(bf16)

    (all_rows, by_head, small), (shared_split,) = march(
        gathering(turned(tokens), [pair_bit]),
        pair_swapping(by_head, pair_bit, 1),
        gathering(small, [far]),
        jobs=((shared_by_unit, shared_gate_up),),
    )
    by_head = by_head.reshape(2, head_rows, head_cols)
    held_grad = []
    results, found = march(
        *(
            gathering(part, order, [pair_bit], whole=dp_count != 2)
            for part, order in (
                (by_head[:, :head_cut], (second, far, first)),
                (by_head[:, head_cut:], (far, first, second)),
                (out_cut[:, :out_mid], (second, first, far)),
                (out_cut[:, out_mid:], (far, second, first)),
            )
        ),
        gathering(small, (first, second, pair_bit), [far]),
        jobs=((skip,), (skip,), (lambda results, found, part: held_grad.append(part), out_grad)),
    )

    grad_all = lax.all_gather(held_grad[0], "expert")
    outs, weights, scales, tables, all_rows = attend(all_rows, results[4], results[:2], results[2:4])
    normed, joint, kv_normed, query_parts, key_parts, values, probs, attended, attended_sum = outs
    q_full, kv_up, out_full, kv_down = weights
    attn_scale, kv_scale, ffn_scale = scales
    attended_sum = by_owner(attended_sum)
    shared_w, shared_out = shared_weights(shared_split, shared_down)
    hidden = down_w.shape[0]
    gates_all = results[4][:, slice_rows:gain_row, :gate_cols]
    gates_all = gates_all.reshape(expert_count, expert_count, 2, row_count)
    own_gate = pick(gates_all, me, 1).astype(f32).sum(axis=1)

    capacity = min(row_count, 3 * row_count * TOP // (2 * expert_count))
    slots = expert_count * capacity
    group_rows = expert_count * row_count
    grad_rows = grad_all.reshape(group_rows, width)
    live = own_gate > 0.0
    slot = jnp.cumsum(live.astype(jnp.int32), axis=1) - 1
    slot = slot + capacity * (jnp.arange(expert_count, dtype=jnp.int32) % 2)[:, None]
    slot = jnp.where(live, slot, -1).reshape(expert_count // 2, 1, 2 * row_count)
    gate = own_gate.reshape(expert_count // 2, 1, 2 * row_count)
    chunk = 4 * row_count

    steps = group_rows // chunk
    my_place = [((me & bit) != 0).astype(jnp.int32) for bit in (pair_bit, second, first)]
    my_place = jnp.stack(my_place)

    def group(i):
        return i if pair_bit == 4 else (i % 2) * (steps // 2) + i // 2

    def halves_of(name):
        return [
            (f"{name}{i}{kind}", (group_rows // 2, high - low), bf16)
            for i, (low, high) in enumerate(parts)
            for kind in ("kept", "sent")
        ]

    def from_gradient(results, found, grad_rows):
        return by_rows_call(
            functools.partial(gradient_kernel, 2 * capacity),
            steps,
            ("grad", "slot", "gate", "down", "shared"),
            dict(grad=grad_rows, slot=slot, gate=gate),
            dict(down=down_w, shared=shared_out),
            (
                ("picked", (slots, width), bf16),
                ("d_hidden", (slots, hidden), f32),
                ("d_shared", (group_rows, padded), f32),
            ),
        )

    attended_sum = alone(scattering(attended_sum, [pair_bit], [pair_bit]))
    resid_in = tokens.astype(f32)
    upstream = out_grad.astype(f32)
    resid = resid_in + attended_sum
    ffn_in = norm_apply(resid, ffn_scale).astype(bf16)

    ffn_parts, ((slot_grad, d_hidden, d_shared_hidden), *unused) = march(
        *(gathering(part, order, whole=False) for part, order in zip(column_parts(ffn_in), orders)),
        jobs=((from_gradient, grad_rows),),
    )
    names = [f"in{i}{kind}" for i in range(3) for kind in ("held", "came")]
    ffn_parts = [part.reshape(group_rows // 2, -1) for both in ffn_parts for part in both]
    ffn_rows, rows, expert_hidden, d_pair, shared_hidden, d_shared_pair, *d_parts = by_rows_call(
        functools.partial(expert_kernel, 2 * capacity),
        steps,
        ["slot", "d_hidden", "d_shared", "pair", "shared"] + names,
        dict(zip(names, ffn_parts), slot=slot, d_hidden=d_hidden, d_shared=d_shared_hidden),
        dict(pair=pair_w, shared=shared_w),
        [
            ("x", (group_rows, width), bf16),
            ("rows", (slots, width), bf16),
            ("hidden", (slots, hidden), bf16),
            ("d_pair", (slots, 2 * hidden), bf16),
            ("shared_hidden", (group_rows, padded), bf16),
            ("d_shared_pair", (group_rows, 2 * padded), bf16),
        ]
        + halves_of("out"),
        group=group,
        scalars=(my_place,),
        half=("in0held", "in0came", "out0kept", "out0sent"),
    )
    d_parts = [(d_parts[2 * i], d_parts[2 * i + 1]) for i in range(3)]

    def output_part(results, found, expert_hidden, shared_hidden):
        return by_rows_call(
            functools.partial(output_kernel, 2 * capacity),
            steps,
            ("hidden", "shared_hidden", "slot", "gate", "down", "shared"),
            dict(hidden=expert_hidden, shared_hidden=shared_hidden, slot=slot, gate=gate),
            dict(down=down_w, shared=shared_out),
            halves_of("out"),
            scratch=[pltpu.VMEM((slots // steps, width), bf16)],
            group=group,
            scalars=(my_place,),
            half=("out0kept", "out0sent"),
        )

    def halves(found):
        if dp_count != 2:
            return lax.psum_scatter(found.astype(bf16), "dp", scatter_dimension=0), ()
        return pick(found, core, 0), pick(found, 1 - core, 0).astype(bf16)

    def exchanged(kept, sent):
        if dp_count != 2:
            return kept.astype(f32)
        return kept + lax.ppermute(sent, "dp", [(0, 1), (1, 0)]).astype(f32)

    def pair_sent(results, found, rows, d_pair, expert_hidden, shared_hidden):
        out_part = output_part(results, found, expert_hidden, shared_hidden)
        if dp_count != 2:
            return (), out_part
        return columns_product(rows, d_pair, 1 - core, dp_count, bf16), out_part

    def pair_kept(results, found, rows, d_pair):
        if dp_count != 2:
            whole = dot(rows.T, d_pair).astype(bf16).reshape(dp_count, width // dp_count, -1)
            whole = lax.psum_scatter(whole, "dp", scatter_dimension=0).astype(f32)
            return whole.reshape(-1, 2, hidden)
        came = lax.ppermute(found[0][0], "dp", [(0, 1), (1, 0)])
        return columns_sum(rows, d_pair, came, core)

    def down_gradient(results, found, expert_hidden, slot_grad):
        return halves(
            dot(expert_hidden.T, slot_grad).reshape(dp_count, hidden // dp_count, width)
        )

    def shared_gradient(results, found, shared_hidden, d_shared_pair):
        down = columns_product(shared_hidden, grad_rows, jnp.int32(0), 1, f32)
        down = down[:units].reshape(dp_count, share, width)
        both = columns_product(ffn_rows, d_shared_pair, jnp.int32(0), 1, bf16)
        both = both.reshape(dp_count, expert_count, slice_rows, 2 * padded)
        return dp_scatter(down, bf16), dp_scatter(both, bf16).astype(bf16)

    d_sums, found = march(
        *(scattering(part, order[::-1], bits) for part, order in zip(d_parts, orders)),
        jobs=(
            (pair_sent, rows, d_pair, expert_hidden, shared_hidden),
            (pair_kept, rows, d_pair),
        ),
    )
    (unused, out_part), grad_pair, *unused = found
    d_ffn_in = jnp.concatenate(d_sums, axis=-1)

    d_norm_resid, grad_ffn_scale = norm_back(resid, ffn_scale, d_ffn_in)
    d_resid = upstream + d_norm_resid
    out_part = [(out_part[2 * i], out_part[2 * i + 1]) for i in range(3)]

    def attend_back(results, found, d_branch):
        d_branch = dp_gather(d_branch).transpose(1, 0, 2, 3).reshape(pair_rows, width)
        steps = pair_rows // (4 * row_count)
        wide = nope_cols + 2 * ROPE_LANES
        outs = by_rows_call(
            functools.partial(attend_back_kernel, heads),
            steps,
            (
                "x", "branch", "out", "probs", "heads", "keys", "values", "joint", "kv_gain", "up", "q",
                "down", "cos", "sin",
            ),
            dict(
                x=all_rows,
                branch=d_branch,
                probs=probs,
                heads=query_parts,
                keys=key_parts,
                values=values,
                joint=joint,
                cos=tables[0],
                sin=tables[1],
            ),
            dict(
                out=out_full,
                kv_gain=kv_scale.astype(f32)[None],
                up=kv_up,
                q=q_full,
                down=kv_down,
            ),
            (
                ("d_q", (pair_rows, wide), bf16),
                ("d_kv", (pair_rows, heads * (DH + DV)), bf16),
                ("d_joint", (pair_rows, joint_width), bf16),
                ("d_gain", (steps, 1, KVR), f32),
                ("d_first_gain", (steps, 1, width), f32),
                ("sum", (pair_rows, width), bf16),
            ),
            scratch=[pltpu.VMEM((4 * row_count, DR), f32)],
        )
        return d_branch, outs

    def weight_gradients(results, found):
        d_branch, (d_q_heads, d_kv_heads, d_joint, *unused) = found[0]
        if dp_count == 2:
            *parts, grad_kvdown = whole_call(
                functools.partial(
                    attention_gradients_kernel, (pair_bit.bit_length() - 1, slice_rows, pieces)
                ),
                (normed, d_q_heads, kv_normed, d_kv_heads, attended, d_branch, d_joint),
                (
                    ((expert_count, head_cut, head_cols), bf16),
                    ((expert_count, head_rows - head_cut, head_cols), bf16),
                    ((expert_count, out_mid, head_cols), bf16),
                    ((expert_count, slice_rows - out_mid, head_cols), bf16),
                    ((dp_count, expert_count, slice_rows, joint_width), bf16),
                ),
            )
            return *parts, dp_scatter(grad_kvdown, bf16)
        grad_q = unspread(dot(normed.T, d_q_heads)).astype(bf16)
        grad_q = grad_q.reshape(expert_count, head_rows, q_cols)
        grad_up = dot(kv_normed.T, d_kv_heads).astype(bf16)
        grad_up = grad_up.reshape(dp_count, expert_count, n_kv_gain, -1).transpose(1, 0, 2, 3)
        grad_up = in_pieces(grad_up).reshape(expert_count, head_rows, up_cols)
        by_head = jnp.concatenate([grad_q, grad_up], axis=-1)
        grad_out = cut_out(dot(attended.T, d_branch).astype(bf16))
        grad_kvdown = dot(normed.T, d_joint)
        grad_kvdown = grad_kvdown.reshape(expert_count, dp_count, slice_rows, joint_width)
        parts = (
            by_head[:, :head_cut], by_head[:, head_cut:], grad_out[:, :out_mid], grad_out[:, out_mid:]
        )
        return *parts, dp_scatter(grad_kvdown.transpose(1, 0, 2, 3), bf16)

    def small_gradients(found, grad_kvdown):
        unused, (*unused, grad_kv_scale, grad_attn_scale, unused) = found
        grad_attn_scale = grad_attn_scale.sum(axis=0).reshape(expert_count, dp_count, n_gain)
        scale_sums = jnp.concatenate(
            [
                grad_attn_scale.transpose(1, 0, 2),
                grad_ffn_scale.reshape(dp_count, expert_count, n_gain),
                grad_kv_scale.sum(axis=0).reshape(dp_count, expert_count, n_kv_gain),
            ],
            axis=-1,
        )
        room = joint_width - scale_sums.shape[-1]
        scale_sums = dp_scatter(jnp.pad(scale_sums, ((0, 0), (0, 0), (0, room))))
        return jnp.concatenate([grad_kvdown, scale_sums[:, None]], axis=1).astype(bf16)

    sums = []

    def back_of(results, found):
        return attend_back(results, found, results[0])

    def sum_and_gradients(results, found):
        sums.append(by_owner(found[1][1][-1]))
        *parts, grad_kvdown = weight_gradients(results, found[1:])
        sums.append(small_gradients(found[1], grad_kvdown))
        return parts, sums[1]

    (unused, d_normed, small_sums, *results), found = march(
        gathering(d_resid.astype(bf16), [pair_bit]),
        deferred(3, lambda: scattering(sums[0], [pair_bit], [pair_bit])),
        deferred(3, lambda: scattering(sums[1], [pair_bit], bits, bf16)),
        *(
            scattering(after(part, d_resid), order[::-1], bits)
            for part, order in zip(out_part, orders)
        ),
        jobs=(
            (skip,),
            (back_of,),
            (sum_and_gradients,),
            (shared_gradient, shared_hidden, d_shared_pair),
        ),
    )
    grad_parts, unused = found[2]
    grad_shared_out, grad_shared = found[3]
    output = (resid + jnp.concatenate(results, axis=-1)).astype(bf16)
    d_norm_in, unused = norm_back(turned(resid_in), attn_scale, d_normed)
    grad_in = (d_resid + turned_back(d_norm_in)).astype(bf16)

    def start_down(results, found, expert_hidden, slot_grad, shared):
        shared = lax.all_to_all(shared, "expert", split_axis=0, concat_axis=0, tiled=True)
        return down_gradient(results, found, expert_hidden, slot_grad), shared

    def finish_down(results, found):
        return exchanged(*found[0][0]).reshape(expert_down.shape)

    def finish_shared(results, found):
        both = found[0][1].reshape(expert_count, slice_rows, 2, padded)[..., :units]
        both = both.reshape(expert_count, slice_rows, 2, dp_count, share)
        return both.transpose(1, 2, 3, 0, 4).reshape(shared_gate_up.shape).astype(f32)

    def whole_heads(found, rows, *widths):
        cuts = [heads * sum(widths[: i + 1]) for i in range(len(widths) - 1)]
        lead = (dp_count, 2, rows, head_high, head_low, -1)
        found = jnp.concatenate(
            [part.reshape(lead) for part in jnp.split(found, cuts, axis=-1)], axis=-1
        )
        return found.transpose(2, 0, 3, 1, 4, 5).reshape(rows, -1).astype(f32)

    summed, found = march(
        scattering(small_sums, (second, first, far), rest),
        *(
            scattering(part, order, bits, bf16)
            for part, order in (
                (grad_parts[0], (first, far, second)),
                (grad_parts[1], (second, first, far)),
                (grad_parts[2], (far, first, second)),
                (grad_parts[3], (first, second, far)),
            )
        ),
        jobs=(
            (start_down, *after((expert_hidden, slot_grad, grad_shared), results)),
            (finish_down,),
            (finish_shared,),
        ),
    )
    unused, grad_down, grad_shared = found[:3]
    by_head = jnp.concatenate(summed[1:3], axis=1)
    by_head = alone(pair_swapping(by_head, pair_bit, 0)).reshape(2, dp_count, slice_rows, head_cols)
    by_head = dp_swap(by_head.transpose(1, 0, 2, 3))
    grad_q = whole_heads(by_head[..., :q_cols], slice_rows, DH, DR // 2, DR // 2)
    grad_up = of_pieces(by_head[..., q_cols:])
    grad_up = whole_heads(grad_up, n_kv_gain, DH + DV)
    grad_out = jnp.concatenate(summed[3:5], axis=1).reshape(2, -1, slice_rows, head_cols)
    grad_out = grad_out.transpose(2, 1, 0, 3).reshape(out_weight.shape).astype(f32)
    small_sums = summed[0]
    grad_kvdown = small_sums[:slice_rows]
    scale_sums = small_sums[slice_rows]

    return (
        output,
        grad_in,
        scale_sums[:n_gain],
        scale_sums[2 * n_gain : 2 * n_gain + n_kv_gain],
        scale_sums[n_gain : 2 * n_gain],
        grad_q,
        grad_kvdown,
        grad_up,
        grad_out,
        grad_shared,
        grad_shared_out,
        grad_pair.reshape(expert_gate_up.shape),
        grad_down,
    )


def solution(mesh):
    rows = P(SPLIT, None)
    each = P(SPLIT)
    cube = P(SPLIT, None, None)
    pair = P("expert", "dp", None, None)
    down = P("expert", "dp", None)
    dense = (rows, rows, rows, rows, cube, rows)
    return jax.shard_map(
        shards,
        mesh=mesh,
        in_specs=(rows, each, each, each) + dense + (pair, down, rows, rows, rows, rows),
        out_specs=(rows, rows, each, each, each) + dense + (pair, down),
        check_vma=False,
    )
```
